32 devices in a mesh: dp: 32 (over z, y, x, core).
Axes of the slice: x: 2, y: 2, z: 4, core: 2. Of those that a mesh axis runs over, the one named last changes fastest.
Arguments:
- arrival_descriptors: bfloat16 [2, 32, 128, 1024], P(None, 'dp'), may hold values from -6 to 6
- opening_sheet_amounts: bfloat16 [2, 32, 128, 1024], P(None, 'dp'), may hold values from -6 to 6
- series_spans: int32 [2, 32], P(None, 'dp'), may hold values from 32 to 128, as said below
- arrival_derivative: bfloat16 [2, 32, 128, 1024], P(None, 'dp'), may hold values from -6 to 6
- preceding_merge_ratios: bfloat16 [7, 1024], P(None, 'dp'), may hold values from 0 to 1
- normalizing_stretches: bfloat16 [3, 1024], P(None, 'dp'), may hold values from 0.5 to 1.5
- normalizing_translations: bfloat16 [3, 1024], P(None, 'dp'), may hold values from -3 to 3
- deletion_tying_ratios: bfloat16 [2, 1024], P(None, 'dp'), may hold values from 0.5 to 1.5
- immediate_extra_ratios: bfloat16 [1024], P('dp'), may hold values from -0.25 to 0.25
- dwindle_footing: bfloat16 [1024], P('dp'), may hold values from -8 to -1
- squashing_footings: bfloat16 [2, 1024], P(None, 'dp'), may hold values from -1 to 1
- reducing_transforms: bfloat16 [1024, 288], P('dp'), may hold values from -0.1875 to 0.1875
- enlarging_transforms: bfloat16 [288, 1024], P(None, 'dp'), may hold values from -0.75 to 0.75
- ingoing_affine_transforms: bfloat16 [3, 1024, 1024], P(None, None, 'dp'), may hold values from -0.1875 to 0.1875
- concluding_affine_transform: bfloat16 [1024, 1024], P(None, 'dp'), may hold values from -0.1875 to 0.1875
- perceptron_address_transform: bfloat16 [1024, 4096], P('dp'), may hold values from -0.1875 to 0.1875
- perceptron_amount_transform: bfloat16 [4096, 1024], P('dp'), may hold values from -0.09375 to 0.09375
Outputs:
- outputs: bfloat16 [2, 32, 128, 1024], P(None, 'dp')
- input_grad: bfloat16 [2, 32, 128, 1024], P(None, 'dp')
- first_value_grad: bfloat16 [2, 32, 128, 1024], P(None, 'dp')
- mix_coef_grad: float32 [7, 1024], P(None, 'dp')
- norm_gain_grad: float32 [3, 1024], P(None, 'dp')
- norm_bias_grad: float32 [3, 1024], P(None, 'dp')
- head_coef_grad: float32 [2, 1024], P(None, 'dp')
- bonus_coef_grad: float32 [1024], P('dp')
- decay_base_grad: float32 [1024], P('dp')
- gate_base_grad: float32 [2, 1024], P(None, 'dp')
- lora_in_grad: float32 [1024, 288], P('dp')
- lora_out_grad: float32 [288, 1024], P(None, 'dp')
- proj_in_grad: float32 [3, 1024, 1024], P(None, None, 'dp')
- proj_out_grad: float32 [1024, 1024], P(None, 'dp')
- ffn_key_grad: float32 [1024, 4096], P('dp')
- ffn_value_grad: float32 [4096, 1024], P('dp')
The draws below stay inside these ranges and needn't reach their ends.
Inputs may be any that keep to these rules, and one draw needn't show every extreme that they name: `series_spans`: valid slots of each sequence, counted from its first slot; in each micro-batch some sequence has all 128 slots valid.
All inputs are finite; a program needn't handle non-finite values.
Results may differ from the reference program's by a relative error of at most 0.012.
Values may be sent and summed in bfloat16 or wider, within the bound.
No kernel may reach another device: no remote copies, remote signals or barrier semaphores. Data moves between devices by JAX's collectives and lax.ppermute only.
A program may use at most 256 MiB of HBM per device.

```python
import math
import jax
import jax.numpy as jnp
from jax import lax

MODEL_BREADTHS = 1024
HEAD_SIZE = 64
FF = 4096
DECAY_RANK = 64
RATE_RANK = 64
VALUE_RANK = 32
GATE_RANK = 128
SEQ_LEN = 128
MICRO = 2
SPAN = 64
SEQS = 32


def draw_series_spans(key, part):
    first_key, second_key = jax.random.split(key)
    drawn = jax.random.randint(first_key, (MICRO, SEQS), SEQ_LEN // 4, SEQ_LEN + 1)
    chosen = jax.random.randint(second_key, (MICRO, 1), 0, SEQS)
    columns = jnp.arange(SEQS)[None, :]
    return jnp.where(columns == chosen, SEQ_LEN, drawn).astype(jnp.int32)


def strengthened(entries, rng, source, target, blocks, factor):
    def block_of(dim):
        return (jnp.arange(entries.shape[dim]) // (entries.shape[dim] // blocks)).reshape((-1,) + (1,) * (entries.ndim - 1 - dim))

    one_side = jax.random.permutation(rng, blocks)[block_of(target)]
    far = (block_of(target) + blocks // 2) % blocks
    return jnp.where((block_of(source) == one_side) | (block_of(source) == far), factor * entries, entries)


def level_of(rng, dims, shards, smallest, high):
    def one(axis_at, blocks):
        steps = jax.random.uniform(jax.random.fold_in(jax.random.fold_in(rng, 6), axis_at), (blocks,), jnp.float32, smallest / len(shards), high / len(shards))
        return jnp.repeat(jnp.exp(steps), dims[axis_at] // blocks).reshape((-1,) + (1,) * (len(dims) - axis_at - 1))

    gain = one(*shards[0])
    for cut in shards[1:]:
        gain = gain * one(*cut)
    return gain


def centred(stream_key, shape, width, reach, shards=(), held_as=jnp.bfloat16):
    loudness = level_of(stream_key, shape, shards, -0.22, 0.18) if shards else 1.0
    values = jax.random.normal(stream_key, shape, jnp.float32) * width * loudness
    return jnp.minimum(jnp.maximum(values, -reach), reach).astype(held_as)


def bell_draw_with(rng, shape, width, most, pieces, heavy, kind=jnp.bfloat16):
    values = width * jax.random.normal(rng, shape, jnp.float32)
    if pieces:
        values = values * level_of(rng, shape, pieces, -0.22, 0.18)
    return jnp.clip(strengthened(values, jax.random.fold_in(rng, 3), *heavy), -most, most).astype(kind)


def setup_inputs(seed: int = 0) -> dict:
    splits = jax.random.split(jax.random.key(seed), 18)
    arrival_descriptors = centred(splits[0], (MICRO, SEQS, SEQ_LEN, MODEL_BREADTHS), 1.0, 6.0, ((1, 32),))
    opening_sheet_amounts = centred(splits[1], (MICRO, SEQS, SEQ_LEN, MODEL_BREADTHS), 1.0, 6.0, ((1, 32),))
    series_spans = draw_series_spans(jax.random.fold_in(splits[17], 71), 0)
    arrival_derivative = bell_draw_with(splits[3], (MICRO, SEQS, SEQ_LEN, MODEL_BREADTHS), 1.0, 6.0, ((1, 32),), (1, 3, 32, 2.75))
    preceding_merge_ratios = jnp.clip(1.0 * jax.random.uniform(splits[4], (7, MODEL_BREADTHS), jnp.float32) ** level_of(splits[4], (7, MODEL_BREADTHS), ((1, 32),), -0.2, 0.2), 0.0, 1.0).astype(jnp.bfloat16)
    normalizing_stretches = jnp.clip(0.5 + 1.0 * jax.random.uniform(splits[5], (3, MODEL_BREADTHS), jnp.float32) ** level_of(splits[5], (3, MODEL_BREADTHS), ((1, 32),), -0.2, 0.2), 0.5, 1.5).astype(jnp.bfloat16)
    normalizing_translations = centred(splits[6], (3, MODEL_BREADTHS), 0.5, 3.0, ((1, 32),))
    deletion_tying_ratios = jnp.clip(0.5 + 1.0 * jax.random.uniform(splits[7], (2, MODEL_BREADTHS), jnp.float32) ** level_of(splits[7], (2, MODEL_BREADTHS), ((1, 32),), -0.2, 0.2), 0.5, 1.5).astype(jnp.bfloat16)
    immediate_extra_ratios = jnp.clip(jax.random.uniform(splits[8], (MODEL_BREADTHS,), jnp.float32, -0.25, 0.25) * level_of(splits[8], (MODEL_BREADTHS,), ((0, 32),), -0.4, 0.0), -0.25, 0.25).astype(jnp.bfloat16)
    dwindle_footing = jnp.clip(-8.0 + 7.0 * jax.random.uniform(splits[9], (MODEL_BREADTHS,), jnp.float32) ** level_of(splits[9], (MODEL_BREADTHS,), ((0, 32),), -0.2, 0.2), -8.0, -1.0).astype(jnp.bfloat16)
    squashing_footings = jnp.clip(jax.random.uniform(splits[10], (2, MODEL_BREADTHS), jnp.float32, -1.0, 1.0) * level_of(splits[10], (2, MODEL_BREADTHS), ((1, 32),), -0.4, 0.0), -1.0, 1.0).astype(jnp.bfloat16)
    reducing_transforms = centred(splits[11], (MODEL_BREADTHS, DECAY_RANK + RATE_RANK + VALUE_RANK + GATE_RANK), MODEL_BREADTHS ** -0.5, 0.1875, ((0, 32),))
    enlarging_transforms = centred(splits[12], (DECAY_RANK + RATE_RANK + VALUE_RANK + GATE_RANK, MODEL_BREADTHS), DECAY_RANK ** -0.5, 0.75, ((1, 32),))
    ingoing_affine_transforms = centred(splits[13], (3, MODEL_BREADTHS, MODEL_BREADTHS), MODEL_BREADTHS ** -0.5, 0.1875, ((2, 32),))
    concluding_affine_transform = centred(splits[14], (MODEL_BREADTHS, MODEL_BREADTHS), MODEL_BREADTHS ** -0.5, 0.1875, ((1, 32),))
    perceptron_address_transform = centred(splits[15], (MODEL_BREADTHS, FF), MODEL_BREADTHS ** -0.5, 0.1875, ((0, 32),))
    perceptron_amount_transform = centred(splits[16], (FF, MODEL_BREADTHS), FF ** -0.5, 0.09375, ((0, 32),))
    return dict(arrival_descriptors=arrival_descriptors, opening_sheet_amounts=opening_sheet_amounts, series_spans=series_spans, arrival_derivative=arrival_derivative, preceding_merge_ratios=preceding_merge_ratios, normalizing_stretches=normalizing_stretches, normalizing_translations=normalizing_translations, deletion_tying_ratios=deletion_tying_ratios, immediate_extra_ratios=immediate_extra_ratios, dwindle_footing=dwindle_footing, squashing_footings=squashing_footings, reducing_transforms=reducing_transforms, enlarging_transforms=enlarging_transforms, ingoing_affine_transforms=ingoing_affine_transforms, concluding_affine_transform=concluding_affine_transform, perceptron_address_transform=perceptron_address_transform, perceptron_amount_transform=perceptron_amount_transform)


HIGHEST = lax.Precision.HIGHEST

@jax.custom_vjp
def low(v):
    return lax.optimization_barrier(v.astype(jnp.bfloat16)).astype(jnp.float32)

@jax.custom_vjp
def low_back(v):
    return v

def low_keep(v):
    return (low(v), None)

def low_pass(kept, grad):
    return (grad,)

def back_keep(v):
    return (v, None)

def back_low(kept, grad):
    return (low(grad),)
low.defvjp(low_keep, low_pass)
low_back.defvjp(back_keep, back_low)

def layer_norm(values, weight, offset):
    average = lax.optimization_barrier(jnp.mean(values, -1, keepdims=True))
    centered = values - average
    spread = lax.optimization_barrier(jnp.mean(centered * centered, -1, keepdims=True))
    return centered * lax.rsqrt(spread + 1e-05) * weight + offset

def shift_prev(values):
    return jnp.concatenate([jnp.zeros_like(values[:, :1]), values[:, :-1]], axis=1)

def matrix_product(left, right):
    return jnp.einsum('gtd,de->gte', left, right, precision=HIGHEST)

def divide_subspaces(manyfold_lattice):
    return manyfold_lattice.reshape(manyfold_lattice.shape[:-1] + (manyfold_lattice.shape[-1] // HEAD_SIZE, HEAD_SIZE))

def recurrence(acceptance_columns, log_decay, key_rows, value_rows, remove, insert):
    groups, length, head_count, head_size = acceptance_columns.shape
    blocks = length // SPAN

    def token_step(memory, batch_item):
        r_t, d_t, k_t, v_t, a_t, b_t = batch_item
        projected = jnp.einsum('ghk,ghkv->ghv', a_t, memory, precision=HIGHEST)
        memory = jnp.exp(d_t)[..., None] * memory + b_t[..., None] * projected[:, :, None, :] + k_t[..., None] * v_t[:, :, None, :]
        return (memory, jnp.einsum('ghk,ghkv->ghv', r_t, memory, precision=HIGHEST))

    def block_step(memory, sliced):
        return lax.scan(token_step, memory, sliced)

    def arrange(manyfold_lattice):
        return jnp.moveaxis(manyfold_lattice, 1, 0).reshape(blocks, SPAN, groups, head_count, head_size)
    sliced = tuple((arrange(manyfold_lattice) for manyfold_lattice in (acceptance_columns, log_decay, key_rows, value_rows, remove, insert)))
    initial = jnp.zeros((groups, head_count, head_size, head_size), jnp.float32)
    unused_item, emitted = lax.scan(jax.checkpoint(block_step), initial, sliced)
    return jnp.moveaxis(emitted.reshape(length, groups, head_count, head_size), 0, 1)

def repeating_focus_engine(acceptance_columns, address_columns, payoff_columns, dwindle_ratio, adaptation_tempo, payoff_carryover_merge, squashing_ratio, starting_payoff_columns, deletion_tying_ratios, immediate_extra_ratios, dwindle_footing, squashing_footings, subgroup_multiplicand, subgroup_summand):
    log_decay = -jnp.exp(-jax.nn.softplus(-(dwindle_footing + dwindle_ratio)) - 0.5)
    adaptation_sigmoid = jax.nn.sigmoid(squashing_footings[0] + adaptation_tempo)
    amount_sigmoid = jax.nn.sigmoid(squashing_footings[1] + payoff_carryover_merge)
    value_mix = payoff_columns + (starting_payoff_columns - payoff_columns) * amount_sigmoid
    key_mod = address_columns * (1.0 + (adaptation_sigmoid - 1.0) * deletion_tying_ratios[1])
    key_unit = divide_subspaces(address_columns * deletion_tying_ratios[0])
    key_unit = key_unit * lax.rsqrt(lax.optimization_barrier(jnp.sum(key_unit * key_unit, -1, keepdims=True)) + 1e-06)
    reception_per_subspace = divide_subspaces(acceptance_columns)
    lookup_per_subspace = divide_subspaces(key_mod)
    content_per_subspace = divide_subspaces(value_mix)
    mixed = recurrence(reception_per_subspace, divide_subspaces(log_decay), lookup_per_subspace, content_per_subspace, -key_unit, key_unit * divide_subspaces(adaptation_sigmoid))
    average = lax.optimization_barrier(jnp.mean(mixed, -1, keepdims=True))
    centered = mixed - average
    spread = lax.optimization_barrier(jnp.mean(centered * centered, -1, keepdims=True))
    standardized_features = (centered * lax.rsqrt(spread + 4.0)).reshape(acceptance_columns.shape) * subgroup_multiplicand + subgroup_summand
    present_reward_share = lax.optimization_barrier(jnp.sum(reception_per_subspace * lookup_per_subspace * divide_subspaces(immediate_extra_ratios), -1, keepdims=True)) * content_per_subspace
    return (standardized_features + present_reward_share.reshape(acceptance_columns.shape)) * squashing_ratio

def solve_onward(arrival_descriptors, opening_sheet_amounts, filled_cell_selector, preceding_merge_ratios, normalizing_stretches, normalizing_translations, deletion_tying_ratios, immediate_extra_ratios, dwindle_footing, squashing_footings, reducing_transforms, enlarging_transforms, ingoing_affine_transforms, concluding_affine_transform, perceptron_address_transform, perceptron_amount_transform):
    rate_slice = DECAY_RANK
    value_slice = rate_slice + RATE_RANK
    gate_slice = value_slice + VALUE_RANK
    standardized_features = layer_norm(arrival_descriptors, normalizing_stretches[0], normalizing_translations[0])
    change = shift_prev(standardized_features) - standardized_features
    x_r, decay_input, x_k, value_input, rate_input, gate_input = [low(standardized_features + change * preceding_merge_ratios[index_position]) for index_position in range(6)]
    acceptance_columns = low_back(matrix_product(x_r, ingoing_affine_transforms[0]))
    address_columns = low_back(matrix_product(x_k, ingoing_affine_transforms[1]))
    payoff_columns = low_back(matrix_product(value_input, ingoing_affine_transforms[2]))
    decay_preactivation = low_back(matrix_product(decay_input, reducing_transforms[:, :rate_slice]))
    rate_preactivation = low_back(matrix_product(rate_input, reducing_transforms[:, rate_slice:value_slice]))
    value_preactivation = low_back(matrix_product(value_input, reducing_transforms[:, value_slice:gate_slice]))
    gate_preactivation = low_back(matrix_product(gate_input, reducing_transforms[:, gate_slice:]))
    decay_lowrank = low(jnp.tanh(decay_preactivation))
    rate_lowrank = low(rate_preactivation)
    value_lowrank = low(value_preactivation)
    gate_lowrank = low(jax.nn.sigmoid(gate_preactivation))
    dwindle_ratio = low_back(matrix_product(decay_lowrank, enlarging_transforms[:rate_slice]))
    adaptation_tempo = low_back(matrix_product(rate_lowrank, enlarging_transforms[rate_slice:value_slice]))
    payoff_carryover_merge = low_back(matrix_product(value_lowrank, enlarging_transforms[value_slice:gate_slice]))
    squashing_ratio = low_back(matrix_product(gate_lowrank, enlarging_transforms[gate_slice:]))
    squashing_resized_merge = low(repeating_focus_engine(acceptance_columns, address_columns, payoff_columns, dwindle_ratio, adaptation_tempo, payoff_carryover_merge, squashing_ratio, opening_sheet_amounts, deletion_tying_ratios, immediate_extra_ratios, dwindle_footing, squashing_footings, normalizing_stretches[1], normalizing_translations[1]))
    mixed_in = arrival_descriptors + low_back(matrix_product(squashing_resized_merge, concluding_affine_transform))
    normed_two = layer_norm(mixed_in, normalizing_stretches[2], normalizing_translations[2])
    x_c = low(normed_two + (shift_prev(normed_two) - normed_two) * preceding_merge_ratios[6])
    hidden = low(jnp.square(jax.nn.relu(low_back(matrix_product(x_c, perceptron_address_transform)))))
    return filled_cell_selector * (mixed_in + low_back(matrix_product(hidden, perceptron_amount_transform)))

def reference(arrival_descriptors, opening_sheet_amounts, series_spans, arrival_derivative, preceding_merge_ratios, normalizing_stretches, normalizing_translations, deletion_tying_ratios, immediate_extra_ratios, dwindle_footing, squashing_footings, reducing_transforms, enlarging_transforms, ingoing_affine_transforms, concluding_affine_transform, perceptron_address_transform, perceptron_amount_transform):
    learnable_package = tuple((manyfold_lattice.astype(jnp.float32) for manyfold_lattice in (preceding_merge_ratios, normalizing_stretches, normalizing_translations, deletion_tying_ratios, immediate_extra_ratios, dwindle_footing, squashing_footings, reducing_transforms, enlarging_transforms, ingoing_affine_transforms, concluding_affine_transform, perceptron_address_transform, perceptron_amount_transform)))
    total_seqs = MICRO * SEQS
    largest = max(1, 4096 // SEQ_LEN)
    group_size = max((option for option in range(1, largest + 1) if total_seqs % option == 0))
    blocks = total_seqs // group_size

    def arrange(manyfold_lattice):
        return manyfold_lattice.reshape((blocks, group_size) + manyfold_lattice.shape[2:])
    sliced = (arrange(arrival_descriptors), arrange(opening_sheet_amounts), arrange(series_spans), arrange(arrival_derivative))
    positions = jnp.arange(SEQ_LEN, dtype=jnp.int32)

    def group_step(totals, batch_item):
        x_in, first_in, length_in, grad_in = batch_item
        filled_cell_selector = (positions[None, :] < length_in[:, None]).astype(jnp.float32)[:, :, None]

        def bound_fwd(x_val, starting_payoff_columns, *params):
            return solve_onward(x_val, starting_payoff_columns, filled_cell_selector, *params)
        result, pullback = jax.vjp(bound_fwd, x_in.astype(jnp.float32), first_in.astype(jnp.float32), *learnable_package)
        gradients = pullback(grad_in.astype(jnp.float32))
        totals = tuple((running + fresh for running, fresh in zip(totals, gradients[2:])))
        return (totals, (result.astype(jnp.bfloat16), gradients[0].astype(jnp.bfloat16), gradients[1].astype(jnp.bfloat16)))
    zeros_init = tuple((jnp.zeros_like(manyfold_lattice) for manyfold_lattice in learnable_package))
    totals, (results, input_grads, first_grads) = lax.scan(group_step, zeros_init, sliced)
    grad_scale = 1.0 / math.sqrt(MICRO * SEQS * SEQ_LEN)
    full_shape = arrival_descriptors.shape
    return (results.reshape(full_shape), input_grads.reshape(full_shape), first_grads.reshape(full_shape), totals[0] * grad_scale, totals[1] * grad_scale, totals[2] * grad_scale, totals[3] * grad_scale, totals[4] * grad_scale, totals[5] * grad_scale, totals[6] * grad_scale, totals[7] * grad_scale, totals[8] * grad_scale, totals[9] * grad_scale, totals[10] * grad_scale, totals[11] * grad_scale, totals[12] * grad_scale)
```

```python
import math

import jax
import jax.numpy as jnp
from jax import lax
from jax.experimental import pallas as pl
from jax.experimental.pallas import tpu as pltpu
from jax.sharding import PartitionSpec as P

bf16, f32 = jnp.bfloat16, jnp.float32
RANKS = (64, 64, 32, 128)
CUTS = (0, 64, 128, 160, 288)
LOW_FROM = (1, 4, 3, 5)
T = 128

def dn(x, y, cx, cy):
    return lax.dot_general(x, y, (((cx,), (cy,)), ((), ())), preferred_element_type=f32)

def split2(x):
    hi = x.astype(bf16)
    return hi, (x - hi.astype(f32)).astype(bf16)

def dot(x, y, cx=1, cy=0, passes=3):
    if passes == 1:
        return dn(x.astype(bf16), y.astype(bf16), cx, cy)
    xh, xl = split2(x); yh, yl = split2(y)
    return dn(xh, yh, cx, cy) + dn(xh, yl, cx, cy) + dn(xl, yh, cx, cy)

def ones_dot(left, x):
    hi = x.astype(bf16); r = x - hi.astype(f32)
    mid = r.astype(bf16); lo = (r - mid.astype(f32)).astype(bf16)
    w = x.shape[1]
    o = dn(left, jnp.concatenate([hi, mid, lo], 1), 1, 0)
    return o[:, :w] + o[:, w:2*w] + o[:, 2*w:]

def head_sum(x, J):
    hi, lo = split2(x)
    return dn(jnp.concatenate([hi, lo], 1), jnp.concatenate([J, J], 0), 1, 0)

def sig(z):
    return 1.0 / (1.0 + jnp.exp(-z))

def iota(shape, d):
    return lax.broadcasted_iota(jnp.int32, shape, d)

def consts():
    r, c = iota((T, T), 0), iota((T, T), 1)
    J = jnp.where((r // 64) == (c // 64), 1.0, 0.0).astype(bf16)
    low = jnp.where(r >= c, 1.0, 0.0).astype(bf16)
    up = jnp.where(r <= c, 1.0, 0.0).astype(bf16)
    h0 = c < 64
    return r, c, J, low, up, h0

def halves(x, h0):
    z = jnp.zeros_like(x)
    m = h0 if x.shape[0] == T else jnp.concatenate([h0, h0], 0)
    return jnp.where(m, x, z), jnp.where(m, z, x)

def prep(r_, kx, vx, ow, oa, ov, first, par, K):
    r, c, J, low, up, h0 = K
    dk0, dk1, bonus, db, sq0, sq1 = (par[i:i+1] for i in range(6))
    sg = sig(db + ow)
    ld = sg * (-0.6065306597126334)
    cum = ones_dot(low, ld)
    cm = cum - cum[63:64]
    G = jnp.exp(cm); S = jnp.exp(-cm); B = jnp.exp(cm - ld)
    ag = sig(sq0 + oa); vg = sig(sq1 + ov)
    v2 = vx + (first - vx) * vg
    kfac = 1.0 + (ag - 1.0) * dk1
    km = kx * kfac
    cc = kx * dk0
    n = lax.rsqrt(head_sum(cc * cc, J) + 1e-6)
    kk = cc * n
    return sg, ld, G, S, B, ag, vg, v2, kfac, km, n, kk

def inverse(N0, N1, K, passes):
    r, c = K[0], K[1]
    z = jnp.zeros((T, T), f32)
    eye = jnp.where(r == c, 1.0, 0.0)
    m = ((r // 2) == (c // 2))
    T0 = eye + jnp.where(m, N0, 0.0); T1 = eye + jnp.where(m, N1, 0.0)
    s = 2
    def bd(a, b):
        return jnp.concatenate([jnp.concatenate([a, z], 1), jnp.concatenate([z, b], 1)], 0)
    TT = jnp.concatenate([T0, T1], 1)
    while s < T:
        m = ((r // (2*s)) == (c // (2*s))) & ((r // s) != (c // s))
        o = dot(TT, bd(jnp.where(m, N0, 0.0), jnp.where(m, N1, 0.0)), passes=passes)
        TT = TT + dot(o, bd(TT[:, :T], TT[:, T:]), passes=passes)
        s *= 2
    res = jnp.concatenate([eye, eye], 1) - TT + dot(jnp.concatenate([N0, N1], 1), bd(TT[:, :T], TT[:, T:]))
    return TT + dot(TT, bd(res[:, :T], res[:, T:]), passes=1)

def fwd_core(r_, kx, vx, ow, oa, ov, og, first, par, pA=3, pI=1, pO=3):
    K = consts(); r, c, J, low, up, h0 = K
    sg, ld, G, S, B, ag, vg, v2, kfac, km, n, kk = prep(r_, kx, vx, ow, oa, ov, first, par, K)
    at = -kk * B; rt = r_ * G; bt = kk * ag * S; kt = km * S
    Q = jnp.concatenate([at, rt], 0); Kf = jnp.concatenate([bt, kt], 0)
    Q0, Q1 = halves(Q, h0)
    A0 = dot(Q0, Kf, 1, 1, pA); A1 = dot(Q1, Kf, 1, 1, pA)
    st = r > c; inc = r >= c
    def msk(A):
        return (jnp.where(st, A[:T, :T], 0.0), jnp.where(st, A[:T, T:], 0.0),
                jnp.where(inc, A[T:, :T], 0.0), jnp.where(inc, A[T:, T:], 0.0))
    ab0, ak0, rb0, rk0 = msk(A0); ab1, ak1, rb1, rk1 = msk(A1)
    TT = inverse(ab0, ab1, K, pI)
    v0, v1 = halves(v2, h0)
    Pm = dot(jnp.concatenate([ak0, ak1], 1), jnp.concatenate([v0, v1], 0), passes=pO)
    U = dot(TT, jnp.concatenate(halves(Pm, h0), 0), passes=pO)
    u0, u1 = halves(U, h0)
    Y = dot(jnp.concatenate([rb0, rk0, rb1, rk1], 1), jnp.concatenate([u0, v0, u1, v1], 0), passes=pO)
    mean = head_sum(Y, J) * (1/64)
    cy = Y - mean
    rstd = lax.rsqrt(head_sum(cy * cy, J) * (1/64) + 4.0)
    bonus, gain, bias = par[2:3], par[6:7], par[7:8]
    bs = head_sum(r_ * km * bonus, J)
    out = (cy * rstd * gain + bias + bs * v2) * og
    return out, TT, U, Y

def bwd_core(r_, kx, vx, ow, oa, ov, og, first, par, TT, U, Y, gg, pA=3, pW=3, pD=3):
    K = consts(); r, c, J, low, up, h0 = K
    dk0, dk1, bonus, db, sq0, sq1, gain, bias = (par[i:i+1] for i in range(8))
    sg, ld, G, S, B, ag, vg, v2, kfac, km, n, kk = prep(r_, kx, vx, ow, oa, ov, first, par, K)
    at = -kk * B; rt = r_ * G; bt = kk * ag * S; kt = km * S
    mean = head_sum(Y, J) * (1/64)
    cy = Y - mean
    rstd = lax.rsqrt(head_sum(cy * cy, J) * (1/64) + 4.0)
    gn = cy * rstd
    bs = head_sum(r_ * km * bonus, J)
    g_og = gg * (gn * gain + bias + bs * v2)
    gi = gg * og
    g_gn = gi * gain
    gY = rstd * (g_gn - head_sum(g_gn, J) * (1/64) - gn * (head_sum(g_gn * gn, J) * (1/64)))
    g_bs = head_sum(gi * v2, J)
    Q = jnp.concatenate([at, rt], 0); Kf = jnp.concatenate([bt, kt], 0)
    Q0, Q1 = halves(Q, h0)
    At0 = dot(Kf, Q0, 1, 1, pA); At1 = dot(Kf, Q1, 1, 1, pA)
    st = r < c; inc = r <= c
    akT = jnp.concatenate([jnp.where(st, At0[T:, :T], 0.0), jnp.where(st, At1[T:, :T], 0.0)], 1)
    inc2 = jnp.concatenate([inc, inc], 0)
    rT = jnp.concatenate([jnp.where(inc2, At0[:, T:], 0.0), jnp.where(inc2, At1[:, T:], 0.0)], 1)
    gy0, gy1 = halves(gY, h0)
    dUV = dot(rT, jnp.concatenate([gy0, gy1], 0), passes=pW)
    dU, dV = dUV[:T], dUV[T:]
    R = dot(TT, dU, 0, 0, pW)
    W = jnp.where(h0, R[:T], R[T:])
    w0, w1 = halves(W, h0)
    dV = dV + dot(akT, jnp.concatenate([w0, w1], 0), passes=pW)
    X = jnp.concatenate([U, v2], 0)
    Yg0 = jnp.concatenate([w0, gy0], 0); Yg1 = jnp.concatenate([w1, gy1], 0)
    r2, c2 = iota((2*T, 2*T), 0), iota((2*T, 2*T), 1)
    keep = ((r2 & 127) > (c2 & 127)) | ((r2 >= T) & ((r2 & 127) == (c2 & 127)))
    keepT = ((r2 & 127) < (c2 & 127)) | ((c2 >= T) & ((r2 & 127) == (c2 & 127)))
    dA0 = jnp.where(keep, dot(Yg0, X, 1, 1, pD), 0.0)
    dA1 = jnp.where(keep, dot(Yg1, X, 1, 1, pD), 0.0)
    dT0 = jnp.where(keepT, dot(X, Yg0, 1, 1, pD), 0.0)
    dT1 = jnp.where(keepT, dot(X, Yg1, 1, 1, pD), 0.0)
    K0, K1 = halves(Kf, h0)
    dQ = dot(jnp.concatenate([dA0, dA1], 1), jnp.concatenate([K0, K1], 0), passes=pD)
    dK = dot(jnp.concatenate([dT0, dT1], 1), jnp.concatenate([Q0, Q1], 0), passes=pD)
    da_, dr_ = dQ[:T], dQ[T:]; db_, dk_ = dK[:T], dK[T:]
    e = dr_ * rt - db_ * bt - dk_ * kt
    f = da_ * at
    g_ld = ones_dot(up, e + f) - f
    g_kk = db_ * S * ag - da_ * B
    g_b = db_ * S
    g_km = g_bs * r_ * bonus + dk_ * S
    g_r = g_bs * km * bonus + dr_ * G
    g_ag = g_b * kk + g_km * kx * dk1
    g_c = n * (g_kk - kk * head_sum(g_kk * kk, J))
    g_kx = g_km * kfac + g_c * dk0
    g_v2 = gi * bs + dV
    g_first = g_v2 * vg
    g_vx = g_v2 - g_first
    g_ov = g_first * (1.0 - vg) * (first - vx)
    g_oa = g_ag * ag * (1.0 - ag)
    g_ow = g_ld * ld * (1.0 - sg)
    def cs(x): return jnp.sum(x, 0, keepdims=True)
    pg = jnp.concatenate([cs(g_c * kx), cs(g_km * kx * (ag - 1.0)), cs(g_bs * r_ * km),
                          cs(g_ow), cs(g_oa), cs(g_ov), cs(gi * gn), cs(gi)], 0)
    return g_r, g_kx, g_vx, g_ow, g_oa, g_ov, g_og, g_first, pg


def fwd_kernel(r, k, v, ow, oa, ov, og, first, par, out, tt, u, y):
    o, t_, u_, y_ = fwd_core(
        r[...], k[...], v[...], ow[...], oa[...], ov[...], og[...],
        first[...].astype(f32), par[...])
    out[...] = o.astype(bf16)
    tt[...] = t_
    u[...] = u_
    y[...] = y_


def bwd_kernel(r, k, v, ow, oa, ov, og, first, par, tt, u, y, gg,
               gr, gk, gv, gow, goa, gov, gog, gf, gp):
    res = bwd_core(
        r[...], k[...], v[...], ow[...], oa[...], ov[...], og[...],
        first[...].astype(f32), par[...], tt[...], u[...], y[...], gg[...])
    for ref, val in zip((gr, gk, gv, gow, goa, gov, gog, gf), res[:8]):
        ref[...] = val.astype(bf16)
    gp[...] = res[8]


def specs(rows, width):
    tile = pl.BlockSpec((T, 128), lambda s, p: (s, p))
    par = pl.BlockSpec((8, 128), lambda s, p: (0, p))
    pairs = width // 128
    inv = pl.BlockSpec((T, 2 * T), lambda s, p: (s * pairs + p, 0))
    gpar = pl.BlockSpec((8, 128), lambda s, p: (s, p))
    return tile, par, inv, gpar, (rows // T, pairs)


def mixer_fwd(args, par):
    rows, width = args[0].shape
    tile, pspec, inv, gpar, grid = specs(rows, width)
    wide = jax.ShapeDtypeStruct((rows, width), f32)
    return pl.pallas_call(
        fwd_kernel,
        grid=grid,
        in_specs=[tile] * 8 + [pspec],
        out_specs=[tile, inv, tile, tile],
        out_shape=[jax.ShapeDtypeStruct((rows, width), bf16),
                   jax.ShapeDtypeStruct((rows * width // 128, 2 * T), f32), wide, wide],
        compiler_params=pltpu.CompilerParams(vmem_limit_bytes=32 * 1024 * 1024),
        name="mixer_fwd",
    )(*args, par)


def mixer_bwd(args, par, saved, gg, part, before):
    rows, width = args[0].shape
    seqs, pairs = rows // T, width // 128
    half = seqs // 2
    off = part * half
    tile = pl.BlockSpec((T, 128), lambda s, p: (s + off, p))
    pspec = pl.BlockSpec((8, 128), lambda s, p: (0, p))
    inv = pl.BlockSpec((T, 2 * T), lambda s, p: ((s + off) * pairs + p, 0))
    gpar = pl.BlockSpec((8, 128), lambda s, p: (s + off, p))
    thin = jax.ShapeDtypeStruct((rows, width), bf16)

    def body(*refs):
        bwd_kernel(*refs[:13], *refs[13 + len(before):])

    return pl.pallas_call(
        body,
        grid=(half, pairs),
        in_specs=[tile] * 8 + [pspec, inv, tile, tile, tile]
        + [pl.BlockSpec(memory_space=pl.ANY)] * len(before),
        out_specs=[tile] * 8 + [gpar],
        out_shape=[thin] * 8 + [jax.ShapeDtypeStruct((seqs * 8, width), f32)],
        input_output_aliases={13 + i: i for i in range(len(before))},
        compiler_params=pltpu.CompilerParams(vmem_limit_bytes=32 * 1024 * 1024),
        cost_estimate=pl.CostEstimate(flops=20 * 10**9, bytes_accessed=10**7, transcendentals=10**6),
        name="mixer_bwd",
    )(*args, par, *saved, gg, *before)


def layer_norm(x, gain, bias):
    c = x - jnp.mean(x, -1, keepdims=True)
    return c * lax.rsqrt(jnp.mean(c * c, -1, keepdims=True) + 1e-5) * gain + bias


def prev(z):
    z = z.reshape(-1, T, z.shape[-1])
    z = jnp.concatenate([jnp.zeros_like(z[:, :1]), z[:, :-1]], 1)
    return z.reshape(-1, z.shape[-1])


def front(x, mix, gain, bias):
    h = layer_norm(x, gain, bias)
    d = prev(h) - h
    return tuple(h + d * mix[i] for i in range(mix.shape[0]))


def mm(a, b):
    return dn(a, b, 1, 0)


def mmt(a, b):
    return dn(a, b, 1, 1)


def tmm(a, b):
    return dn(a, b, 0, 0)


def lowrank_act(zw, za, zv, zg):
    return jnp.tanh(zw), za, zv, jax.nn.sigmoid(zg)


def swap(x, bit):
    n = lax.axis_size("dp")
    return lax.ppermute(x, "dp", [(i, i ^ bit) for i in range(n)])


def add(a, b):
    return (a.astype(f32) + b.astype(f32)).astype(bf16)


def pick(x, index, axis):
    return lax.dynamic_index_in_dim(x, index, axis, keepdims=False)


def other_way(g, step):
    me = lax.axis_index("dp")
    out = []
    for part, (axis, bit) in zip(g, step):
        mine = (me // bit) % 2
        out.append(add(pick(part, mine, axis), swap(pick(part, 1 - mine, axis), bit)))
    return out


STEPS = (((2, 4), (3, 2)), ((2, 2), (2, 4)), ((1, 8), (1, 8)), ((0, 16), (0, 16)))


def chip_sum_begin(g):
    n = lax.axis_size("dp")
    if n != 32:
        groups = [list(range(c, n, 2)) for c in range(2)]
        return lax.psum_scatter(g, "dp", scatter_dimension=0, axis_index_groups=groups)
    cut = g.shape[1] // 2
    return [p.reshape((2, 2, 2, 2) + p.shape[1:]) for p in (g[:, :cut], g[:, cut:])]


def chip_sum_step(g, count=1):
    if lax.axis_size("dp") != 32:
        return g
    for _ in range(count):
        g = other_way(g, STEPS[6 - g[0].ndim])
    return g


def chip_sum_end(g):
    if lax.axis_size("dp") != 32:
        return g.astype(f32)
    return jnp.concatenate(g, 0).astype(f32)


def tie(*values):
    return lax.optimization_barrier(values)


def on_core(keep, send):
    return (keep + swap(send, 1).astype(f32)).astype(bf16)


def by_chip(g):
    chips = lax.axis_size("dp") // 2
    return g.reshape(chips, g.shape[0] // chips, g.shape[1])


def trade_rows(h):
    core = lax.axis_index("dp") % 2
    h = h.reshape(2, h.shape[0] // 2, h.shape[1])
    own, got = pick(h, core, 0), swap(pick(h, 1 - core, 0).astype(bf16), 1).astype(f32)
    return jnp.where(core == 0, own, got), jnp.where(core == 0, got, own)


def on_device(x_in, first_in, spans, gout_in, mix, gains, biases, tying, extra, dwindle,
              squash, reducing, enlarging, ingoing, concluding, ffn_key, ffn_value):
    micro, seqs, length, width = x_in.shape
    rows = micro * seqs * length
    shard = mix.shape[1]
    small = jnp.concatenate([mix, gains, biases, tying, extra[None], dwindle[None], squash], 0)
    n_small = small.shape[0]
    pad = jnp.zeros((64 - n_small, shard), bf16)
    pack = jnp.concatenate(
        [jnp.swapaxes(ingoing, 1, 2)[i] for i in range(3)]
        + [concluding.T, reducing, enlarging.T, jnp.concatenate([small, pad], 0).T], 1)
    pack = lax.all_gather(pack, "dp", axis=0, tiled=True)
    wk = lax.all_gather(ffn_key, "dp", axis=0, tiled=True)
    wv = lax.all_gather(ffn_value, "dp", axis=0, tiled=True)
    wi = [pack[:, i * width:(i + 1) * width] for i in range(3)]
    wo = pack[:, 3 * width:4 * width]
    base = 4 * width
    w_in = pack[:, base:base + CUTS[4]]
    w_out = pack[:, base + CUTS[4]:base + 2 * CUTS[4]]
    small = pack[:, base + 2 * CUTS[4]:].T.astype(f32)
    mix, gains, biases, tying = small[0:7], small[7:10], small[10:13], small[13:15]
    par = jnp.concatenate([small[13:19], gains[1:2], biases[1:2]], 0)

    x = x_in.reshape(rows, width).astype(f32)
    first = first_in.reshape(rows, width)
    place = jnp.arange(length, dtype=jnp.int32)
    valid = (place[None, None, :] < spans[:, :, None]).astype(f32).reshape(rows, 1)
    g_out = valid * gout_in.reshape(rows, width).astype(f32)
    gf = g_out.astype(bf16)

    xs, pull_front = jax.vjp(front, x, mix[:6], gains[0], biases[0])
    xs = [z.astype(bf16) for z in xs]
    proj = [mmt(xs[j], wi[i]) for i, j in enumerate((0, 2, 3))]
    zs = [mm(xs[j], w_in[:, CUTS[i]:CUTS[i + 1]]) for i, j in enumerate(LOW_FROM)]
    ls, pull_low = jax.vjp(lowrank_act, *zs)
    ls = [z.astype(bf16) for z in ls]
    os_ = [mmt(ls[i], w_out[:, CUTS[i]:CUTS[i + 1]]) for i in range(4)]
    args = (*proj, *os_, first)
    gated, *saved = mixer_fwd(args, par)
    mixed = x + mmt(gated, wo)
    (xc,), pull_chan = jax.vjp(front, mixed, mix[6:7], gains[2], biases[2])
    xc = xc.astype(bf16)
    pre = jax.nn.relu(mm(xc, wk))
    hidden = (pre * pre).astype(bf16)
    out = valid * (mixed + mm(hidden, wv))

    core = lax.axis_index("dp") % 2
    chips = lax.axis_size("dp") // 2
    scale = 1.0 / math.sqrt(rows * lax.axis_size("dp"))

    def cut(a, c):
        return pick(a.reshape(rows, chips, 2, -1), c, 2).reshape(rows, -1)

    def side(a, c):
        return lax.dynamic_slice_in_dim(a, c * (width // 2), width // 2, 1)

    d_value = on_core(tmm(cut(hidden, core), gf), tmm(cut(hidden, 1 - core), gf).astype(bf16))
    d_value = chip_sum_begin(by_chip(d_value))
    g_pre = (mmt(gf, wv) * (2.0 * pre)).astype(bf16)
    d_value, g_pre = tie(d_value, g_pre)
    d_key = on_core(tmm(xc, cut(g_pre, core)), tmm(xc, cut(g_pre, 1 - core)).astype(bf16))
    g_mixed, g_mix_c, g_gain_c, g_bias_c = pull_chan((mmt(g_pre, wk),))
    g_mixed = g_out + g_mixed
    g_att = g_mixed.astype(bf16)
    d_conc = on_core(tmm(g_att, side(gated, core)), tmm(g_att, side(gated, 1 - core)).astype(bf16))
    d_value = chip_sum_step(d_value)
    d_key = chip_sum_begin(by_chip(jnp.concatenate([d_key, d_conc], 1)))
    gg = mm(g_att, wo)
    gg, d_key, d_value = tie(gg, d_key, d_value)
    grads = mixer_bwd(args, par, saved, gg, 0, ())
    d_value = chip_sum_step(d_value)
    d_key = chip_sum_step(d_key)
    grads, d_key, d_value = tie(grads, d_key, d_value)
    grads = mixer_bwd(args, par, saved, gg, 1, grads)
    d_value = chip_sum_step(d_value)
    d_key = chip_sum_step(d_key)
    grads, d_key, d_value = tie(grads, d_key, d_value)
    d_value = chip_sum_end(chip_sum_step(d_value))
    d_key = chip_sum_end(chip_sum_step(d_key, 2))
    gp = jnp.sum(grads[8].reshape(-1, 8, width), 0)
    g_proj, g_os, g_first = grads[:3], grads[3:7], grads[7]
    g_ls = tuple(mm(g_os[i], w_out[:, CUTS[i]:CUTS[i + 1]]) for i in range(4))
    g_zs = [z.astype(bf16) for z in pull_low(g_ls)]
    back = [mmt(g_zs[i], w_in[:, CUTS[i]:CUTS[i + 1]]) for i in range(4)]
    g_xs = (mm(g_proj[0], wi[0]), back[0], mm(g_proj[1], wi[1]),
            mm(g_proj[2], wi[2]) + back[2], back[1], back[3])
    g_x, g_mix_t, g_gain_t, g_bias_t = pull_front(g_xs)
    g_x = g_mixed + g_x
    g_small = jnp.concatenate(
        [g_mix_t, g_mix_c, g_gain_t[None], gp[6:7], g_gain_c[None], g_bias_t[None], gp[7:8],
         g_bias_c[None], gp[0:6], jnp.zeros((13, width), f32)], 0).T
    fill = jnp.zeros((width, 80), f32)
    low_a = jnp.concatenate([tmm(xs[j], g_zs[i]) for i, j in enumerate(LOW_FROM)]
                            + [g_small[:, :16], fill], 1)
    low_b = jnp.concatenate([tmm(g_os[i], ls[i]) for i in range(4)] + [g_small[:, 16:], fill], 1)

    def mixer_half(c):
        return jnp.concatenate(
            [tmm(g_proj[i], side(xs[j], c)) for i, j in enumerate((0, 2, 3))]
            + [jnp.where(c == 0, low_a, low_b)], 1)

    d_mix = on_core(mixer_half(core), mixer_half(1 - core).astype(bf16))
    d_mix = chip_sum_end(chip_sum_step(chip_sum_begin(by_chip(d_mix)), 4))
    half_a, half_b = trade_rows(d_mix * scale)
    key_a, key_b = trade_rows(d_key * scale)
    hw = width // 2
    wide = [jnp.concatenate([half_a[:, i * hw:(i + 1) * hw], half_b[:, i * hw:(i + 1) * hw]], 1)
            for i in range(3)]
    d_in = jnp.stack([w.T for w in wide])
    low_a, low_b = half_a[:, 3 * hw:], half_b[:, 3 * hw:]
    d_conc = jnp.concatenate([key_a[:, -hw:], key_b[:, -hw:]], 1).T
    key_a, key_b = key_a[:, :-hw], key_b[:, :-hw]
    d_small = jnp.concatenate([low_a[:, CUTS[4]:CUTS[4] + 16], low_b[:, CUTS[4]:CUTS[4] + 16]], 1).T
    d_key = jnp.stack([key_a.reshape(shard, chips, -1), key_b.reshape(shard, chips, -1)], 2)
    d_key = d_key.reshape(shard, -1)
    return (
        out.astype(bf16).reshape(x_in.shape), g_x.astype(bf16).reshape(x_in.shape),
        g_first.reshape(x_in.shape), d_small[0:7], d_small[7:10], d_small[10:13],
        d_small[13:15], d_small[15], d_small[16], d_small[17:19],
        low_a[:, :CUTS[4]], low_b[:, :CUTS[4]].T, d_in, d_conc, d_key, d_value * scale)


def solution(mesh):
    tok, row, col = P(None, "dp", None, None), P("dp", None), P(None, "dp")
    vec, cube = P("dp"), P(None, None, "dp")
    in_specs = (tok, tok, col, tok, col, col, col, col, vec, vec, col, row, col, cube, col, row, row)
    out_specs = (tok, tok, tok, col, col, col, col, vec, vec, col, row, col, cube, col, row, row)
    return jax.shard_map(
        on_device, mesh=mesh, in_specs=in_specs, out_specs=out_specs, check_vma=False)
```

```python
import math

import jax
import jax.numpy as jnp
from jax import lax
from jax.experimental import pallas as pl
from jax.experimental.pallas import tpu as pltpu
from jax.sharding import PartitionSpec as P

bf16, f32 = jnp.bfloat16, jnp.float32
RANKS = (64, 64, 32, 128)
CUTS = (0, 64, 128, 160, 288)
LOW_FROM = (1, 4, 3, 5)
T = 128

def dn(x, y, cx, cy):
    return lax.dot_general(x, y, (((cx,), (cy,)), ((), ())), preferred_element_type=f32)

def split2(x):
    hi = x.astype(bf16)
    return hi, (x - hi.astype(f32)).astype(bf16)

def dot(x, y, cx=1, cy=0, passes=3):
    if passes == 1:
        return dn(x.astype(bf16), y.astype(bf16), cx, cy)
    xh, xl = split2(x); yh, yl = split2(y)
    return dn(xh, yh, cx, cy) + dn(xh, yl, cx, cy) + dn(xl, yh, cx, cy)

def ones_dot(left, x):
    hi = x.astype(bf16); r = x - hi.astype(f32)
    mid = r.astype(bf16); lo = (r - mid.astype(f32)).astype(bf16)
    w = x.shape[1]
    o = dn(left, jnp.concatenate([hi, mid, lo], 1), 1, 0)
    return o[:, :w] + o[:, w:2*w] + o[:, 2*w:]

def head_sum(x, J):
    hi, lo = split2(x)
    return dn(jnp.concatenate([hi, lo], 1), jnp.concatenate([J, J], 0), 1, 0)

def sig(z):
    return 1.0 / (1.0 + jnp.exp(-z))

def iota(shape, d):
    return lax.broadcasted_iota(jnp.int32, shape, d)

def consts():
    r, c = iota((T, T), 0), iota((T, T), 1)
    J = jnp.where((r // 64) == (c // 64), 1.0, 0.0).astype(bf16)
    low = jnp.where(r >= c, 1.0, 0.0).astype(bf16)
    up = jnp.where(r <= c, 1.0, 0.0).astype(bf16)
    h0 = c < 64
    return r, c, J, low, up, h0

def halves(x, h0):
    z = jnp.zeros_like(x)
    m = h0 if x.shape[0] == T else jnp.concatenate([h0, h0], 0)
    return jnp.where(m, x, z), jnp.where(m, z, x)

def prep(r_, kx, vx, ow, oa, ov, first, par, K):
    r, c, J, low, up, h0 = K
    dk0, dk1, bonus, db, sq0, sq1 = (par[i:i+1] for i in range(6))
    sg = sig(db + ow)
    ld = sg * (-0.6065306597126334)
    cum = ones_dot(low, ld)
    cm = cum - cum[63:64]
    G = jnp.exp(cm); S = jnp.exp(-cm); B = jnp.exp(cm - ld)
    ag = sig(sq0 + oa); vg = sig(sq1 + ov)
    v2 = vx + (first - vx) * vg
    kfac = 1.0 + (ag - 1.0) * dk1
    km = kx * kfac
    cc = kx * dk0
    n = lax.rsqrt(head_sum(cc * cc, J) + 1e-6)
    kk = cc * n
    return sg, ld, G, S, B, ag, vg, v2, kfac, km, n, kk

def inverse(N0, N1, K, passes):
    r, c = K[0], K[1]
    z = jnp.zeros((T, T), f32)
    eye = jnp.where(r == c, 1.0, 0.0)
    m = ((r // 2) == (c // 2))
    T0 = eye + jnp.where(m, N0, 0.0); T1 = eye + jnp.where(m, N1, 0.0)
    s = 2
    def bd(a, b):
        return jnp.concatenate([jnp.concatenate([a, z], 1), jnp.concatenate([z, b], 1)], 0)
    TT = jnp.concatenate([T0, T1], 1)
    while s < T:
        m = ((r // (2*s)) == (c // (2*s))) & ((r // s) != (c // s))
        o = dot(TT, bd(jnp.where(m, N0, 0.0), jnp.where(m, N1, 0.0)), passes=passes)
        TT = TT + dot(o, bd(TT[:, :T], TT[:, T:]), passes=passes)
        s *= 2
    res = jnp.concatenate([eye, eye], 1) - TT + dot(jnp.concatenate([N0, N1], 1), bd(TT[:, :T], TT[:, T:]))
    return TT + dot(TT, bd(res[:, :T], res[:, T:]), passes=1)

def fwd_core(r_, kx, vx, ow, oa, ov, og, first, par, pA=3, pI=1, pO=3):
    K = consts(); r, c, J, low, up, h0 = K
    sg, ld, G, S, B, ag, vg, v2, kfac, km, n, kk = prep(r_, kx, vx, ow, oa, ov, first, par, K)
    at = -kk * B; rt = r_ * G; bt = kk * ag * S; kt = km * S
    Q = jnp.concatenate([at, rt], 0); Kf = jnp.concatenate([bt, kt], 0)
    Q0, Q1 = halves(Q, h0)
    A0 = dot(Q0, Kf, 1, 1, pA); A1 = dot(Q1, Kf, 1, 1, pA)
    st = r > c; inc = r >= c
    def msk(A):
        return (jnp.where(st, A[:T, :T], 0.0), jnp.where(st, A[:T, T:], 0.0),
                jnp.where(inc, A[T:, :T], 0.0), jnp.where(inc, A[T:, T:], 0.0))
    ab0, ak0, rb0, rk0 = msk(A0); ab1, ak1, rb1, rk1 = msk(A1)
    TT = inverse(ab0, ab1, K, pI)
    v0, v1 = halves(v2, h0)
    Pm = dot(jnp.concatenate([ak0, ak1], 1), jnp.concatenate([v0, v1], 0), passes=pO)
    U = dot(TT, jnp.concatenate(halves(Pm, h0), 0), passes=pO)
    u0, u1 = halves(U, h0)
    Y = dot(jnp.concatenate([rb0, rk0, rb1, rk1], 1), jnp.concatenate([u0, v0, u1, v1], 0), passes=pO)
    mean = head_sum(Y, J) * (1/64)
    cy = Y - mean
    rstd = lax.rsqrt(head_sum(cy * cy, J) * (1/64) + 4.0)
    bonus, gain, bias = par[2:3], par[6:7], par[7:8]
    bs = head_sum(r_ * km * bonus, J)
    out = (cy * rstd * gain + bias + bs * v2) * og
    return out, TT, U, Y

def bwd_core(r_, kx, vx, ow, oa, ov, og, first, par, TT, U, Y, gg, pA=3, pW=3, pD=3):
    K = consts(); r, c, J, low, up, h0 = K
    dk0, dk1, bonus, db, sq0, sq1, gain, bias = (par[i:i+1] for i in range(8))
    sg, ld, G, S, B, ag, vg, v2, kfac, km, n, kk = prep(r_, kx, vx, ow, oa, ov, first, par, K)
    at = -kk * B; rt = r_ * G; bt = kk * ag * S; kt = km * S
    mean = head_sum(Y, J) * (1/64)
    cy = Y - mean
    rstd = lax.rsqrt(head_sum(cy * cy, J) * (1/64) + 4.0)
    gn = cy * rstd
    bs = head_sum(r_ * km * bonus, J)
    g_og = gg * (gn * gain + bias + bs * v2)
    gi = gg * og
    g_gn = gi * gain
    gY = rstd * (g_gn - head_sum(g_gn, J) * (1/64) - gn * (head_sum(g_gn * gn, J) * (1/64)))
    g_bs = head_sum(gi * v2, J)
    Q = jnp.concatenate([at, rt], 0); Kf = jnp.concatenate([bt, kt], 0)
    Q0, Q1 = halves(Q, h0)
    At0 = dot(Kf, Q0, 1, 1, pA); At1 = dot(Kf, Q1, 1, 1, pA)
    st = r < c; inc = r <= c
    akT = jnp.concatenate([jnp.where(st, At0[T:, :T], 0.0), jnp.where(st, At1[T:, :T], 0.0)], 1)
    inc2 = jnp.concatenate([inc, inc], 0)
    rT = jnp.concatenate([jnp.where(inc2, At0[:, T:], 0.0), jnp.where(inc2, At1[:, T:], 0.0)], 1)
    gy0, gy1 = halves(gY, h0)
    dUV = dot(rT, jnp.concatenate([gy0, gy1], 0), passes=pW)
    dU, dV = dUV[:T], dUV[T:]
    R = dot(TT, dU, 0, 0, pW)
    W = jnp.where(h0, R[:T], R[T:])
    w0, w1 = halves(W, h0)
    dV = dV + dot(akT, jnp.concatenate([w0, w1], 0), passes=pW)
    X = jnp.concatenate([U, v2], 0)
    Yg0 = jnp.concatenate([w0, gy0], 0); Yg1 = jnp.concatenate([w1, gy1], 0)
    r2, c2 = iota((2*T, 2*T), 0), iota((2*T, 2*T), 1)
    keep = ((r2 & 127) > (c2 & 127)) | ((r2 >= T) & ((r2 & 127) == (c2 & 127)))
    keepT = ((r2 & 127) < (c2 & 127)) | ((c2 >= T) & ((r2 & 127) == (c2 & 127)))
    dA0 = jnp.where(keep, dot(Yg0, X, 1, 1, pD), 0.0)
    dA1 = jnp.where(keep, dot(Yg1, X, 1, 1, pD), 0.0)
    dT0 = jnp.where(keepT, dot(X, Yg0, 1, 1, pD), 0.0)
    dT1 = jnp.where(keepT, dot(X, Yg1, 1, 1, pD), 0.0)
    K0, K1 = halves(Kf, h0)
    dQ = dot(jnp.concatenate([dA0, dA1], 1), jnp.concatenate([K0, K1], 0), passes=pD)
    dK = dot(jnp.concatenate([dT0, dT1], 1), jnp.concatenate([Q0, Q1], 0), passes=pD)
    da_, dr_ = dQ[:T], dQ[T:]; db_, dk_ = dK[:T], dK[T:]
    e = dr_ * rt - db_ * bt - dk_ * kt
    f = da_ * at
    g_ld = ones_dot(up, e + f) - f
    g_kk = db_ * S * ag - da_ * B
    g_b = db_ * S
    g_km = g_bs * r_ * bonus + dk_ * S
    g_r = g_bs * km * bonus + dr_ * G
    g_ag = g_b * kk + g_km * kx * dk1
    g_c = n * (g_kk - kk * head_sum(g_kk * kk, J))
    g_kx = g_km * kfac + g_c * dk0
    g_v2 = gi * bs + dV
    g_first = g_v2 * vg
    g_vx = g_v2 - g_first
    g_ov = g_first * (1.0 - vg) * (first - vx)
    g_oa = g_ag * ag * (1.0 - ag)
    g_ow = g_ld * ld * (1.0 - sg)
    def cs(x): return jnp.sum(x, 0, keepdims=True)
    pg = jnp.concatenate([cs(g_c * kx), cs(g_km * kx * (ag - 1.0)), cs(g_bs * r_ * km),
                          cs(g_ow), cs(g_oa), cs(g_ov), cs(gi * gn), cs(gi)], 0)
    return g_r, g_kx, g_vx, g_ow, g_oa, g_ov, g_og, g_first, pg


def fwd_kernel(*refs):
    ins, par, outs = refs[:8], refs[8], refs[9:]
    for q in range(2):
        rows = pl.ds(q * T, T)
        vals = [ref[rows, :] for ref in ins]
        res = fwd_core(*vals[:7], vals[7].astype(f32), par[...])
        outs[0][rows, :] = res[0].astype(bf16)
        for ref, val in zip(outs[1:], res[1:]):
            ref[rows, :] = val


def bwd_kernel(*refs):
    ins, par, saved, outs = refs[:8], refs[8], refs[9:13], refs[13:]
    for q in range(2):
        rows = pl.ds(q * T, T)
        vals = [ref[rows, :] for ref in ins]
        res = bwd_core(*vals[:7], vals[7].astype(f32), par[...], *[ref[rows, :] for ref in saved])
        for ref, val in zip(outs[:8], res[:8]):
            ref[rows, :] = val.astype(bf16)
        outs[8][pl.ds(q * 8, 8), :] = res[8]
        for ref, val in zip(outs[9:], res[:3]):
            ref[rows, :] = val.astype(bf16)


MIXER = dict(
    compiler_params=pltpu.CompilerParams(vmem_limit_bytes=32 * 1024 * 1024),
    cost_estimate=pl.CostEstimate(flops=10 * 10**9, bytes_accessed=10**7, transcendentals=10**6))


def mixer_fwd(args, par, part, before):
    rows, width = args[0].shape
    seqs, pairs = rows // T, width // 128
    p0 = part * (pairs // 4)
    tile = pl.BlockSpec((2 * T, 128), lambda s, p: (s, p + p0))
    pspec = pl.BlockSpec((8, 128), lambda s, p: (0, p + p0))
    inv = pl.BlockSpec((2 * T, 2 * T), lambda s, p: (s * pairs + p + p0, 0))
    wide = jax.ShapeDtypeStruct((rows, width), f32)

    def body(*refs):
        fwd_kernel(*refs[:9], *refs[9 + len(before):])

    return pl.pallas_call(
        body,
        grid=(seqs // 2, pairs // 4),
        in_specs=[tile] * 8 + [pspec] + [pl.BlockSpec(memory_space=pl.ANY)] * len(before),
        out_specs=[tile, inv, tile, tile],
        out_shape=[jax.ShapeDtypeStruct((rows, width), bf16),
                   jax.ShapeDtypeStruct((rows * pairs, 2 * T), f32), wide, wide],
        input_output_aliases={9 + i: i for i in range(len(before))},
        name="mixer_fwd",
        **MIXER,
    )(*args, par, *before)


def mixer_bwd(args, par, saved, gg, side, part, before):
    rows, width = args[0].shape
    seqs, pairs = rows // T, width // 128
    keep, p0 = part // 2, part % 2 * (pairs // 4)

    def pair(p, side):
        return 2 * (p + p0) + (side[0] if keep else 1 - side[0])

    tile = pl.BlockSpec((2 * T, 128), lambda s, p, side: (s, pair(p, side)))
    pspec = pl.BlockSpec((8, 128), lambda s, p, side: (0, pair(p, side)))
    inv = pl.BlockSpec((2 * T, 2 * T), lambda s, p, side: (s * pairs + pair(p, side), 0))
    gpar = pl.BlockSpec((16, 128), lambda s, p, side: (s, pair(p, side)))
    rel = pl.BlockSpec((2 * T, 128), lambda s, p, side: (s, p + p0 + keep * (pairs // 2)))
    thin = jax.ShapeDtypeStruct((rows, width), bf16)

    def body(*refs):
        bwd_kernel(*refs[1:14], *refs[14 + len(before):])

    return pl.pallas_call(
        body,
        grid_spec=pltpu.PrefetchScalarGridSpec(
            num_scalar_prefetch=1,
            grid=(seqs // 2, pairs // 4),
            in_specs=[tile] * 8 + [pspec, inv, tile, tile, tile]
            + [pl.BlockSpec(memory_space=pl.ANY)] * len(before),
            out_specs=[tile] * 8 + [gpar] + [rel] * 3),
        out_shape=[thin] * 8 + [jax.ShapeDtypeStruct((seqs * 8, width), f32)] + [thin] * 3,
        input_output_aliases={14 + i: i for i in range(len(before))},
        name="mixer_bwd",
        **MIXER,
    )(side, *args, par, *saved, gg, *before)


def ffn_kernel(xc, xct, gf, wk, wv, hid, gpre, gx, *grads):
    pre = jnp.maximum(mm(xc[...], wk[...]), 0.0)
    h = (pre * pre).astype(bf16)
    hid[...] = h
    g = (mmt(gf[...], wv[...]) * (2.0 * pre)).astype(bf16)
    gpre[...] = g
    if grads:
        d_val, d_key = grads
        d_val[...] = tmm(h, gf[...]).astype(bf16)
        d_key[...] = mm(xct[...], g).astype(bf16)
    g = mmt(g, wk[...])

    @pl.when(pl.program_id(0) == 0)
    def _():
        gx[...] = g

    @pl.when(pl.program_id(0) > 0)
    def _():
        gx[...] += g


FFN_BLOCK = 512


def ffn_params(name):
    return dict(
        compiler_params=pltpu.CompilerParams(vmem_limit_bytes=32 * 1024 * 1024),
        cost_estimate=pl.CostEstimate(flops=5 * 10**9, bytes_accessed=10**7, transcendentals=0),
        name=name)


def ffn_half(xc, xct, gf, wk, wv, with_grads):
    rows, width = xc.shape
    units = wv.shape[0]
    tall = pl.BlockSpec((rows, width), lambda j: (0, 0))
    unit = pl.BlockSpec((rows, FFN_BLOCK), lambda j: (0, j))
    down = pl.BlockSpec((FFN_BLOCK, width), lambda j: (j, 0))
    across = pl.BlockSpec((width, FFN_BLOCK), lambda j: (0, j))
    hidden = jax.ShapeDtypeStruct((rows, units), bf16)
    more = with_grads * 1
    return pl.pallas_call(
        ffn_kernel,
        grid=(units // FFN_BLOCK,),
        in_specs=[tall, pl.BlockSpec((width, rows), lambda j: (0, 0)), tall, across, down],
        out_specs=[unit, unit, tall] + [down, across] * more,
        out_shape=[hidden, hidden, jax.ShapeDtypeStruct((rows, width), f32)]
        + [jax.ShapeDtypeStruct((units, width), bf16), jax.ShapeDtypeStruct((width, units), bf16)] * more,
        **ffn_params("ffn_half"),
    )(xc, xct, gf, wk, wv)


def grad_kernel(xct, gf, hid, gpre, val_got, key_got, d_val, d_key):
    d_val[...] = (tmm(hid[...], gf[...]) + val_got[...].astype(f32)).astype(bf16)
    d_key[...] = (mm(xct[...], gpre[...]) + key_got[...].astype(f32)).astype(bf16)


def ffn_grads(xct, gf, hid, gpre, val_got, key_got):
    width, rows = xct.shape
    units = hid.shape[1]
    unit = pl.BlockSpec((rows, FFN_BLOCK), lambda j: (0, j))
    down = pl.BlockSpec((FFN_BLOCK, width), lambda j: (j, 0))
    across = pl.BlockSpec((width, FFN_BLOCK), lambda j: (0, j))
    return pl.pallas_call(
        grad_kernel,
        grid=(units // FFN_BLOCK,),
        in_specs=[pl.BlockSpec((width, rows), lambda j: (0, 0)),
                  pl.BlockSpec((rows, width), lambda j: (0, 0)), unit, unit, down, across],
        out_specs=[down, across],
        out_shape=[jax.ShapeDtypeStruct((units, width), bf16),
                   jax.ShapeDtypeStruct((width, units + width // 2), bf16)],
        **ffn_params("ffn_grads"),
    )(xct, gf, hid, gpre, val_got, key_got)


def conc_kernel(att, gated, got, before, d_key):
    d_key[...] = (tmm(att[...], gated[...]) + got[...].astype(f32)).astype(bf16)


def conc_grad(att, gated, got, d_key):
    rows, width = att.shape
    cols = gated.shape[1]
    last = d_key.shape[1] // cols - 1
    return pl.pallas_call(
        conc_kernel,
        grid=(1,),
        in_specs=[pl.BlockSpec((rows, width), lambda j: (0, 0)),
                  pl.BlockSpec((rows, cols), lambda j: (0, 0)),
                  pl.BlockSpec((width, cols), lambda j: (0, 0)),
                  pl.BlockSpec(memory_space=pl.ANY)],
        out_specs=pl.BlockSpec((width, cols), lambda j: (0, last)),
        out_shape=jax.ShapeDtypeStruct(d_key.shape, bf16),
        input_output_aliases={3: 0},
        **ffn_params("conc_grad"),
    )(att, gated, got, d_key)


def layer_norm(x, gain, bias):
    c = x - jnp.mean(x, -1, keepdims=True)
    return c * lax.rsqrt(jnp.mean(c * c, -1, keepdims=True) + 1e-5) * gain + bias


def prev(z):
    z = z.reshape(-1, T, z.shape[-1])
    z = jnp.concatenate([jnp.zeros_like(z[:, :1]), z[:, :-1]], 1)
    return z.reshape(-1, z.shape[-1])


def front(x, mix, gain, bias):
    h = layer_norm(x, gain, bias)
    d = prev(h) - h
    return tuple(h + d * mix[i] for i in range(mix.shape[0]))


def mm(a, b):
    return dn(a, b, 1, 0)


def mmt(a, b):
    return dn(a, b, 1, 1)


def tmm(a, b):
    return dn(a, b, 0, 0)


def lowrank_act(zw, za, zv, zg):
    return jnp.tanh(zw), za, zv, jax.nn.sigmoid(zg)


def swap(x, bit):
    n = lax.axis_size("dp")
    return lax.ppermute(x, "dp", [(i, i ^ bit) for i in range(n)])


def add(a, b):
    return (a.astype(f32) + b.astype(f32)).astype(bf16)


def pick(x, index, axis):
    return lax.dynamic_index_in_dim(x, index, axis, keepdims=False)


BOTH = (((2, 4), (3, 2)), ((2, 2), (2, 4)), ((1, 8), (1, 8)), ((0, 16), (0, 16)))
ONE = (((2, 4),), ((2, 2),), ((1, 8),), ((0, 16),))
TAIL = (((2, 2), (1, 8)), ((1, 8), (0, 16)), ((0, 16), (0, 2)))


def side_of(bit):
    return (lax.axis_index("dp") // bit) % 2


def sum_send(parts, step):
    return [swap(pick(part, 1 - side_of(bit), axis), bit) for part, (axis, bit) in zip(parts, step)]


def sum_take(parts, got, step):
    return [add(pick(part, side_of(bit), axis), g) for part, g, (axis, bit) in zip(parts, got, step)]


def two(g):
    g = g.reshape(2, 2, 2, 2, g.shape[0] // 16, g.shape[1])
    cut = g.shape[4] // 2
    return [g[..., :cut, :], g[..., cut:, :]]


def whole_sum(g):
    n = lax.axis_size("dp")
    groups = [list(range(c, n, 2)) for c in range(2)]
    g = g.reshape(n // 2, g.shape[0] // (n // 2), g.shape[1])
    return lax.psum_scatter(g, "dp", scatter_dimension=0, axis_index_groups=groups).astype(f32)


def join(a, b, axis, bit):
    mine = (lax.axis_index("dp") // bit) % 2
    return jnp.where(mine == 0, jnp.stack([a, b], axis), jnp.stack([b, a], axis))


def gather_send(parts, step):
    if lax.axis_size("dp") != 32:
        return parts
    return [swap(p, bit) for p, (axis, bit) in zip(parts, BOTH[3 - step])]


def gather_take(parts, got, step):
    if lax.axis_size("dp") != 32:
        return parts
    return [join(p, g, axis, bit) for p, g, (axis, bit) in zip(parts, got, BOTH[3 - step])]


def gather_step(parts, step):
    return gather_take(parts, gather_send(parts, step), step)


def chip_gather_end(parts):
    n = lax.axis_size("dp")
    if n != 32:
        groups = [list(range(c, n, 2)) for c in range(2)]
        return [lax.all_gather(p, "dp", axis=0, axis_index_groups=groups, tiled=True) for p in parts]
    return [p.reshape(-1, p.shape[-1]) for p in parts]


def tie(*values):
    return lax.optimization_barrier(values)


def on_core(keep, send):
    return (keep + swap(send, 1).astype(f32)).astype(bf16)


def trade_rows(h):
    core = lax.axis_index("dp") % 2
    h = h.reshape(2, h.shape[0] // 2, h.shape[1])
    own, got = pick(h, core, 0), swap(pick(h, 1 - core, 0).astype(bf16), 1).astype(f32)
    return jnp.where(core == 0, own, got), jnp.where(core == 0, got, own)


def on_device(x_in, first_in, spans, gout_in, mix, gains, biases, tying, extra, dwindle,
              squash, reducing, enlarging, ingoing, concluding, ffn_key, ffn_value):
    micro, seqs, length, width = x_in.shape
    rows = micro * seqs * length
    shard = mix.shape[1]
    core = lax.axis_index("dp") % 2
    chips = lax.axis_size("dp") // 2
    half = width // 2
    small = jnp.concatenate([mix, gains, biases, tying, extra[None], dwindle[None], squash], 0)
    n_small = small.shape[0]
    fill = jnp.zeros((80, shard), bf16)
    low_a = jnp.concatenate([reducing, jnp.concatenate([small[:16], fill], 0).T], 1)
    low_b = jnp.concatenate(
        [enlarging, small[16:], jnp.zeros((16 - n_small + 16, shard), bf16), fill], 0).T
    turned = jnp.swapaxes(ingoing, 1, 2)
    q_halves = jnp.stack([jnp.concatenate([turned[0][:, c * half:(c + 1) * half],
                                           turned[1][:, c * half:(c + 1) * half]], 1)
                          for c in range(2)])
    r_halves = jnp.stack([jnp.concatenate([turned[2][:, c * half:(c + 1) * half], low], 1)
                          for c, low in enumerate((low_a, low_b))])
    keys = ffn_key.reshape(shard, chips, 2, -1)
    k_halves = jnp.stack([jnp.concatenate([keys[:, :, c].reshape(shard, -1),
                                           concluding.T[:, c * half:(c + 1) * half]], 1)
                          for c in range(2)])

    def trade(halves):
        own, sent = pick(halves, core, 0), pick(halves, 1 - core, 0)
        return join(own, swap(sent, 1), 0, 1).reshape(2 * shard, -1)

    mixer = [trade(q_halves), trade(r_halves)]
    mixer = gather_step(gather_step(mixer, 0), 1)
    ffn = [trade(k_halves), ffn_value]
    mixer, ffn = tie(mixer, ffn)

    def one_send(p, step, which):
        axis, bit = BOTH[3 - step][which]
        return swap(p, bit) if lax.axis_size("dp") == 32 else p

    def one_take(p, got, step, which):
        axis, bit = BOTH[3 - step][which]
        return join(p, got, axis, bit) if lax.axis_size("dp") == 32 else p

    got, k_got = tie(gather_send(mixer, 2), one_send(ffn[0], 0, 0))
    mixer = gather_take(mixer, got, 2)
    f_key, f_val = one_take(ffn[0], k_got, 0, 0), ffn[1]
    got, k_got, v_got = tie(gather_send(mixer, 3), one_send(f_key, 1, 0), one_send(f_val, 0, 1))
    f_key, f_val = one_take(f_key, k_got, 1, 0), one_take(f_val, v_got, 0, 1)
    got, f_key, f_val = tie(got, f_key, f_val)
    v_got, k_got = one_send(f_val, 1, 1), one_send(f_key, 2, 0)
    mixer = chip_gather_end(gather_take(mixer, got, 3))
    far = [swap(p, 1) for p in mixer]

    def in_core_order(a, b, axis):
        return jnp.where(core == 0, jnp.concatenate([a, b], axis), jnp.concatenate([b, a], axis))

    wi = [(mixer[0][:, :half], far[0][:, :half]), (mixer[0][:, half:], far[0][:, half:]),
          (mixer[1][:, :half], far[1][:, :half])]
    low_a = jnp.where(core == 0, mixer[1][:, half:], far[1][:, half:])
    low_b = jnp.where(core == 0, far[1][:, half:], mixer[1][:, half:])
    w_in, w_out = low_a[:, :CUTS[4]], low_b[:, :CUTS[4]]
    small = jnp.concatenate([low_a[:, CUTS[4]:CUTS[4] + 16], low_b[:, CUTS[4]:CUTS[4] + 16]], 1)
    small = small.T.astype(f32)
    mix, gains, biases, tying = small[0:7], small[7:10], small[10:13], small[13:15]

    def by_core(a):
        return in_core_order(a[..., :half], a[..., half:], -1)

    par = jnp.concatenate([small[13:19], gains[1:2], biases[1:2]], 0)

    x = x_in.reshape(rows, width).astype(f32)
    first = first_in.reshape(rows, width)
    place = jnp.arange(length, dtype=jnp.int32)
    valid = (place[None, None, :] < spans[:, :, None]).astype(f32).reshape(rows, 1)
    g_out = valid * gout_in.reshape(rows, width).astype(f32)
    gf = g_out.astype(bf16)

    xs, pull_front = jax.vjp(front, by_core(x), by_core(mix[:6]), by_core(gains[0]), by_core(biases[0]))
    xs = [z.astype(bf16) for z in xs]
    xs, v_got, gf = tie(xs, v_got, gf)
    f_val = one_take(f_val, v_got, 1, 1)
    v_got = one_send(f_val, 2, 1)
    proj = [mmt(xs[j][:, :half], wi[i][0]) + mmt(xs[j][:, half:], wi[i][1])
            for i, j in enumerate((0, 2, 3))]
    w_in = in_core_order(w_in[:half], w_in[half:], 0)
    zs = [mm(xs[j], w_in[:, CUTS[i]:CUTS[i + 1]]) for i, j in enumerate(LOW_FROM)]
    ls, pull_low = jax.vjp(lowrank_act, *zs)
    ls = [z.astype(bf16) for z in ls]
    os_ = [mmt(ls[i], w_out[:, CUTS[i]:CUTS[i + 1]]) for i in range(4)]
    args = (*proj, *os_, first)
    done = mixer_fwd(args, par, 0, ())
    done, k_got, v_got = tie(done, k_got, v_got)
    ffn = [one_take(f_key, k_got, 2, 0), one_take(f_val, v_got, 2, 1)]
    ffn_got = gather_send(ffn, 3)
    for part in (1, 2, 3):
        done = mixer_fwd(args, par, part, done)
    done, ffn_got = tie(done, ffn_got)
    ffn = chip_gather_end(gather_take(ffn, ffn_got, 3))
    gated, *saved = done
    wk, wv = ffn
    wo = wk[:, -half:]
    wo_far, wk, wv = tie(swap(wo, 1), wk, wv)
    wk_far, wv_far = swap(wk, 1), swap(wv, 1)

    def side(a, c):
        return lax.dynamic_slice_in_dim(a, c * half, half, 1)

    gated_near, gated_far = side(gated, core), side(gated, 1 - core)
    mixed = x + mmt(gated_near, wo) + mmt(gated_far, wo_far)
    (xc,), pull_chan = jax.vjp(front, mixed, mix[6:7], gains[2], biases[2])
    xc = xc.astype(bf16)
    xct = xc.T
    hidden, g_pre, g_xc = ffn_half(xc, xct, gf, wk, wv, False)
    g_pre, wk_far, wv_far = tie(g_pre, wk_far, wv_far)
    hidden_far, _, g_xc_far, val_far, key_far = ffn_half(xc, xct, gf, wk_far, wv_far, True)

    scale = 1.0 / math.sqrt(rows * lax.axis_size("dp"))

    small_slice = lax.axis_size("dp") == 32
    side_y = lax.axis_index("dp") // 4 % 2 if small_slice else jnp.int32(0)
    side_y = side_y.reshape(1)
    steps = BOTH if small_slice else ((), (), (), ())

    def start(g):
        return two(g) if small_slice else whole_sum(g)

    def send(parts, step):
        return sum_send(parts, steps[step]) if small_slice else []

    def take(parts, got, step):
        return sum_take(parts, got, steps[step]) if small_slice else parts

    def finish(parts):
        return jnp.concatenate(parts, 0).astype(f32) if small_slice else parts

    val_got, key_got = swap(val_far, 1), swap(key_far, 1)
    g_mixed, g_mix_c, g_gain_c, g_bias_c = pull_chan((g_xc + g_xc_far,))
    g_mixed = g_out + g_mixed
    g_att = g_mixed.astype(bf16)
    conc_got = swap(tmm(g_att, gated_far).astype(bf16), 1)
    gg = in_core_order(mm(g_att, wo), mm(g_att, wo_far), 1)
    gg, val_got, key_got, conc_got = tie(gg, val_got, key_got, conc_got)
    d_value, d_key = ffn_grads(xct, gf, hidden, g_pre, val_got, key_got)
    d_key = conc_grad(g_att, gated_near, conc_got, d_key)
    d_value, d_key = start(d_value), start(d_key)
    v_got, k_got = send(d_value, 0), send(d_key, 0)
    gg, d_value, d_key = tie(gg, d_value, d_key)
    grads = mixer_bwd(args, par, saved, gg, side_y, 0, ())
    grads, v_got = tie(grads, v_got)
    d_value = take(d_value, v_got, 0)
    v_got = send(d_value, 1)
    grads = mixer_bwd(args, par, saved, gg, side_y, 1, grads)

    def proj_part(near, keep):
        cols = slice(0, half) if near else slice(half, width)
        outs = slice(half, width) if keep else slice(0, half)
        return jnp.concatenate(
            [tmm(grads[9 + i][:, outs], xs[j][:, cols]) for i, j in enumerate((0, 2, 3))], 1)

    away = on_core(proj_part(True, False), proj_part(False, False).astype(bf16))
    grads = mixer_bwd(args, par, saved, gg, side_y, 2, grads)
    grads, v_got, k_got, away = tie(grads, v_got, k_got, away)
    d_value, d_key = take(d_value, v_got, 1), take(d_key, k_got, 0)
    v_got, k_got = send(d_value, 2), send(d_key, 1)
    if small_slice:
        away = swap(away, 4)
    grads = mixer_bwd(args, par, saved, gg, side_y, 3, grads)
    grads, v_got, k_got = tie(grads, v_got, k_got)
    d_value, d_key = take(d_value, v_got, 2), take(d_key, k_got, 1)
    v_got, k_got = send(d_value, 3), send(d_key, 2)
    home = proj_part(True, True) + swap(proj_part(False, True).astype(bf16), 1).astype(f32)
    gp = jnp.sum(grads[8].reshape(-1, 8, width), 0)
    g_proj, g_os, g_first = grads[:3], grads[3:7], grads[7]
    g_ls = tuple(mm(g_os[i], w_out[:, CUTS[i]:CUTS[i + 1]]) for i in range(4))
    g_zs = [z.astype(bf16) for z in pull_low(g_ls)]
    back = [mmt(g_zs[i], w_in[:, CUTS[i]:CUTS[i + 1]]) for i in range(4)]

    def down(i):
        return jnp.concatenate([mm(g_proj[i], wi[i][0]), mm(g_proj[i], wi[i][1])], 1)

    g_xs = (down(0), back[0], down(1), down(2) + back[2], back[1], back[3])
    low_a = jnp.concatenate([tmm(xs[j], g_zs[i]) for i, j in enumerate(LOW_FROM)], 1)
    low_a = in_core_order(low_a[:half], low_a[half:], 0)
    low_b = jnp.concatenate([tmm(g_os[i], ls[i]) for i in range(4)], 1)
    d_low = on_core(jnp.where(core == 0, low_a, low_b),
                    jnp.where(core == 0, low_b, low_a).astype(bf16))
    if small_slice:
        d_low = [d_low.reshape(2, 2, 2, 2, 64, -1)]
        l_got = sum_send(d_low, ONE[0])
    if small_slice:
        g_xs, away, home, v_got, k_got, l_got = tie(g_xs, away, home, v_got, k_got, l_got)
        d_proj = (home + away.astype(f32)).astype(bf16)
        d_proj = d_proj.reshape(2, 2, 2, 64, d_proj.shape[1])
        d_proj = [d_proj[..., :32, :], d_proj[..., 32:, :]]
        d_key, d_low = take(d_key, k_got, 2), sum_take(d_low, l_got, ONE[0])
        p_got, l_got, k_got = sum_send(d_proj, TAIL[0]), sum_send(d_low, ONE[1]), send(d_key, 3)
    g_x, g_mix_t, g_gain_t, g_bias_t = pull_front(g_xs)
    g_x = g_mixed + by_core(g_x)
    g_mix_t, g_gain_t, g_bias_t = by_core(g_mix_t), by_core(g_gain_t), by_core(g_bias_t)
    d_small = jnp.concatenate(
        [g_mix_t, g_mix_c, g_gain_t[None], gp[6:7], g_gain_c[None], g_bias_t[None], gp[7:8],
         g_bias_c[None], gp[0:6], jnp.zeros((5, width), f32)], 0)
    if small_slice:
        d_small, p_got, l_got, hidden, hidden_far = tie(d_small, p_got, l_got, hidden, hidden_far)
        d_proj, d_low = sum_take(d_proj, p_got, TAIL[0]), sum_take(d_low, l_got, ONE[1])
        p_got, l_got = sum_send(d_proj, TAIL[1]), sum_send(d_low, ONE[2])
        for bit in (1, 2, 4, 8, 16):
            d_small = d_small + swap(d_small, bit)
        out = mixed + mm(hidden, wv)
        out, p_got, l_got = tie(out, p_got, l_got)
        d_proj, d_low = sum_take(d_proj, p_got, TAIL[1]), sum_take(d_low, l_got, ONE[2])
        p_got, l_got = sum_send(d_proj, TAIL[2]), sum_send(d_low, ONE[3])
        out = valid * (out + mm(hidden_far, wv_far))
        d_proj = finish(sum_take(d_proj, p_got, TAIL[2]))
        d_low = finish(sum_take(d_low, l_got, ONE[3]))
    else:
        home = home.astype(bf16).reshape(width // 256, 1, 128, -1)
        d_proj = whole_sum(jnp.concatenate([home, away.reshape(home.shape)], 1).reshape(width, -1))
        d_low = whole_sum(d_low)
        d_small = lax.psum(d_small, "dp")
        out = valid * (mixed + mm(hidden, wv) + mm(hidden_far, wv_far))
    d_key = finish(take(d_key, k_got, 3))
    d_value = finish(take(d_value, v_got, 3))
    d_small = scale * lax.dynamic_slice_in_dim(d_small, lax.axis_index("dp") * shard, shard, 1)
    half_a, half_b = trade_rows(d_proj * scale)
    low_a, low_b = trade_rows(d_low * scale)
    key_a, key_b = trade_rows(d_key * scale)
    hw = half
    wide = [jnp.concatenate([half_a[:, i * hw:(i + 1) * hw], half_b[:, i * hw:(i + 1) * hw]], 1)
            for i in range(3)]
    d_in = jnp.stack([w.T for w in wide])
    d_conc = jnp.concatenate([key_a[:, -hw:], key_b[:, -hw:]], 1).T
    key_a, key_b = key_a[:, :-hw], key_b[:, :-hw]
    d_key = jnp.stack([key_a.reshape(shard, chips, -1), key_b.reshape(shard, chips, -1)], 2)
    d_key = d_key.reshape(shard, -1)
    return (
        out.astype(bf16).reshape(x_in.shape), g_x.astype(bf16).reshape(x_in.shape),
        g_first.reshape(x_in.shape), d_small[0:7], d_small[7:10], d_small[10:13],
        d_small[13:15], d_small[15], d_small[16], d_small[17:19],
        low_a, low_b.T, d_in, d_conc, d_key, d_value * scale)


def solution(mesh):
    tok, row, col = P(None, "dp", None, None), P("dp", None), P(None, "dp")
    vec, cube = P("dp"), P(None, None, "dp")
    in_specs = (tok, tok, col, tok, col, col, col, col, vec, vec, col, row, col, cube, col, row, row)
    out_specs = (tok, tok, tok, col, col, col, col, vec, vec, col, row, col, cube, col, row, row)
    return jax.shard_map(
        on_device, mesh=mesh, in_specs=in_specs, out_specs=out_specs, check_vma=False)
```

```python
import functools
import math

import jax
import jax.numpy as jnp
from jax import lax
from jax.experimental import pallas as pl
from jax.experimental.pallas import tpu as pltpu
from jax.sharding import PartitionSpec as P

bf16, f32 = jnp.bfloat16, jnp.float32
RANKS = (64, 64, 32, 128)
CUTS = (0, 64, 128, 160, 288)
LOW_FROM = (1, 4, 3, 5)
T = 128

def dn(x, y, cx, cy):
    return lax.dot_general(x, y, (((cx,), (cy,)), ((), ())), preferred_element_type=f32)

def split2(x):
    hi = x.astype(bf16)
    return hi, (x - hi.astype(f32)).astype(bf16)

def dot(x, y, cx=1, cy=0, passes=3):
    if passes == 1:
        return dn(x.astype(bf16), y.astype(bf16), cx, cy)
    xh, xl = split2(x); yh, yl = split2(y)
    return dn(xh, yh, cx, cy) + dn(xh, yl, cx, cy) + dn(xl, yh, cx, cy)

def ones_dot(left, x):
    hi = x.astype(bf16); r = x - hi.astype(f32)
    mid = r.astype(bf16); lo = (r - mid.astype(f32)).astype(bf16)
    w = x.shape[1]
    o = dn(left, jnp.concatenate([hi, mid, lo], 1), 1, 0)
    return o[:, :w] + o[:, w:2*w] + o[:, 2*w:]

def head_sum(x, J):
    hi, lo = split2(x)
    return dn(jnp.concatenate([hi, lo], 1), jnp.concatenate([J, J], 0), 1, 0)

def sig(z):
    return 1.0 / (1.0 + jnp.exp(-z))

def iota(shape, d):
    return lax.broadcasted_iota(jnp.int32, shape, d)

def consts():
    r, c = iota((T, T), 0), iota((T, T), 1)
    J = jnp.where((r // 64) == (c // 64), 1.0, 0.0).astype(bf16)
    low = jnp.where(r >= c, 1.0, 0.0).astype(bf16)
    up = jnp.where(r <= c, 1.0, 0.0).astype(bf16)
    h0 = c < 64
    return r, c, J, low, up, h0

def halves(x, h0):
    z = jnp.zeros_like(x)
    m = h0 if x.shape[0] == T else jnp.concatenate([h0, h0], 0)
    return jnp.where(m, x, z), jnp.where(m, z, x)

def prep(r_, kx, vx, ow, oa, ov, first, par, K):
    r, c, J, low, up, h0 = K
    dk0, dk1, bonus, db, sq0, sq1 = (par[i:i+1] for i in range(6))
    sg = sig(db + ow)
    ld = sg * (-0.6065306597126334)
    cum = ones_dot(low, ld)
    cm = cum - cum[63:64]
    G = jnp.exp(cm); S = jnp.exp(-cm); B = jnp.exp(cm - ld)
    ag = sig(sq0 + oa); vg = sig(sq1 + ov)
    v2 = vx + (first - vx) * vg
    kfac = 1.0 + (ag - 1.0) * dk1
    km = kx * kfac
    cc = kx * dk0
    n = lax.rsqrt(head_sum(cc * cc, J) + 1e-6)
    kk = cc * n
    return sg, ld, G, S, B, ag, vg, v2, kfac, km, n, kk

def inverse(N0, N1, K, passes):
    r, c = K[0], K[1]
    z = jnp.zeros((T, T), f32)
    eye = jnp.where(r == c, 1.0, 0.0)
    m = ((r // 2) == (c // 2))
    T0 = eye + jnp.where(m, N0, 0.0); T1 = eye + jnp.where(m, N1, 0.0)
    s = 2
    def bd(a, b):
        return jnp.concatenate([jnp.concatenate([a, z], 1), jnp.concatenate([z, b], 1)], 0)
    TT = jnp.concatenate([T0, T1], 1)
    while s < T:
        m = ((r // (2*s)) == (c // (2*s))) & ((r // s) != (c // s))
        o = dot(TT, bd(jnp.where(m, N0, 0.0), jnp.where(m, N1, 0.0)), passes=passes)
        TT = TT + dot(o, bd(TT[:, :T], TT[:, T:]), passes=passes)
        s *= 2
    res = jnp.concatenate([eye, eye], 1) - TT + dot(jnp.concatenate([N0, N1], 1), bd(TT[:, :T], TT[:, T:]))
    return TT + dot(TT, bd(res[:, :T], res[:, T:]), passes=1)

def fwd_core(r_, kx, vx, ow, oa, ov, og, first, par, pA=3, pI=1, pO=3):
    K = consts(); r, c, J, low, up, h0 = K
    sg, ld, G, S, B, ag, vg, v2, kfac, km, n, kk = prep(r_, kx, vx, ow, oa, ov, first, par, K)
    at = -kk * B; rt = r_ * G; bt = kk * ag * S; kt = km * S
    Q = jnp.concatenate([at, rt], 0); Kf = jnp.concatenate([bt, kt], 0)
    Q0, Q1 = halves(Q, h0)
    A0 = dot(Q0, Kf, 1, 1, pA); A1 = dot(Q1, Kf, 1, 1, pA)
    st = r > c; inc = r >= c
    def msk(A):
        return (jnp.where(st, A[:T, :T], 0.0), jnp.where(st, A[:T, T:], 0.0),
                jnp.where(inc, A[T:, :T], 0.0), jnp.where(inc, A[T:, T:], 0.0))
    ab0, ak0, rb0, rk0 = msk(A0); ab1, ak1, rb1, rk1 = msk(A1)
    TT = inverse(ab0, ab1, K, pI)
    v0, v1 = halves(v2, h0)
    Pm = dot(jnp.concatenate([ak0, ak1], 1), jnp.concatenate([v0, v1], 0), passes=pO)
    U = dot(TT, jnp.concatenate(halves(Pm, h0), 0), passes=pO)
    u0, u1 = halves(U, h0)
    Y = dot(jnp.concatenate([rb0, rk0, rb1, rk1], 1), jnp.concatenate([u0, v0, u1, v1], 0), passes=pO)
    mean = head_sum(Y, J) * (1/64)
    cy = Y - mean
    rstd = lax.rsqrt(head_sum(cy * cy, J) * (1/64) + 4.0)
    bonus, gain, bias = par[2:3], par[6:7], par[7:8]
    bs = head_sum(r_ * km * bonus, J)
    out = (cy * rstd * gain + bias + bs * v2) * og
    return out, TT, U, Y

def bwd_core(r_, kx, vx, ow, oa, ov, og, first, par, TT, U, Y, gg, pA=3, pW=3, pD=3):
    K = consts(); r, c, J, low, up, h0 = K
    dk0, dk1, bonus, db, sq0, sq1, gain, bias = (par[i:i+1] for i in range(8))
    sg, ld, G, S, B, ag, vg, v2, kfac, km, n, kk = prep(r_, kx, vx, ow, oa, ov, first, par, K)
    at = -kk * B; rt = r_ * G; bt = kk * ag * S; kt = km * S
    mean = head_sum(Y, J) * (1/64)
    cy = Y - mean
    rstd = lax.rsqrt(head_sum(cy * cy, J) * (1/64) + 4.0)
    gn = cy * rstd
    bs = head_sum(r_ * km * bonus, J)
    g_og = gg * (gn * gain + bias + bs * v2)
    gi = gg * og
    g_gn = gi * gain
    gY = rstd * (g_gn - head_sum(g_gn, J) * (1/64) - gn * (head_sum(g_gn * gn, J) * (1/64)))
    g_bs = head_sum(gi * v2, J)
    Q = jnp.concatenate([at, rt], 0); Kf = jnp.concatenate([bt, kt], 0)
    Q0, Q1 = halves(Q, h0)
    At0 = dot(Kf, Q0, 1, 1, pA); At1 = dot(Kf, Q1, 1, 1, pA)
    st = r < c; inc = r <= c
    akT = jnp.concatenate([jnp.where(st, At0[T:, :T], 0.0), jnp.where(st, At1[T:, :T], 0.0)], 1)
    inc2 = jnp.concatenate([inc, inc], 0)
    rT = jnp.concatenate([jnp.where(inc2, At0[:, T:], 0.0), jnp.where(inc2, At1[:, T:], 0.0)], 1)
    gy0, gy1 = halves(gY, h0)
    dUV = dot(rT, jnp.concatenate([gy0, gy1], 0), passes=pW)
    dU, dV = dUV[:T], dUV[T:]
    R = dot(TT, dU, 0, 0, pW)
    W = jnp.where(h0, R[:T], R[T:])
    w0, w1 = halves(W, h0)
    dV = dV + dot(akT, jnp.concatenate([w0, w1], 0), passes=pW)
    X = jnp.concatenate([U, v2], 0)
    Yg0 = jnp.concatenate([w0, gy0], 0); Yg1 = jnp.concatenate([w1, gy1], 0)
    r2, c2 = iota((2*T, 2*T), 0), iota((2*T, 2*T), 1)
    keep = ((r2 & 127) > (c2 & 127)) | ((r2 >= T) & ((r2 & 127) == (c2 & 127)))
    keepT = ((r2 & 127) < (c2 & 127)) | ((c2 >= T) & ((r2 & 127) == (c2 & 127)))
    dA0 = jnp.where(keep, dot(Yg0, X, 1, 1, pD), 0.0)
    dA1 = jnp.where(keep, dot(Yg1, X, 1, 1, pD), 0.0)
    dT0 = jnp.where(keepT, dot(X, Yg0, 1, 1, pD), 0.0)
    dT1 = jnp.where(keepT, dot(X, Yg1, 1, 1, pD), 0.0)
    K0, K1 = halves(Kf, h0)
    dQ = dot(jnp.concatenate([dA0, dA1], 1), jnp.concatenate([K0, K1], 0), passes=pD)
    dK = dot(jnp.concatenate([dT0, dT1], 1), jnp.concatenate([Q0, Q1], 0), passes=pD)
    da_, dr_ = dQ[:T], dQ[T:]; db_, dk_ = dK[:T], dK[T:]
    e = dr_ * rt - db_ * bt - dk_ * kt
    f = da_ * at
    g_ld = ones_dot(up, e + f) - f
    g_kk = db_ * S * ag - da_ * B
    g_b = db_ * S
    g_km = g_bs * r_ * bonus + dk_ * S
    g_r = g_bs * km * bonus + dr_ * G
    g_ag = g_b * kk + g_km * kx * dk1
    g_c = n * (g_kk - kk * head_sum(g_kk * kk, J))
    g_kx = g_km * kfac + g_c * dk0
    g_v2 = gi * bs + dV
    g_first = g_v2 * vg
    g_vx = g_v2 - g_first
    g_ov = g_first * (1.0 - vg) * (first - vx)
    g_oa = g_ag * ag * (1.0 - ag)
    g_ow = g_ld * ld * (1.0 - sg)
    def cs(x): return jnp.sum(x, 0, keepdims=True)
    pg = jnp.concatenate([cs(g_c * kx), cs(g_km * kx * (ag - 1.0)), cs(g_bs * r_ * km),
                          cs(g_ow), cs(g_oa), cs(g_ov), cs(gi * gn), cs(gi)], 0)
    return g_r, g_kx, g_vx, g_ow, g_oa, g_ov, g_og, g_first, pg


def fwd_kernel(*refs):
    ins, par, outs = refs[:8], refs[8], refs[9:]
    for q in range(2):
        rows = pl.ds(q * T, T)
        vals = [ref[rows, :] for ref in ins]
        res = fwd_core(*vals[:7], vals[7].astype(f32), par[...])
        outs[0][rows, :] = res[0].astype(bf16)
        for ref, val in zip(outs[1:], res[1:]):
            ref[rows, :] = val


def bwd_kernel(*refs):
    ins, par, saved, outs = refs[:8], refs[8], refs[9:13], refs[13:]
    for q in range(2):
        rows = pl.ds(q * T, T)
        vals = [ref[rows, :] for ref in ins]
        res = bwd_core(*vals[:7], vals[7].astype(f32), par[...], *[ref[rows, :] for ref in saved])
        for ref, val in zip(outs[:8], res[:8]):
            ref[rows, :] = val.astype(bf16)
        outs[8][pl.ds(q * 8, 8), :] = res[8]
        for ref, val in zip(outs[9:], res[:3]):
            ref[rows, :] = val.astype(bf16)


MIXER = dict(
    compiler_params=pltpu.CompilerParams(vmem_limit_bytes=32 * 1024 * 1024),
    cost_estimate=pl.CostEstimate(flops=10 * 10**9, bytes_accessed=10**7, transcendentals=10**6))


def mixer_fwd(args, par, part, before):
    rows, width = args[0].shape
    seqs, pairs = rows // T, width // 128
    p0 = part * (pairs // 4)
    tile = pl.BlockSpec((2 * T, 128), lambda s, p: (s, p + p0))
    pspec = pl.BlockSpec((8, 128), lambda s, p: (0, p + p0))
    inv = pl.BlockSpec((2 * T, 2 * T), lambda s, p: (s * pairs + p + p0, 0))
    wide = jax.ShapeDtypeStruct((rows, width), f32)

    def body(*refs):
        fwd_kernel(*refs[:9], *refs[9 + len(before):])

    return pl.pallas_call(
        body,
        grid=(seqs // 2, pairs // 4),
        in_specs=[tile] * 8 + [pspec] + [pl.BlockSpec(memory_space=pl.ANY)] * len(before),
        out_specs=[tile, inv, tile, tile],
        out_shape=[jax.ShapeDtypeStruct((rows, width), bf16),
                   jax.ShapeDtypeStruct((rows * pairs, 2 * T), f32), wide, wide],
        input_output_aliases={9 + i: i for i in range(len(before))},
        name="mixer_fwd",
        **MIXER,
    )(*args, par, *before)


def mixer_bwd(args, par, saved, gg, side, part, before):
    rows, width = args[0].shape
    seqs, pairs = rows // T, width // 128
    keep, p0 = part // 2, part % 2 * (pairs // 4)

    def pair(p, side):
        return 2 * (p + p0) + (side[0] if keep else 1 - side[0])

    tile = pl.BlockSpec((2 * T, 128), lambda s, p, side: (s, pair(p, side)))
    pspec = pl.BlockSpec((8, 128), lambda s, p, side: (0, pair(p, side)))
    inv = pl.BlockSpec((2 * T, 2 * T), lambda s, p, side: (s * pairs + pair(p, side), 0))
    gpar = pl.BlockSpec((16, 128), lambda s, p, side: (s, pair(p, side)))
    rel = pl.BlockSpec((2 * T, 128), lambda s, p, side: (s, p + p0 + keep * (pairs // 2)))
    thin = jax.ShapeDtypeStruct((rows, width), bf16)

    def body(*refs):
        bwd_kernel(*refs[1:14], *refs[14 + len(before):])

    return pl.pallas_call(
        body,
        grid_spec=pltpu.PrefetchScalarGridSpec(
            num_scalar_prefetch=1,
            grid=(seqs // 2, pairs // 4),
            in_specs=[tile] * 8 + [pspec, inv, tile, tile, tile]
            + [pl.BlockSpec(memory_space=pl.ANY)] * len(before),
            out_specs=[tile] * 8 + [gpar] + [rel] * 3),
        out_shape=[thin] * 8 + [jax.ShapeDtypeStruct((seqs * 8, width), f32)] + [thin] * 3,
        input_output_aliases={14 + i: i for i in range(len(before))},
        name="mixer_bwd",
        **MIXER,
    )(side, *args, par, *saved, gg, *before)


def ffn_kernel(xc, xct, gf, wk, wv, hid, gpre, gx, *grads):
    pre = jnp.maximum(mm(xc[...], wk[...]), 0.0)
    h = (pre * pre).astype(bf16)
    hid[...] = h
    g = (mmt(gf[...], wv[...]) * (2.0 * pre)).astype(bf16)
    gpre[...] = g
    if grads:
        d_val, d_key = grads
        d_val[...] = tmm(h, gf[...]).astype(bf16)
        d_key[...] = mm(xct[...], g).astype(bf16)
    g = mmt(g, wk[...])

    @pl.when(pl.program_id(0) == 0)
    def _():
        gx[...] = g

    @pl.when(pl.program_id(0) > 0)
    def _():
        gx[...] += g


FFN_BLOCK = 512


def ffn_params(name, flops=5 * 10**9, moved=10**7):
    return dict(
        compiler_params=pltpu.CompilerParams(vmem_limit_bytes=32 * 1024 * 1024),
        cost_estimate=pl.CostEstimate(flops=flops, bytes_accessed=moved, transcendentals=0),
        name=name)


def ffn_half(xc, xct, gf, wk, wv, with_grads):
    rows, width = xc.shape
    units = wv.shape[0]
    tall = pl.BlockSpec((rows, width), lambda j: (0, 0))
    unit = pl.BlockSpec((rows, FFN_BLOCK), lambda j: (0, j))
    down = pl.BlockSpec((FFN_BLOCK, width), lambda j: (j, 0))
    across = pl.BlockSpec((width, FFN_BLOCK), lambda j: (0, j))
    hidden = jax.ShapeDtypeStruct((rows, units), bf16)
    more = with_grads * 1
    return pl.pallas_call(
        ffn_kernel,
        grid=(units // FFN_BLOCK,),
        in_specs=[tall, pl.BlockSpec((width, rows), lambda j: (0, 0)), tall, across, down],
        out_specs=[unit, unit, tall] + [down, across] * more,
        out_shape=[hidden, hidden, jax.ShapeDtypeStruct((rows, width), f32)]
        + [jax.ShapeDtypeStruct((units, width), bf16), jax.ShapeDtypeStruct((width, units), bf16)] * more,
        **ffn_params("ffn_half"),
    )(xc, xct, gf, wk, wv)


def grad_kernel(xct, gf, hid, gpre, val_got, key_got, d_val, d_key):
    d_val[...] = (tmm(hid[...], gf[...]) + val_got[...].astype(f32)).astype(bf16)
    d_key[...] = (mm(xct[...], gpre[...]) + key_got[...].astype(f32)).astype(bf16)


def ffn_grads(xct, gf, hid, gpre, val_got, key_got):
    width, rows = xct.shape
    units = hid.shape[1]
    unit = pl.BlockSpec((rows, FFN_BLOCK), lambda j: (0, j))
    down = pl.BlockSpec((FFN_BLOCK, width), lambda j: (j, 0))
    across = pl.BlockSpec((width, FFN_BLOCK), lambda j: (0, j))
    return pl.pallas_call(
        grad_kernel,
        grid=(units // FFN_BLOCK,),
        in_specs=[pl.BlockSpec((width, rows), lambda j: (0, 0)),
                  pl.BlockSpec((rows, width), lambda j: (0, 0)), unit, unit, down, across],
        out_specs=[down, across],
        out_shape=[jax.ShapeDtypeStruct((units, width), bf16),
                   jax.ShapeDtypeStruct((width, units + width // 2), bf16)],
        **ffn_params("ffn_grads"),
    )(xct, gf, hid, gpre, val_got, key_got)


def conc_kernel(att, gated, got, before, d_key):
    d_key[...] = (tmm(att[...], gated[...]) + got[...].astype(f32)).astype(bf16)


def conc_grad(att, gated, got, d_key):
    rows, width = att.shape
    cols = gated.shape[1]
    last = d_key.shape[1] // cols - 1
    return pl.pallas_call(
        conc_kernel,
        grid=(1,),
        in_specs=[pl.BlockSpec((rows, width), lambda j: (0, 0)),
                  pl.BlockSpec((rows, cols), lambda j: (0, 0)),
                  pl.BlockSpec((width, cols), lambda j: (0, 0)),
                  pl.BlockSpec(memory_space=pl.ANY)],
        out_specs=pl.BlockSpec((width, cols), lambda j: (0, last)),
        out_shape=jax.ShapeDtypeStruct(d_key.shape, bf16),
        input_output_aliases={3: 0},
        **ffn_params("conc_grad"),
    )(att, gated, got, d_key)


def proj_kernel(*refs, gots, split):
    cols = refs[0].shape[1]
    outs = refs[6 + gots:]
    for i in range(3):
        at = slice(i * cols, (i + 1) * cols)
        val = tmm(refs[i][...], refs[3 + i][...])
        for ref in refs[6:6 + gots]:
            val = val + ref[:, at].astype(f32)
        if not split:
            outs[0][:, at] = val.astype(bf16)
            continue
        for c in range(cols // 64):
            for h in range(2):
                outs[h][c * 32:(c + 1) * 32, at] = val[c * 64 + h * 32:c * 64 + h * 32 + 32].astype(bf16)


def proj_grad(gs, xs, keep, near, gots, split):
    rows, width = xs[0].shape
    half = width // 2
    full = pl.BlockSpec((half, 3 * half), lambda j: (0, 0))
    part = half // 2 if split else half
    n_out = 2 if split else 1
    res = pl.pallas_call(
        functools.partial(proj_kernel, gots=len(gots), split=split),
        grid=(1,),
        in_specs=[pl.BlockSpec((rows, half), lambda j: (0, keep))] * 3
        + [pl.BlockSpec((rows, half), lambda j: (0, 0 if near else 1))] * 3 + [full] * len(gots),
        out_specs=[pl.BlockSpec((part, 3 * half), lambda j: (0, 0))] * n_out,
        out_shape=[jax.ShapeDtypeStruct((part, 3 * half), bf16)] * n_out,
        **ffn_params("proj_grad", 3 * 10**8, 10**6),
    )(*gs, *xs, *gots)
    return res if split else res[0]


def layer_norm(x, gain, bias):
    c = x - jnp.mean(x, -1, keepdims=True)
    return c * lax.rsqrt(jnp.mean(c * c, -1, keepdims=True) + 1e-5) * gain + bias


def prev(z):
    z = z.reshape(-1, T, z.shape[-1])
    z = jnp.concatenate([jnp.zeros_like(z[:, :1]), z[:, :-1]], 1)
    return z.reshape(-1, z.shape[-1])


def front(x, mix, gain, bias):
    h = layer_norm(x, gain, bias)
    d = prev(h) - h
    return tuple(h + d * mix[i] for i in range(mix.shape[0]))


def mm(a, b):
    return dn(a, b, 1, 0)


def mmt(a, b):
    return dn(a, b, 1, 1)


def tmm(a, b):
    return dn(a, b, 0, 0)


def lowrank_act(zw, za, zv, zg):
    return jnp.tanh(zw), za, zv, jax.nn.sigmoid(zg)


def swap(x, bit):
    n = lax.axis_size("dp")
    return lax.ppermute(x, "dp", [(i, i ^ bit) for i in range(n)])


def add(a, b):
    return (a.astype(f32) + b.astype(f32)).astype(bf16)


def pick(x, index, axis):
    return lax.dynamic_index_in_dim(x, index, axis, keepdims=False)


BOTH = (((2, 4), (3, 2)), ((2, 2), (2, 4)), ((1, 8), (1, 8)), ((0, 16), (0, 16)))
ONE = (((2, 4),), ((2, 2),), ((1, 8),), ((0, 16),))
TAIL = (((2, 2), (1, 8)), ((1, 8), (0, 16)), ((0, 16), (0, 2)))


def side_of(bit):
    return (lax.axis_index("dp") // bit) % 2


def sum_send(parts, step):
    return [swap(pick(part, 1 - side_of(bit), axis), bit) for part, (axis, bit) in zip(parts, step)]


def sum_take(parts, got, step):
    return [add(pick(part, side_of(bit), axis), g) for part, g, (axis, bit) in zip(parts, got, step)]


def two(g):
    g = g.reshape(2, 2, 2, 2, g.shape[0] // 16, g.shape[1])
    cut = g.shape[4] // 2
    return [g[..., :cut, :], g[..., cut:, :]]


def whole_sum(g):
    n = lax.axis_size("dp")
    groups = [list(range(c, n, 2)) for c in range(2)]
    g = g.reshape(n // 2, g.shape[0] // (n // 2), g.shape[1])
    return lax.psum_scatter(g, "dp", scatter_dimension=0, axis_index_groups=groups).astype(f32)


def join(a, b, axis, bit):
    mine = (lax.axis_index("dp") // bit) % 2
    return jnp.where(mine == 0, jnp.stack([a, b], axis), jnp.stack([b, a], axis))


def gather_send(parts, step):
    if lax.axis_size("dp") != 32:
        return parts
    return [swap(p, bit) for p, (axis, bit) in zip(parts, BOTH[3 - step])]


def gather_take(parts, got, step):
    if lax.axis_size("dp") != 32:
        return parts
    return [join(p, g, axis, bit) for p, g, (axis, bit) in zip(parts, got, BOTH[3 - step])]


def gather_step(parts, step):
    return gather_take(parts, gather_send(parts, step), step)


def chip_gather_end(parts):
    n = lax.axis_size("dp")
    if n != 32:
        groups = [list(range(c, n, 2)) for c in range(2)]
        return [lax.all_gather(p, "dp", axis=0, axis_index_groups=groups, tiled=True) for p in parts]
    return [p.reshape(-1, p.shape[-1]) for p in parts]


def tie(*values):
    return lax.optimization_barrier(values)


def on_core(keep, send):
    return (keep + swap(send, 1).astype(f32)).astype(bf16)


def trade_rows(h):
    core = lax.axis_index("dp") % 2
    h = h.reshape(2, h.shape[0] // 2, h.shape[1])
    own, got = pick(h, core, 0), swap(pick(h, 1 - core, 0).astype(bf16), 1).astype(f32)
    return jnp.where(core == 0, own, got), jnp.where(core == 0, got, own)


def on_device(x_in, first_in, spans, gout_in, mix, gains, biases, tying, extra, dwindle,
              squash, reducing, enlarging, ingoing, concluding, ffn_key, ffn_value):
    micro, seqs, length, width = x_in.shape
    rows = micro * seqs * length
    shard = mix.shape[1]
    core = lax.axis_index("dp") % 2
    chips = lax.axis_size("dp") // 2
    half = width // 2
    small = jnp.concatenate([mix, gains, biases, tying, extra[None], dwindle[None], squash], 0)
    n_small = small.shape[0]
    fill = jnp.zeros((80, shard), bf16)
    low_a = jnp.concatenate([reducing, jnp.concatenate([small[:16], fill], 0).T], 1)
    low_b = jnp.concatenate(
        [enlarging, small[16:], jnp.zeros((16 - n_small + 16, shard), bf16), fill], 0).T
    turned = jnp.swapaxes(ingoing, 1, 2)
    q_halves = jnp.stack([jnp.concatenate([turned[0][:, c * half:(c + 1) * half],
                                           turned[1][:, c * half:(c + 1) * half]], 1)
                          for c in range(2)])
    r_halves = jnp.stack([jnp.concatenate([turned[2][:, c * half:(c + 1) * half], low], 1)
                          for c, low in enumerate((low_a, low_b))])
    keys = ffn_key.reshape(shard, chips, 2, -1)
    k_halves = jnp.stack([jnp.concatenate([keys[:, :, c].reshape(shard, -1),
                                           concluding.T[:, c * half:(c + 1) * half]], 1)
                          for c in range(2)])

    def trade(halves):
        own, sent = pick(halves, core, 0), pick(halves, 1 - core, 0)
        return join(own, swap(sent, 1), 0, 1).reshape(2 * shard, -1)

    mixer = [trade(q_halves), trade(r_halves)]
    mixer = gather_step(gather_step(mixer, 0), 1)
    ffn = [trade(k_halves), ffn_value]
    mixer, ffn = tie(mixer, ffn)

    def one_send(p, step, which):
        axis, bit = BOTH[3 - step][which]
        return swap(p, bit) if lax.axis_size("dp") == 32 else p

    def one_take(p, got, step, which):
        axis, bit = BOTH[3 - step][which]
        return join(p, got, axis, bit) if lax.axis_size("dp") == 32 else p

    got, k_got = tie(gather_send(mixer, 2), one_send(ffn[0], 0, 0))
    mixer = gather_take(mixer, got, 2)
    f_key, f_val = one_take(ffn[0], k_got, 0, 0), ffn[1]
    got, k_got, v_got = tie(gather_send(mixer, 3), one_send(f_key, 1, 0), one_send(f_val, 0, 1))
    f_key, f_val = one_take(f_key, k_got, 1, 0), one_take(f_val, v_got, 0, 1)
    got, f_key, f_val = tie(got, f_key, f_val)
    v_got, k_got = one_send(f_val, 1, 1), one_send(f_key, 2, 0)
    mixer = chip_gather_end(gather_take(mixer, got, 3))
    far = [swap(p, 1) for p in mixer]

    def in_core_order(a, b, axis):
        return jnp.where(core == 0, jnp.concatenate([a, b], axis), jnp.concatenate([b, a], axis))

    wi = [(mixer[0][:, :half], far[0][:, :half]), (mixer[0][:, half:], far[0][:, half:]),
          (mixer[1][:, :half], far[1][:, :half])]
    low_a = jnp.where(core == 0, mixer[1][:, half:], far[1][:, half:])
    low_b = jnp.where(core == 0, far[1][:, half:], mixer[1][:, half:])
    w_in, w_out = low_a[:, :CUTS[4]], low_b[:, :CUTS[4]]
    small = jnp.concatenate([low_a[:, CUTS[4]:CUTS[4] + 16], low_b[:, CUTS[4]:CUTS[4] + 16]], 1)
    small = small.T.astype(f32)
    mix, gains, biases, tying = small[0:7], small[7:10], small[10:13], small[13:15]

    def by_core(a):
        return in_core_order(a[..., :half], a[..., half:], -1)

    par = jnp.concatenate([small[13:19], gains[1:2], biases[1:2]], 0)

    x = x_in.reshape(rows, width).astype(f32)
    first = first_in.reshape(rows, width)
    place = jnp.arange(length, dtype=jnp.int32)
    valid = (place[None, None, :] < spans[:, :, None]).astype(f32).reshape(rows, 1)
    g_out = valid * gout_in.reshape(rows, width).astype(f32)
    gf = g_out.astype(bf16)

    xs, pull_front = jax.vjp(front, by_core(x), by_core(mix[:6]), by_core(gains[0]), by_core(biases[0]))
    xs = [z.astype(bf16) for z in xs]
    xs, v_got, gf = tie(xs, v_got, gf)
    f_val = one_take(f_val, v_got, 1, 1)
    v_got = one_send(f_val, 2, 1)
    proj = [mmt(xs[j][:, :half], wi[i][0]) + mmt(xs[j][:, half:], wi[i][1])
            for i, j in enumerate((0, 2, 3))]
    w_in = in_core_order(w_in[:half], w_in[half:], 0)
    zs = [mm(xs[j], w_in[:, CUTS[i]:CUTS[i + 1]]) for i, j in enumerate(LOW_FROM)]
    ls, pull_low = jax.vjp(lowrank_act, *zs)
    ls = [z.astype(bf16) for z in ls]
    os_ = [mmt(ls[i], w_out[:, CUTS[i]:CUTS[i + 1]]) for i in range(4)]
    args = (*proj, *os_, first)
    done = mixer_fwd(args, par, 0, ())
    done, k_got, v_got = tie(done, k_got, v_got)
    ffn = [one_take(f_key, k_got, 2, 0), one_take(f_val, v_got, 2, 1)]
    ffn_got = gather_send(ffn, 3)
    for part in (1, 2, 3):
        done = mixer_fwd(args, par, part, done)
    done, ffn_got = tie(done, ffn_got)
    ffn = chip_gather_end(gather_take(ffn, ffn_got, 3))
    gated, *saved = done
    wk, wv = ffn
    wo = wk[:, -half:]
    wo_far, wk, wv = tie(swap(wo, 1), wk, wv)
    wk_far, wv_far = swap(wk, 1), swap(wv, 1)

    def side(a, c):
        return lax.dynamic_slice_in_dim(a, c * half, half, 1)

    gated_near, gated_far = side(gated, core), side(gated, 1 - core)
    mixed = x + mmt(gated_near, wo) + mmt(gated_far, wo_far)
    (xc,), pull_chan = jax.vjp(front, mixed, mix[6:7], gains[2], biases[2])
    xc = xc.astype(bf16)
    xct = xc.T
    hidden, g_pre, g_xc = ffn_half(xc, xct, gf, wk, wv, False)
    g_pre, wk_far, wv_far = tie(g_pre, wk_far, wv_far)
    hidden_far, _, g_xc_far, val_far, key_far = ffn_half(xc, xct, gf, wk_far, wv_far, True)

    scale = 1.0 / math.sqrt(rows * lax.axis_size("dp"))

    small_slice = lax.axis_size("dp") == 32
    side_y = lax.axis_index("dp") // 4 % 2 if small_slice else jnp.int32(0)
    side_y = side_y.reshape(1)
    steps = BOTH if small_slice else ((), (), (), ())

    def start(g):
        return two(g) if small_slice else whole_sum(g)

    def send(parts, step):
        return sum_send(parts, steps[step]) if small_slice else []

    def take(parts, got, step):
        return sum_take(parts, got, steps[step]) if small_slice else parts

    def finish(parts):
        return jnp.concatenate(parts, 0).astype(f32) if small_slice else parts

    val_got, key_got = swap(val_far, 1), swap(key_far, 1)
    g_mixed, g_mix_c, g_gain_c, g_bias_c = pull_chan((g_xc + g_xc_far,))
    g_mixed = g_out + g_mixed
    early = jnp.concatenate(
        [g_mix_c, g_gain_c[None], g_bias_c[None], jnp.zeros((5, width), f32)], 0)
    g_att = g_mixed.astype(bf16)
    conc_got = swap(tmm(g_att, gated_far).astype(bf16), 1)
    gg = in_core_order(mm(g_att, wo), mm(g_att, wo_far), 1)
    gg, val_got, key_got, conc_got = tie(gg, val_got, key_got, conc_got)
    d_value, d_key = ffn_grads(xct, gf, hidden, g_pre, val_got, key_got)
    d_key = conc_grad(g_att, gated_near, conc_got, d_key)
    d_value, d_key = start(d_value), start(d_key)
    v_got, k_got = send(d_value, 0), send(d_key, 0)
    gg, d_value, d_key = tie(gg, d_value, d_key)
    grads = mixer_bwd(args, par, saved, gg, side_y, 0, ())
    grads, v_got = tie(grads, v_got)
    d_value = take(d_value, v_got, 0)
    v_got = send(d_value, 1)
    grads = mixer_bwd(args, par, saved, gg, side_y, 1, grads)

    x_proj = [xs[0], xs[2], xs[3]]

    def proj_part(near):
        cols = slice(0, half) if near else slice(half, width)
        return jnp.concatenate([tmm(grads[9 + i][:, :half], x_proj[i][:, cols]) for i in range(3)], 1)

    away = on_core(proj_part(True), proj_part(False).astype(bf16))
    grads = mixer_bwd(args, par, saved, gg, side_y, 2, grads)
    grads, v_got, k_got, away = tie(grads, v_got, k_got, away)
    d_value, d_key = take(d_value, v_got, 1), take(d_key, k_got, 0)
    v_got, k_got = send(d_value, 2), send(d_key, 1)
    if small_slice:
        away = swap(away, 4)
    grads = mixer_bwd(args, par, saved, gg, side_y, 3, grads)
    grads, v_got, k_got = tie(grads, v_got, k_got)
    d_value, d_key = take(d_value, v_got, 2), take(d_key, k_got, 1)
    v_got, k_got = send(d_value, 3), send(d_key, 2)
    home = swap(proj_grad(grads[9:12], x_proj, 1, False, [], False), 1)
    gp = jnp.sum(grads[8].reshape(-1, 8, width), 0)
    g_proj, g_os, g_first = grads[:3], grads[3:7], grads[7]
    g_ls = tuple(mm(g_os[i], w_out[:, CUTS[i]:CUTS[i + 1]]) for i in range(4))
    g_zs = [z.astype(bf16) for z in pull_low(g_ls)]
    back = [mmt(g_zs[i], w_in[:, CUTS[i]:CUTS[i + 1]]) for i in range(4)]

    def down(i):
        return jnp.concatenate([mm(g_proj[i], wi[i][0]), mm(g_proj[i], wi[i][1])], 1)

    g_xs = (down(0), back[0], down(1), down(2) + back[2], back[1], back[3])
    low_a = jnp.concatenate([tmm(xs[j], g_zs[i]) for i, j in enumerate(LOW_FROM)], 1)
    low_a = in_core_order(low_a[:half], low_a[half:], 0)
    low_b = jnp.concatenate([tmm(g_os[i], ls[i]) for i in range(4)], 1)
    d_low = on_core(jnp.where(core == 0, low_a, low_b),
                    jnp.where(core == 0, low_b, low_a).astype(bf16))
    if small_slice:
        d_low = [d_low.reshape(2, 2, 2, 2, 64, -1)]
        l_got = sum_send(d_low, ONE[0])
    if small_slice:
        g_xs, away, home = tie(g_xs, away, home)
        d_proj = proj_grad(grads[9:12], x_proj, 1, True, [home, away], True)
        d_proj = [p.reshape(2, 2, 2, 32, -1) for p in d_proj]
        p_send = [pick(p, 1 - side_of(bit), axis) for p, (axis, bit) in zip(d_proj, TAIL[0])]
        p_send, v_got, k_got, l_got = tie(p_send, v_got, k_got, l_got)
        p_got = [swap(p, bit) for p, (axis, bit) in zip(p_send, TAIL[0])]
        d_key, d_low = take(d_key, k_got, 2), sum_take(d_low, l_got, ONE[0])
        l_got, k_got = sum_send(d_low, ONE[1]), send(d_key, 3)
    g_x, g_mix_t, g_gain_t, g_bias_t = pull_front(g_xs)
    g_x = g_mixed + by_core(g_x)
    g_mix_t, g_gain_t, g_bias_t = by_core(g_mix_t), by_core(g_gain_t), by_core(g_bias_t)
    d_small = jnp.concatenate(
        [gp, jnp.concatenate([g_mix_t, g_gain_t[None], g_bias_t[None]], 0), early], 0)
    if small_slice:
        d_small, p_got, l_got, hidden, hidden_far = tie(d_small, p_got, l_got, hidden, hidden_far)
        d_proj, d_low = sum_take(d_proj, p_got, TAIL[0]), sum_take(d_low, l_got, ONE[1])
        p_got, l_got = sum_send(d_proj, TAIL[1]), sum_send(d_low, ONE[2])
        for bit in (1, 2, 4, 8, 16):
            d_small = d_small + swap(d_small, bit)
        out = mixed + mm(hidden, wv)
        out, p_got, l_got, k_got, v_got = tie(out, p_got, l_got, k_got, v_got)
        d_proj, d_low = sum_take(d_proj, p_got, TAIL[1]), sum_take(d_low, l_got, ONE[2])
        p_send = [pick(p, 1 - side_of(bit), axis) for p, (axis, bit) in zip(d_proj, TAIL[2])]
        p_send, v_got, k_got = tie(p_send, v_got, k_got)
        p_got = [swap(p, bit) for p, (axis, bit) in zip(p_send, TAIL[2])]
        l_got = sum_send(d_low, ONE[3])
        out = valid * (out + mm(hidden_far, wv_far))
        d_proj = finish(sum_take(d_proj, p_got, TAIL[2]))
        d_low = finish(sum_take(d_low, l_got, ONE[3]))
    else:
        home = proj_grad(grads[9:12], x_proj, 1, True, [home], False).reshape(width // 256, 1, 128, -1)
        d_proj = whole_sum(jnp.concatenate([home, away.reshape(home.shape)], 1).reshape(width, -1))
        d_low = whole_sum(d_low)
        d_small = lax.psum(d_small, "dp")
        out = valid * (mixed + mm(hidden, wv) + mm(hidden_far, wv_far))
    d_key = finish(take(d_key, k_got, 3))
    d_value = finish(take(d_value, v_got, 3))
    d_small = scale * lax.dynamic_slice_in_dim(d_small, lax.axis_index("dp") * shard, shard, 1)
    half_a, half_b = trade_rows(d_proj * scale)
    low_a, low_b = trade_rows(d_low * scale)
    key_a, key_b = trade_rows(d_key * scale)
    hw = half
    wide = [jnp.concatenate([half_a[:, i * hw:(i + 1) * hw], half_b[:, i * hw:(i + 1) * hw]], 1)
            for i in range(3)]
    d_in = jnp.stack([w.T for w in wide])
    d_conc = jnp.concatenate([key_a[:, -hw:], key_b[:, -hw:]], 1).T
    key_a, key_b = key_a[:, :-hw], key_b[:, :-hw]
    d_key = jnp.stack([key_a.reshape(shard, chips, -1), key_b.reshape(shard, chips, -1)], 2)
    d_key = d_key.reshape(shard, -1)
    return (
        out.astype(bf16).reshape(x_in.shape), g_x.astype(bf16).reshape(x_in.shape),
        g_first.reshape(x_in.shape),
        jnp.concatenate([d_small[8:14], d_small[16:17]], 0),
        jnp.concatenate([d_small[14:15], d_small[6:7], d_small[17:18]], 0),
        jnp.concatenate([d_small[15:16], d_small[7:8], d_small[18:19]], 0),
        d_small[0:2], d_small[2], d_small[3], d_small[4:6],
        low_a, low_b.T, d_in, d_conc, d_key, d_value * scale)


def solution(mesh):
    tok, row, col = P(None, "dp", None, None), P("dp", None), P(None, "dp")
    vec, cube = P("dp"), P(None, None, "dp")
    in_specs = (tok, tok, col, tok, col, col, col, col, vec, vec, col, row, col, cube, col, row, row)
    out_specs = (tok, tok, tok, col, col, col, col, vec, vec, col, row, col, cube, col, row, row)
    return jax.shard_map(
        on_device, mesh=mesh, in_specs=in_specs, out_specs=out_specs, check_vma=False)
```

```python
import functools
import math

import jax
import jax.numpy as jnp
from jax import lax
from jax.experimental import pallas as pl
from jax.experimental.pallas import tpu as pltpu
from jax.sharding import PartitionSpec as P

bf16, f32 = jnp.bfloat16, jnp.float32
RANKS = (64, 64, 32, 128)
CUTS = (0, 64, 128, 160, 288)
LOW_FROM = (1, 4, 3, 5)
T = 128

def dn(x, y, cx, cy):
    return lax.dot_general(x, y, (((cx,), (cy,)), ((), ())), preferred_element_type=f32)

def split2(x):
    hi = x.astype(bf16)
    return hi, (x - hi.astype(f32)).astype(bf16)

def dot(x, y, cx=1, cy=0, passes=3):
    if passes == 1:
        return dn(x.astype(bf16), y.astype(bf16), cx, cy)
    xh, xl = split2(x); yh, yl = split2(y)
    return dn(xh, yh, cx, cy) + dn(xh, yl, cx, cy) + dn(xl, yh, cx, cy)

def ones_dot(left, x):
    hi = x.astype(bf16); r = x - hi.astype(f32)
    mid = r.astype(bf16); lo = (r - mid.astype(f32)).astype(bf16)
    w = x.shape[1]
    o = dn(left, jnp.concatenate([hi, mid, lo], 1), 1, 0)
    return o[:, :w] + o[:, w:2*w] + o[:, 2*w:]

def head_sum(x, J):
    hi, lo = split2(x)
    return dn(jnp.concatenate([hi, lo], 1), jnp.concatenate([J, J], 0), 1, 0)

def sig(z):
    return 1.0 / (1.0 + jnp.exp(-z))

def iota(shape, d):
    return lax.broadcasted_iota(jnp.int32, shape, d)

def consts():
    r, c = iota((T, T), 0), iota((T, T), 1)
    J = jnp.where((r // 64) == (c // 64), 1.0, 0.0).astype(bf16)
    low = jnp.where(r >= c, 1.0, 0.0).astype(bf16)
    up = jnp.where(r <= c, 1.0, 0.0).astype(bf16)
    h0 = c < 64
    return r, c, J, low, up, h0

def halves(x, h0):
    z = jnp.zeros_like(x)
    m = h0 if x.shape[0] == T else jnp.concatenate([h0, h0], 0)
    return jnp.where(m, x, z), jnp.where(m, z, x)

def prep(r_, kx, vx, ow, oa, ov, first, par, K):
    r, c, J, low, up, h0 = K
    dk0, dk1, bonus, db, sq0, sq1 = (par[i:i+1] for i in range(6))
    sg = sig(db + ow)
    ld = sg * (-0.6065306597126334)
    cum = ones_dot(low, ld)
    cm = cum - cum[63:64]
    G = jnp.exp(cm); S = jnp.exp(-cm); B = jnp.exp(cm - ld)
    ag = sig(sq0 + oa); vg = sig(sq1 + ov)
    v2 = vx + (first - vx) * vg
    kfac = 1.0 + (ag - 1.0) * dk1
    km = kx * kfac
    cc = kx * dk0
    n = lax.rsqrt(head_sum(cc * cc, J) + 1e-6)
    kk = cc * n
    return sg, ld, G, S, B, ag, vg, v2, kfac, km, n, kk

def inverse(N0, N1, K, passes):
    r, c = K[0], K[1]
    z = jnp.zeros((T, T), f32)
    eye = jnp.where(r == c, 1.0, 0.0)
    m = ((r // 2) == (c // 2))
    T0 = eye + jnp.where(m, N0, 0.0); T1 = eye + jnp.where(m, N1, 0.0)
    s = 2
    def bd(a, b):
        return jnp.concatenate([jnp.concatenate([a, z], 1), jnp.concatenate([z, b], 1)], 0)
    TT = jnp.concatenate([T0, T1], 1)
    while s < T:
        m = ((r // (2*s)) == (c // (2*s))) & ((r // s) != (c // s))
        yield
        o = dot(TT, bd(jnp.where(m, N0, 0.0), jnp.where(m, N1, 0.0)), passes=passes)
        yield
        TT = TT + dot(o, bd(TT[:, :T], TT[:, T:]), passes=passes)
        s *= 2
    yield
    res = jnp.concatenate([eye, eye], 1) - TT + dot(jnp.concatenate([N0, N1], 1), bd(TT[:, :T], TT[:, T:]))
    yield
    return TT + dot(TT, bd(res[:, :T], res[:, T:]), passes=1)

def fwd_core(r_, kx, vx, ow, oa, ov, og, first, par, pA=3, pI=1, pO=3):
    K = consts(); r, c, J, low, up, h0 = K
    sg, ld, G, S, B, ag, vg, v2, kfac, km, n, kk = prep(r_, kx, vx, ow, oa, ov, first, par, K)
    at = -kk * B; rt = r_ * G; bt = kk * ag * S; kt = km * S
    Q = jnp.concatenate([at, rt], 0); Kf = jnp.concatenate([bt, kt], 0)
    Q0, Q1 = halves(Q, h0)
    yield
    A0 = dot(Q0, Kf, 1, 1, pA); A1 = dot(Q1, Kf, 1, 1, pA)
    yield
    st = r > c; inc = r >= c
    def msk(A):
        return (jnp.where(st, A[:T, :T], 0.0), jnp.where(st, A[:T, T:], 0.0),
                jnp.where(inc, A[T:, :T], 0.0), jnp.where(inc, A[T:, T:], 0.0))
    ab0, ak0, rb0, rk0 = msk(A0); ab1, ak1, rb1, rk1 = msk(A1)
    TT = yield from inverse(ab0, ab1, K, pI)
    yield
    v0, v1 = halves(v2, h0)
    Pm = dot(jnp.concatenate([ak0, ak1], 1), jnp.concatenate([v0, v1], 0), passes=pO)
    yield
    U = dot(TT, jnp.concatenate(halves(Pm, h0), 0), passes=pO)
    yield
    u0, u1 = halves(U, h0)
    Y = dot(jnp.concatenate([rb0, rk0, rb1, rk1], 1), jnp.concatenate([u0, v0, u1, v1], 0), passes=pO)
    yield
    mean = head_sum(Y, J) * (1/64)
    yield
    cy = Y - mean
    rstd = lax.rsqrt(head_sum(cy * cy, J) * (1/64) + 4.0)
    yield
    bonus, gain, bias = par[2:3], par[6:7], par[7:8]
    bs = head_sum(r_ * km * bonus, J)
    out = (cy * rstd * gain + bias + bs * v2) * og
    return out, TT, U, Y

def bwd_core(r_, kx, vx, ow, oa, ov, og, first, par, TT, U, Y, gg, pA=3, pW=3, pD=3):
    K = consts(); r, c, J, low, up, h0 = K
    dk0, dk1, bonus, db, sq0, sq1, gain, bias = (par[i:i+1] for i in range(8))
    sg, ld, G, S, B, ag, vg, v2, kfac, km, n, kk = prep(r_, kx, vx, ow, oa, ov, first, par, K)
    at = -kk * B; rt = r_ * G; bt = kk * ag * S; kt = km * S
    yield
    mean = head_sum(Y, J) * (1/64)
    yield
    cy = Y - mean
    rstd = lax.rsqrt(head_sum(cy * cy, J) * (1/64) + 4.0)
    yield
    gn = cy * rstd
    bs = head_sum(r_ * km * bonus, J)
    g_og = gg * (gn * gain + bias + bs * v2)
    gi = gg * og
    g_gn = gi * gain
    gY = rstd * (g_gn - head_sum(g_gn, J) * (1/64) - gn * (head_sum(g_gn * gn, J) * (1/64)))
    yield
    g_bs = head_sum(gi * v2, J)
    yield
    Q = jnp.concatenate([at, rt], 0); Kf = jnp.concatenate([bt, kt], 0)
    Q0, Q1 = halves(Q, h0)
    At0 = dot(Kf, Q0, 1, 1, pA)
    yield
    At1 = dot(Kf, Q1, 1, 1, pA)
    yield
    st = r < c; inc = r <= c
    akT = jnp.concatenate([jnp.where(st, At0[T:, :T], 0.0), jnp.where(st, At1[T:, :T], 0.0)], 1)
    inc2 = jnp.concatenate([inc, inc], 0)
    rT = jnp.concatenate([jnp.where(inc2, At0[:, T:], 0.0), jnp.where(inc2, At1[:, T:], 0.0)], 1)
    yield
    gy0, gy1 = halves(gY, h0)
    dUV = dot(rT, jnp.concatenate([gy0, gy1], 0), passes=pW)
    yield
    dU, dV = dUV[:T], dUV[T:]
    R = dot(TT, dU, 0, 0, pW)
    yield
    W = jnp.where(h0, R[:T], R[T:])
    w0, w1 = halves(W, h0)
    dV = dV + dot(akT, jnp.concatenate([w0, w1], 0), passes=pW)
    yield
    X = jnp.concatenate([U, v2], 0)
    Yg0 = jnp.concatenate([w0, gy0], 0); Yg1 = jnp.concatenate([w1, gy1], 0)
    r2, c2 = iota((2*T, 2*T), 0), iota((2*T, 2*T), 1)
    keep = ((r2 & 127) > (c2 & 127)) | ((r2 >= T) & ((r2 & 127) == (c2 & 127)))
    keepT = ((r2 & 127) < (c2 & 127)) | ((c2 >= T) & ((r2 & 127) == (c2 & 127)))
    yield
    dA0 = jnp.where(keep, dot(Yg0, X, 1, 1, pD), 0.0)
    yield
    dA1 = jnp.where(keep, dot(Yg1, X, 1, 1, pD), 0.0)
    yield
    dT0 = jnp.where(keepT, dot(X, Yg0, 1, 1, pD), 0.0)
    yield
    dT1 = jnp.where(keepT, dot(X, Yg1, 1, 1, pD), 0.0)
    yield
    K0, K1 = halves(Kf, h0)
    dQ = dot(jnp.concatenate([dA0, dA1], 1), jnp.concatenate([K0, K1], 0), passes=pD)
    yield
    dK = dot(jnp.concatenate([dT0, dT1], 1), jnp.concatenate([Q0, Q1], 0), passes=pD)
    yield
    da_, dr_ = dQ[:T], dQ[T:]; db_, dk_ = dK[:T], dK[T:]
    e = dr_ * rt - db_ * bt - dk_ * kt
    f = da_ * at
    yield
    g_ld = ones_dot(up, e + f) - f
    g_kk = db_ * S * ag - da_ * B
    g_b = db_ * S
    g_km = g_bs * r_ * bonus + dk_ * S
    g_r = g_bs * km * bonus + dr_ * G
    g_ag = g_b * kk + g_km * kx * dk1
    yield
    g_c = n * (g_kk - kk * head_sum(g_kk * kk, J))
    g_kx = g_km * kfac + g_c * dk0
    g_v2 = gi * bs + dV
    g_first = g_v2 * vg
    g_vx = g_v2 - g_first
    g_ov = g_first * (1.0 - vg) * (first - vx)
    g_oa = g_ag * ag * (1.0 - ag)
    g_ow = g_ld * ld * (1.0 - sg)
    yield
    def cs(x): return jnp.sum(x, 0, keepdims=True)
    pg = jnp.concatenate([cs(g_c * kx), cs(g_km * kx * (ag - 1.0)), cs(g_bs * r_ * km),
                          cs(g_ow), cs(g_oa), cs(g_ov), cs(gi * gn), cs(gi)], 0)
    return g_r, g_kx, g_vx, g_ow, g_oa, g_ov, g_og, g_first, pg


def in_step(parts):
    results, live = [None] * len(parts), list(range(len(parts)))
    while live:
        for i in list(live):
            try:
                next(parts[i])
            except StopIteration as end:
                results[i] = end.value
                live.remove(i)
    return results


def two_seqs(ins, par, saved, core):
    work = []
    for q in range(2):
        rows = pl.ds(q * T, T)
        vals = [ref[rows, :] for ref in ins]
        work.append(core(*vals[:7], vals[7].astype(f32), par[...], *[ref[rows, :] for ref in saved]))
    return in_step(work)


def fwd_kernel(*refs):
    outs = refs[9:]
    for q, res in enumerate(two_seqs(refs[:8], refs[8], [], fwd_core)):
        rows = pl.ds(q * T, T)
        outs[0][rows, :] = res[0].astype(bf16)
        for ref, val in zip(outs[1:], res[1:]):
            ref[rows, :] = val


def bwd_kernel(*refs):
    outs = refs[13:]
    for q, res in enumerate(two_seqs(refs[:8], refs[8], refs[9:13], bwd_core)):
        rows = pl.ds(q * T, T)
        for ref, val in zip(outs[:8], res[:8]):
            ref[rows, :] = val.astype(bf16)
        outs[8][pl.ds(q * 8, 8), :] = res[8]
        for ref, val in zip(outs[9:], res[:3]):
            ref[rows, :] = val.astype(bf16)


MIXER = dict(
    compiler_params=pltpu.CompilerParams(vmem_limit_bytes=32 * 1024 * 1024),
    cost_estimate=pl.CostEstimate(flops=10 * 10**9, bytes_accessed=10**7, transcendentals=10**6))


def mixer_fwd(args, par, part, before):
    rows, width = args[0].shape
    seqs, pairs = rows // T, width // 128
    p0 = part * (pairs // 4)
    tile = pl.BlockSpec((2 * T, 128), lambda s, p: (s, p + p0))
    pspec = pl.BlockSpec((8, 128), lambda s, p: (0, p + p0))
    inv = pl.BlockSpec((2 * T, 2 * T), lambda s, p: (s * pairs + p + p0, 0))
    wide = jax.ShapeDtypeStruct((rows, width), f32)

    def body(*refs):
        fwd_kernel(*refs[:9], *refs[9 + len(before):])

    return pl.pallas_call(
        body,
        grid=(seqs // 2, pairs // 4),
        in_specs=[tile] * 8 + [pspec] + [pl.BlockSpec(memory_space=pl.ANY)] * len(before),
        out_specs=[tile, inv, tile, tile],
        out_shape=[jax.ShapeDtypeStruct((rows, width), bf16),
                   jax.ShapeDtypeStruct((rows * pairs, 2 * T), f32), wide, wide],
        input_output_aliases={9 + i: i for i in range(len(before))},
        name="mixer_fwd",
        **MIXER,
    )(*args, par, *before)


def mixer_bwd(args, par, saved, gg, side, part, before):
    rows, width = args[0].shape
    seqs, pairs = rows // T, width // 128
    keep, p0 = part // 2, part % 2 * (pairs // 4)

    def pair(p, side):
        return 2 * (p + p0) + (side[0] if keep else 1 - side[0])

    tile = pl.BlockSpec((2 * T, 128), lambda s, p, side: (s, pair(p, side)))
    pspec = pl.BlockSpec((8, 128), lambda s, p, side: (0, pair(p, side)))
    inv = pl.BlockSpec((2 * T, 2 * T), lambda s, p, side: (s * pairs + pair(p, side), 0))
    gpar = pl.BlockSpec((16, 128), lambda s, p, side: (s, pair(p, side)))
    rel = pl.BlockSpec((2 * T, 128), lambda s, p, side: (s, p + p0 + keep * (pairs // 2)))
    thin = jax.ShapeDtypeStruct((rows, width), bf16)

    def body(*refs):
        bwd_kernel(*refs[1:14], *refs[14 + len(before):])

    return pl.pallas_call(
        body,
        grid_spec=pltpu.PrefetchScalarGridSpec(
            num_scalar_prefetch=1,
            grid=(seqs // 2, pairs // 4),
            in_specs=[tile] * 8 + [pspec, inv, tile, tile, tile]
            + [pl.BlockSpec(memory_space=pl.ANY)] * len(before),
            out_specs=[tile] * 8 + [gpar] + [rel] * 3),
        out_shape=[thin] * 8 + [jax.ShapeDtypeStruct((seqs * 8, width), f32)] + [thin] * 3,
        input_output_aliases={14 + i: i for i in range(len(before))},
        name="mixer_bwd",
        **MIXER,
    )(side, *args, par, *saved, gg, *before)


def ffn_kernel(xc, xct, gf, wk, wv, hid, gpre, gx, *grads):
    pre = jnp.maximum(mm(xc[...], wk[...]), 0.0)
    h = (pre * pre).astype(bf16)
    hid[...] = h
    g = (mmt(gf[...], wv[...]) * (2.0 * pre)).astype(bf16)
    gpre[...] = g
    if grads:
        d_val, d_key = grads
        d_val[...] = tmm(h, gf[...]).astype(bf16)
        d_key[...] = mm(xct[...], g).astype(bf16)
    g = mmt(g, wk[...])

    @pl.when(pl.program_id(0) == 0)
    def _():
        gx[...] = g

    @pl.when(pl.program_id(0) > 0)
    def _():
        gx[...] += g


FFN_BLOCK = 512


def ffn_params(name, flops=5 * 10**9, moved=10**7):
    return dict(
        compiler_params=pltpu.CompilerParams(vmem_limit_bytes=32 * 1024 * 1024),
        cost_estimate=pl.CostEstimate(flops=flops, bytes_accessed=moved, transcendentals=0),
        name=name)


def ffn_half(xc, xct, gf, wk, wv, with_grads):
    rows, width = xc.shape
    units = wv.shape[0]
    tall = pl.BlockSpec((rows, width), lambda j: (0, 0))
    unit = pl.BlockSpec((rows, FFN_BLOCK), lambda j: (0, j))
    down = pl.BlockSpec((FFN_BLOCK, width), lambda j: (j, 0))
    across = pl.BlockSpec((width, FFN_BLOCK), lambda j: (0, j))
    hidden = jax.ShapeDtypeStruct((rows, units), bf16)
    more = with_grads * 1
    return pl.pallas_call(
        ffn_kernel,
        grid=(units // FFN_BLOCK,),
        in_specs=[tall, pl.BlockSpec((width, rows), lambda j: (0, 0)), tall, across, down],
        out_specs=[unit, unit, tall] + [down, across] * more,
        out_shape=[hidden, hidden, jax.ShapeDtypeStruct((rows, width), f32)]
        + [jax.ShapeDtypeStruct((units, width), bf16), jax.ShapeDtypeStruct((width, units), bf16)] * more,
        **ffn_params("ffn_half"),
    )(xc, xct, gf, wk, wv)


def grad_kernel(xct, gf, hid, gpre, val_got, key_got, d_val, d_key):
    d_val[...] = (tmm(hid[...], gf[...]) + val_got[...].astype(f32)).astype(bf16)
    d_key[...] = (mm(xct[...], gpre[...]) + key_got[...].astype(f32)).astype(bf16)


def ffn_grads(xct, gf, hid, gpre, val_got, key_got):
    width, rows = xct.shape
    units = hid.shape[1]
    unit = pl.BlockSpec((rows, FFN_BLOCK), lambda j: (0, j))
    down = pl.BlockSpec((FFN_BLOCK, width), lambda j: (j, 0))
    across = pl.BlockSpec((width, FFN_BLOCK), lambda j: (0, j))
    return pl.pallas_call(
        grad_kernel,
        grid=(units // FFN_BLOCK,),
        in_specs=[pl.BlockSpec((width, rows), lambda j: (0, 0)),
                  pl.BlockSpec((rows, width), lambda j: (0, 0)), unit, unit, down, across],
        out_specs=[down, across],
        out_shape=[jax.ShapeDtypeStruct((units, width), bf16),
                   jax.ShapeDtypeStruct((width, units + width // 2), bf16)],
        **ffn_params("ffn_grads"),
    )(xct, gf, hid, gpre, val_got, key_got)


def conc_kernel(att, gated, got, before, d_key):
    d_key[...] = (tmm(att[...], gated[...]) + got[...].astype(f32)).astype(bf16)


def conc_grad(att, gated, got, d_key):
    rows, width = att.shape
    cols = gated.shape[1]
    last = d_key.shape[1] // cols - 1
    return pl.pallas_call(
        conc_kernel,
        grid=(1,),
        in_specs=[pl.BlockSpec((rows, width), lambda j: (0, 0)),
                  pl.BlockSpec((rows, cols), lambda j: (0, 0)),
                  pl.BlockSpec((width, cols), lambda j: (0, 0)),
                  pl.BlockSpec(memory_space=pl.ANY)],
        out_specs=pl.BlockSpec((width, cols), lambda j: (0, last)),
        out_shape=jax.ShapeDtypeStruct(d_key.shape, bf16),
        input_output_aliases={3: 0},
        **ffn_params("conc_grad"),
    )(att, gated, got, d_key)


def proj_kernel(*refs, gots, split):
    cols = refs[0].shape[1]
    outs = refs[6 + gots:]
    for i in range(3):
        at = slice(i * cols, (i + 1) * cols)
        val = tmm(refs[i][...], refs[3 + i][...])
        for ref in refs[6:6 + gots]:
            val = val + ref[:, at].astype(f32)
        if not split:
            outs[0][:, at] = val.astype(bf16)
            continue
        for c in range(cols // 64):
            for h in range(2):
                outs[h][c * 32:(c + 1) * 32, at] = val[c * 64 + h * 32:c * 64 + h * 32 + 32].astype(bf16)


def proj_grad(gs, xs, keep, near, gots, split):
    rows, width = xs[0].shape
    half = width // 2
    full = pl.BlockSpec((half, 3 * half), lambda j: (0, 0))
    part = half // 2 if split else half
    n_out = 2 if split else 1
    res = pl.pallas_call(
        functools.partial(proj_kernel, gots=len(gots), split=split),
        grid=(1,),
        in_specs=[pl.BlockSpec((rows, half), lambda j: (0, keep))] * 3
        + [pl.BlockSpec((rows, half), lambda j: (0, 0 if near else 1))] * 3 + [full] * len(gots),
        out_specs=[pl.BlockSpec((part, 3 * half), lambda j: (0, 0))] * n_out,
        out_shape=[jax.ShapeDtypeStruct((part, 3 * half), bf16)] * n_out,
        **ffn_params("proj_grad", 3 * 10**8, 10**6),
    )(*gs, *xs, *gots)
    return res if split else res[0]


def layer_norm(x, gain, bias):
    c = x - jnp.mean(x, -1, keepdims=True)
    return c * lax.rsqrt(jnp.mean(c * c, -1, keepdims=True) + 1e-5) * gain + bias


def prev(z):
    z = z.reshape(-1, T, z.shape[-1])
    z = jnp.concatenate([jnp.zeros_like(z[:, :1]), z[:, :-1]], 1)
    return z.reshape(-1, z.shape[-1])


def front(x, mix, gain, bias):
    h = layer_norm(x, gain, bias)
    d = prev(h) - h
    return tuple(h + d * mix[i] for i in range(mix.shape[0]))


def mm(a, b):
    return dn(a, b, 1, 0)


def mmt(a, b):
    return dn(a, b, 1, 1)


def tmm(a, b):
    return dn(a, b, 0, 0)


def lowrank_act(zw, za, zv, zg):
    return jnp.tanh(zw), za, zv, jax.nn.sigmoid(zg)


def swap(x, bit):
    n = lax.axis_size("dp")
    return lax.ppermute(x, "dp", [(i, i ^ bit) for i in range(n)])


def add(a, b):
    return (a.astype(f32) + b.astype(f32)).astype(bf16)


def pick(x, index, axis):
    return lax.dynamic_index_in_dim(x, index, axis, keepdims=False)


BOTH = (((2, 4), (3, 2)), ((2, 2), (2, 4)), ((1, 8), (1, 8)), ((0, 16), (0, 16)))
ONE = (((2, 4),), ((2, 2),), ((1, 8),), ((0, 16),))
TAIL = (((2, 2), (1, 8)), ((1, 8), (0, 16)), ((0, 16), (0, 2)))


def side_of(bit):
    return (lax.axis_index("dp") // bit) % 2


def sum_send(parts, step):
    return [swap(pick(part, 1 - side_of(bit), axis), bit) for part, (axis, bit) in zip(parts, step)]


def sum_take(parts, got, step):
    return [add(pick(part, side_of(bit), axis), g) for part, g, (axis, bit) in zip(parts, got, step)]


def two(g):
    g = g.reshape(2, 2, 2, 2, g.shape[0] // 16, g.shape[1])
    cut = g.shape[4] // 2
    return [g[..., :cut, :], g[..., cut:, :]]


def whole_sum(g):
    n = lax.axis_size("dp")
    groups = [list(range(c, n, 2)) for c in range(2)]
    g = g.reshape(n // 2, g.shape[0] // (n // 2), g.shape[1])
    return lax.psum_scatter(g, "dp", scatter_dimension=0, axis_index_groups=groups).astype(f32)


def join(a, b, axis, bit):
    mine = (lax.axis_index("dp") // bit) % 2
    return jnp.where(mine == 0, jnp.stack([a, b], axis), jnp.stack([b, a], axis))


def gather_send(parts, step):
    if lax.axis_size("dp") != 32:
        return parts
    return [swap(p, bit) for p, (axis, bit) in zip(parts, BOTH[3 - step])]


def gather_take(parts, got, step):
    if lax.axis_size("dp") != 32:
        return parts
    return [join(p, g, axis, bit) for p, g, (axis, bit) in zip(parts, got, BOTH[3 - step])]


def gather_step(parts, step):
    return gather_take(parts, gather_send(parts, step), step)


def chip_gather_end(parts):
    n = lax.axis_size("dp")
    if n != 32:
        groups = [list(range(c, n, 2)) for c in range(2)]
        return [lax.all_gather(p, "dp", axis=0, axis_index_groups=groups, tiled=True) for p in parts]
    return [p.reshape(-1, p.shape[-1]) for p in parts]


def tie(*values):
    return lax.optimization_barrier(values)


def on_core(keep, send):
    return (keep + swap(send, 1).astype(f32)).astype(bf16)


def trade_rows(h):
    core = lax.axis_index("dp") % 2
    h = h.reshape(2, h.shape[0] // 2, h.shape[1])
    own, got = pick(h, core, 0), swap(pick(h, 1 - core, 0).astype(bf16), 1).astype(f32)
    return jnp.where(core == 0, own, got), jnp.where(core == 0, got, own)


def on_device(x_in, first_in, spans, gout_in, mix, gains, biases, tying, extra, dwindle,
              squash, reducing, enlarging, ingoing, concluding, ffn_key, ffn_value):
    micro, seqs, length, width = x_in.shape
    rows = micro * seqs * length
    shard = mix.shape[1]
    core = lax.axis_index("dp") % 2
    chips = lax.axis_size("dp") // 2
    half = width // 2
    small = jnp.concatenate([mix, gains, biases, tying, extra[None], dwindle[None], squash], 0)
    n_small = small.shape[0]
    fill = jnp.zeros((80, shard), bf16)
    low_a = jnp.concatenate([reducing, jnp.concatenate([small[:16], fill], 0).T], 1)
    low_b = jnp.concatenate(
        [enlarging, small[16:], jnp.zeros((16 - n_small + 16, shard), bf16), fill], 0).T
    turned = jnp.swapaxes(ingoing, 1, 2)
    q_halves = jnp.stack([jnp.concatenate([turned[0][:, c * half:(c + 1) * half],
                                           turned[1][:, c * half:(c + 1) * half]], 1)
                          for c in range(2)])
    r_halves = jnp.stack([jnp.concatenate([turned[2][:, c * half:(c + 1) * half], low], 1)
                          for c, low in enumerate((low_a, low_b))])
    keys = ffn_key.reshape(shard, chips, 2, -1)
    k_halves = jnp.stack([jnp.concatenate([keys[:, :, c].reshape(shard, -1),
                                           concluding.T[:, c * half:(c + 1) * half]], 1)
                          for c in range(2)])

    def trade(halves):
        own, sent = pick(halves, core, 0), pick(halves, 1 - core, 0)
        return join(own, swap(sent, 1), 0, 1).reshape(2 * shard, -1)

    mixer = [trade(q_halves), trade(r_halves)]
    mixer = gather_step(gather_step(mixer, 0), 1)
    ffn = [trade(k_halves), ffn_value]
    mixer, ffn = tie(mixer, ffn)

    def one_send(p, step, which):
        axis, bit = BOTH[3 - step][which]
        return swap(p, bit) if lax.axis_size("dp") == 32 else p

    def one_take(p, got, step, which):
        axis, bit = BOTH[3 - step][which]
        return join(p, got, axis, bit) if lax.axis_size("dp") == 32 else p

    got, k_got = tie(gather_send(mixer, 2), one_send(ffn[0], 0, 0))
    mixer = gather_take(mixer, got, 2)
    f_key, f_val = one_take(ffn[0], k_got, 0, 0), ffn[1]
    got, k_got, v_got = tie(gather_send(mixer, 3), one_send(f_key, 1, 0), one_send(f_val, 0, 1))
    f_key, f_val = one_take(f_key, k_got, 1, 0), one_take(f_val, v_got, 0, 1)
    got, f_key, f_val = tie(got, f_key, f_val)
    v_got, k_got = one_send(f_val, 1, 1), one_send(f_key, 2, 0)
    mixer = chip_gather_end(gather_take(mixer, got, 3))
    far = [swap(p, 1) for p in mixer]

    def in_core_order(a, b, axis):
        return jnp.where(core == 0, jnp.concatenate([a, b], axis), jnp.concatenate([b, a], axis))

    wi = [(mixer[0][:, :half], far[0][:, :half]), (mixer[0][:, half:], far[0][:, half:]),
          (mixer[1][:, :half], far[1][:, :half])]
    low_a = jnp.where(core == 0, mixer[1][:, half:], far[1][:, half:])
    low_b = jnp.where(core == 0, far[1][:, half:], mixer[1][:, half:])
    w_in, w_out = low_a[:, :CUTS[4]], low_b[:, :CUTS[4]]
    small = jnp.concatenate([low_a[:, CUTS[4]:CUTS[4] + 16], low_b[:, CUTS[4]:CUTS[4] + 16]], 1)
    small = small.T.astype(f32)
    mix, gains, biases, tying = small[0:7], small[7:10], small[10:13], small[13:15]

    def by_core(a):
        return in_core_order(a[..., :half], a[..., half:], -1)

    par = jnp.concatenate([small[13:19], gains[1:2], biases[1:2]], 0)

    x = x_in.reshape(rows, width).astype(f32)
    first = first_in.reshape(rows, width)
    place = jnp.arange(length, dtype=jnp.int32)
    valid = (place[None, None, :] < spans[:, :, None]).astype(f32).reshape(rows, 1)
    g_out = valid * gout_in.reshape(rows, width).astype(f32)
    gf = g_out.astype(bf16)

    xs, pull_front = jax.vjp(front, by_core(x), by_core(mix[:6]), by_core(gains[0]), by_core(biases[0]))
    xs = [z.astype(bf16) for z in xs]
    xs, v_got, gf = tie(xs, v_got, gf)
    f_val = one_take(f_val, v_got, 1, 1)
    v_got = one_send(f_val, 2, 1)
    proj = [mmt(xs[j][:, :half], wi[i][0]) + mmt(xs[j][:, half:], wi[i][1])
            for i, j in enumerate((0, 2, 3))]
    w_in = in_core_order(w_in[:half], w_in[half:], 0)
    zs = [mm(xs[j], w_in[:, CUTS[i]:CUTS[i + 1]]) for i, j in enumerate(LOW_FROM)]
    ls, pull_low = jax.vjp(lowrank_act, *zs)
    ls = [z.astype(bf16) for z in ls]
    os_ = [mmt(ls[i], w_out[:, CUTS[i]:CUTS[i + 1]]) for i in range(4)]
    args = (*proj, *os_, first)
    done = mixer_fwd(args, par, 0, ())
    done, k_got, v_got = tie(done, k_got, v_got)
    ffn = [one_take(f_key, k_got, 2, 0), one_take(f_val, v_got, 2, 1)]
    ffn_got = gather_send(ffn, 3)
    for part in (1, 2, 3):
        done = mixer_fwd(args, par, part, done)
    done, ffn_got = tie(done, ffn_got)
    ffn = chip_gather_end(gather_take(ffn, ffn_got, 3))
    gated, *saved = done
    wk, wv = ffn
    wo = wk[:, -half:]
    wo_far, wk, wv = tie(swap(wo, 1), wk, wv)
    wk_far, wv_far = swap(wk, 1), swap(wv, 1)

    def side(a, c):
        return lax.dynamic_slice_in_dim(a, c * half, half, 1)

    gated_near, gated_far = side(gated, core), side(gated, 1 - core)
    mixed = x + mmt(gated_near, wo) + mmt(gated_far, wo_far)
    (xc,), pull_chan = jax.vjp(front, mixed, mix[6:7], gains[2], biases[2])
    xc = xc.astype(bf16)
    xct = xc.T
    hidden, g_pre, g_xc = ffn_half(xc, xct, gf, wk, wv, False)
    g_pre, wk_far, wv_far = tie(g_pre, wk_far, wv_far)
    hidden_far, _, g_xc_far, val_far, key_far = ffn_half(xc, xct, gf, wk_far, wv_far, True)

    scale = 1.0 / math.sqrt(rows * lax.axis_size("dp"))

    small_slice = lax.axis_size("dp") == 32
    side_y = lax.axis_index("dp") // 4 % 2 if small_slice else jnp.int32(0)
    side_y = side_y.reshape(1)
    steps = BOTH if small_slice else ((), (), (), ())

    def start(g):
        return two(g) if small_slice else whole_sum(g)

    def send(parts, step):
        return sum_send(parts, steps[step]) if small_slice else []

    def take(parts, got, step):
        return sum_take(parts, got, steps[step]) if small_slice else parts

    def finish(parts):
        return jnp.concatenate(parts, 0).astype(f32) if small_slice else parts

    val_got, key_got = swap(val_far, 1), swap(key_far, 1)
    g_mixed, g_mix_c, g_gain_c, g_bias_c = pull_chan((g_xc + g_xc_far,))
    g_mixed = g_out + g_mixed
    early = jnp.concatenate(
        [g_mix_c, g_gain_c[None], g_bias_c[None], jnp.zeros((5, width), f32)], 0)
    g_att = g_mixed.astype(bf16)
    conc_got = swap(tmm(g_att, gated_far).astype(bf16), 1)
    gg = in_core_order(mm(g_att, wo), mm(g_att, wo_far), 1)
    gg, val_got, key_got, conc_got = tie(gg, val_got, key_got, conc_got)
    d_value, d_key = ffn_grads(xct, gf, hidden, g_pre, val_got, key_got)
    d_key = conc_grad(g_att, gated_near, conc_got, d_key)
    d_value, d_key = start(d_value), start(d_key)
    v_got, k_got = send(d_value, 0), send(d_key, 0)
    gg, d_value, d_key = tie(gg, d_value, d_key)
    grads = mixer_bwd(args, par, saved, gg, side_y, 0, ())
    grads, v_got = tie(grads, v_got)
    d_value = take(d_value, v_got, 0)
    v_got = send(d_value, 1)
    grads = mixer_bwd(args, par, saved, gg, side_y, 1, grads)

    x_proj = [xs[0], xs[2], xs[3]]

    def proj_part(near):
        cols = slice(0, half) if near else slice(half, width)
        return jnp.concatenate([tmm(grads[9 + i][:, :half], x_proj[i][:, cols]) for i in range(3)], 1)

    away = on_core(proj_part(True), proj_part(False).astype(bf16))
    grads = mixer_bwd(args, par, saved, gg, side_y, 2, grads)
    grads, v_got, k_got, away = tie(grads, v_got, k_got, away)
    d_value, d_key = take(d_value, v_got, 1), take(d_key, k_got, 0)
    v_got, k_got = send(d_value, 2), send(d_key, 1)
    if small_slice:
        away = swap(away, 4)
    grads = mixer_bwd(args, par, saved, gg, side_y, 3, grads)
    grads, v_got, k_got = tie(grads, v_got, k_got)
    d_value, d_key = take(d_value, v_got, 2), take(d_key, k_got, 1)
    v_got, k_got = send(d_value, 3), send(d_key, 2)
    home = swap(proj_grad(grads[9:12], x_proj, 1, False, [], False), 1)
    gp = jnp.sum(grads[8].reshape(-1, 8, width), 0)
    g_proj, g_os, g_first = grads[:3], grads[3:7], grads[7]
    g_ls = tuple(mm(g_os[i], w_out[:, CUTS[i]:CUTS[i + 1]]) for i in range(4))
    g_zs = [z.astype(bf16) for z in pull_low(g_ls)]
    back = [mmt(g_zs[i], w_in[:, CUTS[i]:CUTS[i + 1]]) for i in range(4)]

    def down(i):
        return jnp.concatenate([mm(g_proj[i], wi[i][0]), mm(g_proj[i], wi[i][1])], 1)

    g_xs = (down(0), back[0], down(1), down(2) + back[2], back[1], back[3])
    low_a = jnp.concatenate([tmm(xs[j], g_zs[i]) for i, j in enumerate(LOW_FROM)], 1)
    low_a = in_core_order(low_a[:half], low_a[half:], 0)
    low_b = jnp.concatenate([tmm(g_os[i], ls[i]) for i in range(4)], 1)
    d_low = on_core(jnp.where(core == 0, low_a, low_b),
                    jnp.where(core == 0, low_b, low_a).astype(bf16))
    if small_slice:
        d_low = [d_low.reshape(2, 2, 2, 2, 64, -1)]
        l_got = sum_send(d_low, ONE[0])
    if small_slice:
        g_xs, away, home = tie(g_xs, away, home)
        d_proj = proj_grad(grads[9:12], x_proj, 1, True, [home, away], True)
        d_proj = [p.reshape(2, 2, 2, 32, -1) for p in d_proj]
        p_send = [pick(p, 1 - side_of(bit), axis) for p, (axis, bit) in zip(d_proj, TAIL[0])]
        p_send, v_got, k_got, l_got = tie(p_send, v_got, k_got, l_got)
        p_got = [swap(p, bit) for p, (axis, bit) in zip(p_send, TAIL[0])]
        d_key, d_low = take(d_key, k_got, 2), sum_take(d_low, l_got, ONE[0])
        l_got, k_got = sum_send(d_low, ONE[1]), send(d_key, 3)
    g_x, g_mix_t, g_gain_t, g_bias_t = pull_front(g_xs)
    g_x = g_mixed + by_core(g_x)
    g_mix_t, g_gain_t, g_bias_t = by_core(g_mix_t), by_core(g_gain_t), by_core(g_bias_t)
    d_small = jnp.concatenate(
        [gp, jnp.concatenate([g_mix_t, g_gain_t[None], g_bias_t[None]], 0), early], 0)
    if small_slice:
        d_small, p_got, l_got, hidden, hidden_far = tie(d_small, p_got, l_got, hidden, hidden_far)
        d_proj, d_low = sum_take(d_proj, p_got, TAIL[0]), sum_take(d_low, l_got, ONE[1])
        p_got, l_got = sum_send(d_proj, TAIL[1]), sum_send(d_low, ONE[2])
        for bit in (1, 2, 4, 8, 16):
            d_small = d_small + swap(d_small, bit)
        out = mixed + mm(hidden, wv)
        out, p_got, l_got, k_got, v_got = tie(out, p_got, l_got, k_got, v_got)
        d_proj, d_low = sum_take(d_proj, p_got, TAIL[1]), sum_take(d_low, l_got, ONE[2])
        p_send = [pick(p, 1 - side_of(bit), axis) for p, (axis, bit) in zip(d_proj, TAIL[2])]
        p_send, v_got, k_got = tie(p_send, v_got, k_got)
        p_got = [swap(p, bit) for p, (axis, bit) in zip(p_send, TAIL[2])]
        l_got = sum_send(d_low, ONE[3])
        out = valid * (out + mm(hidden_far, wv_far))
        d_proj = finish(sum_take(d_proj, p_got, TAIL[2]))
        d_low = finish(sum_take(d_low, l_got, ONE[3]))
    else:
        home = proj_grad(grads[9:12], x_proj, 1, True, [home], False).reshape(width // 256, 1, 128, -1)
        d_proj = whole_sum(jnp.concatenate([home, away.reshape(home.shape)], 1).reshape(width, -1))
        d_low = whole_sum(d_low)
        d_small = lax.psum(d_small, "dp")
        out = valid * (mixed + mm(hidden, wv) + mm(hidden_far, wv_far))
    d_key = finish(take(d_key, k_got, 3))
    d_value = finish(take(d_value, v_got, 3))
    d_small = scale * lax.dynamic_slice_in_dim(d_small, lax.axis_index("dp") * shard, shard, 1)
    half_a, half_b = trade_rows(d_proj * scale)
    low_a, low_b = trade_rows(d_low * scale)
    key_a, key_b = trade_rows(d_key * scale)
    hw = half
    wide = [jnp.concatenate([half_a[:, i * hw:(i + 1) * hw], half_b[:, i * hw:(i + 1) * hw]], 1)
            for i in range(3)]
    d_in = jnp.stack([w.T for w in wide])
    d_conc = jnp.concatenate([key_a[:, -hw:], key_b[:, -hw:]], 1).T
    key_a, key_b = key_a[:, :-hw], key_b[:, :-hw]
    d_key = jnp.stack([key_a.reshape(shard, chips, -1), key_b.reshape(shard, chips, -1)], 2)
    d_key = d_key.reshape(shard, -1)
    return (
        out.astype(bf16).reshape(x_in.shape), g_x.astype(bf16).reshape(x_in.shape),
        g_first.reshape(x_in.shape),
        jnp.concatenate([d_small[8:14], d_small[16:17]], 0),
        jnp.concatenate([d_small[14:15], d_small[6:7], d_small[17:18]], 0),
        jnp.concatenate([d_small[15:16], d_small[7:8], d_small[18:19]], 0),
        d_small[0:2], d_small[2], d_small[3], d_small[4:6],
        low_a, low_b.T, d_in, d_conc, d_key, d_value * scale)


def solution(mesh):
    tok, row, col = P(None, "dp", None, None), P("dp", None), P(None, "dp")
    vec, cube = P("dp"), P(None, None, "dp")
    in_specs = (tok, tok, col, tok, col, col, col, col, vec, vec, col, row, col, cube, col, row, row)
    out_specs = (tok, tok, tok, col, col, col, col, vec, vec, col, row, col, cube, col, row, row)
    return jax.shard_map(
        on_device, mesh=mesh, in_specs=in_specs, out_specs=out_specs, check_vma=False)
```

```python
import functools
import math

import jax
import jax.numpy as jnp
from jax import lax
from jax.experimental import pallas as pl
from jax.experimental.pallas import tpu as pltpu
from jax.sharding import PartitionSpec as P

bf16, f32 = jnp.bfloat16, jnp.float32
RANKS = (64, 64, 32, 128)
CUTS = (0, 64, 128, 160, 288)
LOW_FROM = (1, 4, 3, 5)
T = 128

def dn(x, y, cx, cy):
    return lax.dot_general(x, y, (((cx,), (cy,)), ((), ())), preferred_element_type=f32)

def split2(x):
    hi = x.astype(bf16)
    return hi, (x - hi.astype(f32)).astype(bf16)

def dot(x, y, cx=1, cy=0, passes=3):
    if passes == 1:
        return dn(x.astype(bf16), y.astype(bf16), cx, cy)
    xh, xl = split2(x); yh, yl = split2(y)
    return dn(xh, yh, cx, cy) + dn(xh, yl, cx, cy) + dn(xl, yh, cx, cy)

def ones_dot(left, x):
    hi = x.astype(bf16); r = x - hi.astype(f32)
    mid = r.astype(bf16); lo = (r - mid.astype(f32)).astype(bf16)
    w = x.shape[1]
    o = dn(left, jnp.concatenate([hi, mid, lo], 1), 1, 0)
    return o[:, :w] + o[:, w:2*w] + o[:, 2*w:]

def head_sum(x, J):
    hi, lo = split2(x)
    return dn(jnp.concatenate([hi, lo], 1), jnp.concatenate([J, J], 0), 1, 0)

def sig(z):
    return 1.0 / (1.0 + jnp.exp(-z))

def iota(shape, d):
    return lax.broadcasted_iota(jnp.int32, shape, d)

def consts():
    r, c = iota((T, T), 0), iota((T, T), 1)
    J = jnp.where((r // 64) == (c // 64), 1.0, 0.0).astype(bf16)
    low = jnp.where(r >= c, 1.0, 0.0).astype(bf16)
    up = jnp.where(r <= c, 1.0, 0.0).astype(bf16)
    h0 = c < 64
    return r, c, J, low, up, h0

def halves(x, h0):
    z = jnp.zeros_like(x)
    m = h0 if x.shape[0] == T else jnp.concatenate([h0, h0], 0)
    return jnp.where(m, x, z), jnp.where(m, z, x)

def prep(r_, kx, vx, ow, oa, ov, first, par, K):
    r, c, J, low, up, h0 = K
    dk0, dk1, bonus, db, sq0, sq1 = (par[i:i+1] for i in range(6))
    sg = sig(db + ow)
    ld = sg * (-0.6065306597126334)
    cum = ones_dot(low, ld)
    cm = cum - cum[63:64]
    G = jnp.exp(cm); S = jnp.exp(-cm); B = jnp.exp(cm - ld)
    ag = sig(sq0 + oa); vg = sig(sq1 + ov)
    v2 = vx + (first - vx) * vg
    kfac = 1.0 + (ag - 1.0) * dk1
    km = kx * kfac
    cc = kx * dk0
    n = lax.rsqrt(head_sum(cc * cc, J) + 1e-6)
    kk = cc * n
    return sg, ld, G, S, B, ag, vg, v2, kfac, km, n, kk

def inverse(N0, N1, K, passes):
    r, c = K[0], K[1]
    z = jnp.zeros((T, T), f32)
    eye = jnp.where(r == c, 1.0, 0.0)
    m = ((r // 2) == (c // 2))
    T0 = eye + jnp.where(m, N0, 0.0); T1 = eye + jnp.where(m, N1, 0.0)
    s = 2
    def bd(a, b):
        return jnp.concatenate([jnp.concatenate([a, z], 1), jnp.concatenate([z, b], 1)], 0)
    TT = jnp.concatenate([T0, T1], 1)
    while s < T:
        m = ((r // (2*s)) == (c // (2*s))) & ((r // s) != (c // s))
        yield
        o = dot(TT, bd(jnp.where(m, N0, 0.0), jnp.where(m, N1, 0.0)), passes=passes)
        yield
        TT = TT + dot(o, bd(TT[:, :T], TT[:, T:]), passes=passes)
        s *= 2
    yield
    res = jnp.concatenate([eye, eye], 1) - TT + dot(jnp.concatenate([N0, N1], 1), bd(TT[:, :T], TT[:, T:]))
    yield
    return TT + dot(TT, bd(res[:, :T], res[:, T:]), passes=1)

def fwd_core(r_, kx, vx, ow, oa, ov, og, first, par, pA=3, pI=1, pO=3):
    K = consts(); r, c, J, low, up, h0 = K
    sg, ld, G, S, B, ag, vg, v2, kfac, km, n, kk = prep(r_, kx, vx, ow, oa, ov, first, par, K)
    at = -kk * B; rt = r_ * G; bt = kk * ag * S; kt = km * S
    Q = jnp.concatenate([at, rt], 0); Kf = jnp.concatenate([bt, kt], 0)
    Q0, Q1 = halves(Q, h0)
    yield
    A0 = dot(Q0, Kf, 1, 1, pA); A1 = dot(Q1, Kf, 1, 1, pA)
    yield
    st = r > c; inc = r >= c
    def msk(A):
        return (jnp.where(st, A[:T, :T], 0.0), jnp.where(st, A[:T, T:], 0.0),
                jnp.where(inc, A[T:, :T], 0.0), jnp.where(inc, A[T:, T:], 0.0))
    ab0, ak0, rb0, rk0 = msk(A0); ab1, ak1, rb1, rk1 = msk(A1)
    TT = yield from inverse(ab0, ab1, K, pI)
    yield
    v0, v1 = halves(v2, h0)
    Pm = dot(jnp.concatenate([ak0, ak1], 1), jnp.concatenate([v0, v1], 0), passes=pO)
    yield
    U = dot(TT, jnp.concatenate(halves(Pm, h0), 0), passes=pO)
    yield
    u0, u1 = halves(U, h0)
    Y = dot(jnp.concatenate([rb0, rk0, rb1, rk1], 1), jnp.concatenate([u0, v0, u1, v1], 0), passes=pO)
    yield
    mean = head_sum(Y, J) * (1/64)
    yield
    cy = Y - mean
    rstd = lax.rsqrt(head_sum(cy * cy, J) * (1/64) + 4.0)
    yield
    bonus, gain, bias = par[2:3], par[6:7], par[7:8]
    bs = head_sum(r_ * km * bonus, J)
    out = (cy * rstd * gain + bias + bs * v2) * og
    return out, TT, U, Y

def bwd_core(r_, kx, vx, ow, oa, ov, og, first, par, TT, U, Y, gg, pA=3, pW=3, pD=3):
    K = consts(); r, c, J, low, up, h0 = K
    dk0, dk1, bonus, db, sq0, sq1, gain, bias = (par[i:i+1] for i in range(8))
    sg, ld, G, S, B, ag, vg, v2, kfac, km, n, kk = prep(r_, kx, vx, ow, oa, ov, first, par, K)
    at = -kk * B; rt = r_ * G; bt = kk * ag * S; kt = km * S
    yield
    mean = head_sum(Y, J) * (1/64)
    yield
    cy = Y - mean
    rstd = lax.rsqrt(head_sum(cy * cy, J) * (1/64) + 4.0)
    yield
    gn = cy * rstd
    bs = head_sum(r_ * km * bonus, J)
    g_og = gg * (gn * gain + bias + bs * v2)
    gi = gg * og
    g_gn = gi * gain
    gY = rstd * (g_gn - head_sum(g_gn, J) * (1/64) - gn * (head_sum(g_gn * gn, J) * (1/64)))
    yield
    g_bs = head_sum(gi * v2, J)
    yield
    Q = jnp.concatenate([at, rt], 0); Kf = jnp.concatenate([bt, kt], 0)
    Q0, Q1 = halves(Q, h0)
    At0 = dot(Kf, Q0, 1, 1, pA)
    yield
    At1 = dot(Kf, Q1, 1, 1, pA)
    yield
    st = r < c; inc = r <= c
    akT = jnp.concatenate([jnp.where(st, At0[T:, :T], 0.0), jnp.where(st, At1[T:, :T], 0.0)], 1)
    inc2 = jnp.concatenate([inc, inc], 0)
    rT = jnp.concatenate([jnp.where(inc2, At0[:, T:], 0.0), jnp.where(inc2, At1[:, T:], 0.0)], 1)
    yield
    gy0, gy1 = halves(gY, h0)
    dUV = dot(rT, jnp.concatenate([gy0, gy1], 0), passes=pW)
    yield
    dU, dV = dUV[:T], dUV[T:]
    R = dot(TT, dU, 0, 0, pW)
    yield
    W = jnp.where(h0, R[:T], R[T:])
    w0, w1 = halves(W, h0)
    dV = dV + dot(akT, jnp.concatenate([w0, w1], 0), passes=pW)
    yield
    X = jnp.concatenate([U, v2], 0)
    Yg0 = jnp.concatenate([w0, gy0], 0); Yg1 = jnp.concatenate([w1, gy1], 0)
    r2, c2 = iota((2*T, 2*T), 0), iota((2*T, 2*T), 1)
    keep = ((r2 & 127) > (c2 & 127)) | ((r2 >= T) & ((r2 & 127) == (c2 & 127)))
    keepT = ((r2 & 127) < (c2 & 127)) | ((c2 >= T) & ((r2 & 127) == (c2 & 127)))
    yield
    dA0 = jnp.where(keep, dot(Yg0, X, 1, 1, pD), 0.0)
    yield
    dA1 = jnp.where(keep, dot(Yg1, X, 1, 1, pD), 0.0)
    yield
    dT0 = jnp.where(keepT, dot(X, Yg0, 1, 1, pD), 0.0)
    yield
    dT1 = jnp.where(keepT, dot(X, Yg1, 1, 1, pD), 0.0)
    yield
    K0, K1 = halves(Kf, h0)
    dQ = dot(jnp.concatenate([dA0, dA1], 1), jnp.concatenate([K0, K1], 0), passes=pD)
    yield
    dK = dot(jnp.concatenate([dT0, dT1], 1), jnp.concatenate([Q0, Q1], 0), passes=pD)
    yield
    da_, dr_ = dQ[:T], dQ[T:]; db_, dk_ = dK[:T], dK[T:]
    e = dr_ * rt - db_ * bt - dk_ * kt
    f = da_ * at
    yield
    g_ld = ones_dot(up, e + f) - f
    g_kk = db_ * S * ag - da_ * B
    g_b = db_ * S
    g_km = g_bs * r_ * bonus + dk_ * S
    g_r = g_bs * km * bonus + dr_ * G
    g_ag = g_b * kk + g_km * kx * dk1
    yield
    g_c = n * (g_kk - kk * head_sum(g_kk * kk, J))
    g_kx = g_km * kfac + g_c * dk0
    g_v2 = gi * bs + dV
    g_first = g_v2 * vg
    g_vx = g_v2 - g_first
    g_ov = g_first * (1.0 - vg) * (first - vx)
    g_oa = g_ag * ag * (1.0 - ag)
    g_ow = g_ld * ld * (1.0 - sg)
    yield
    def cs(x): return jnp.sum(x, 0, keepdims=True)
    pg = jnp.concatenate([cs(g_c * kx), cs(g_km * kx * (ag - 1.0)), cs(g_bs * r_ * km),
                          cs(g_ow), cs(g_oa), cs(g_ov), cs(gi * gn), cs(gi)], 0)
    return g_r, g_kx, g_vx, g_ow, g_oa, g_ov, g_og, g_first, pg


def in_step(parts):
    results, live = [None] * len(parts), list(range(len(parts)))
    while live:
        for i in list(live):
            try:
                next(parts[i])
            except StopIteration as end:
                results[i] = end.value
                live.remove(i)
    return results


def two_seqs(ins, par, saved, core):
    work = []
    for q in range(2):
        rows = pl.ds(q * T, T)
        vals = [ref[rows, :] for ref in ins]
        work.append(core(*vals[:7], vals[7].astype(f32), par[...], *[ref[rows, :] for ref in saved]))
    return in_step(work)


def fwd_kernel(*refs):
    outs = refs[9:]
    for q, res in enumerate(two_seqs(refs[:8], refs[8], [], fwd_core)):
        rows = pl.ds(q * T, T)
        outs[0][rows, :] = res[0].astype(bf16)
        for ref, val in zip(outs[1:], res[1:]):
            ref[rows, :] = val


def bwd_kernel(*refs):
    outs = refs[13:]
    for q, res in enumerate(two_seqs(refs[:8], refs[8], refs[9:13], bwd_core)):
        rows = pl.ds(q * T, T)
        for ref, val in zip(outs[:8], res[:8]):
            ref[rows, :] = val.astype(bf16)
        outs[8][pl.ds(q * 8, 8), :] = res[8]
        for ref, val in zip(outs[9:], res[:3]):
            ref[rows, :] = val.astype(bf16)


MIXER = dict(
    compiler_params=pltpu.CompilerParams(vmem_limit_bytes=32 * 1024 * 1024),
    cost_estimate=pl.CostEstimate(flops=10 * 10**9, bytes_accessed=10**7, transcendentals=10**6))


def mixer_fwd(args, par, part, before):
    rows, width = args[0].shape
    seqs, pairs = rows // T, width // 128
    p0 = part * (pairs // 4)
    tile = pl.BlockSpec((2 * T, 128), lambda s, p: (s, p + p0))
    pspec = pl.BlockSpec((8, 128), lambda s, p: (0, p + p0))
    inv = pl.BlockSpec((2 * T, 2 * T), lambda s, p: (s * pairs + p + p0, 0))
    wide = jax.ShapeDtypeStruct((rows, width), f32)

    def body(*refs):
        fwd_kernel(*refs[:9], *refs[9 + len(before):])

    return pl.pallas_call(
        body,
        grid=(seqs // 2, pairs // 4),
        in_specs=[tile] * 8 + [pspec] + [pl.BlockSpec(memory_space=pl.ANY)] * len(before),
        out_specs=[tile, inv, tile, tile],
        out_shape=[jax.ShapeDtypeStruct((rows, width), bf16),
                   jax.ShapeDtypeStruct((rows * pairs, 2 * T), f32), wide, wide],
        input_output_aliases={9 + i: i for i in range(len(before))},
        name="mixer_fwd",
        **MIXER,
    )(*args, par, *before)


def mixer_bwd(args, par, saved, gg, side, part, before):
    rows, width = args[0].shape
    seqs, pairs = rows // T, width // 128
    keep, p0 = part // 2, part % 2 * (pairs // 4)

    def pair(p, side):
        return 2 * (p + p0) + (side[0] if keep else 1 - side[0])

    tile = pl.BlockSpec((2 * T, 128), lambda s, p, side: (s, pair(p, side)))
    pspec = pl.BlockSpec((8, 128), lambda s, p, side: (0, pair(p, side)))
    inv = pl.BlockSpec((2 * T, 2 * T), lambda s, p, side: (s * pairs + pair(p, side), 0))
    gpar = pl.BlockSpec((16, 128), lambda s, p, side: (s, pair(p, side)))
    rel = pl.BlockSpec((2 * T, 128), lambda s, p, side: (s, p + p0 + keep * (pairs // 2)))
    thin = jax.ShapeDtypeStruct((rows, width), bf16)

    def body(*refs):
        bwd_kernel(*refs[1:14], *refs[14 + len(before):])

    return pl.pallas_call(
        body,
        grid_spec=pltpu.PrefetchScalarGridSpec(
            num_scalar_prefetch=1,
            grid=(seqs // 2, pairs // 4),
            in_specs=[tile] * 8 + [pspec, inv, tile, tile, tile]
            + [pl.BlockSpec(memory_space=pl.ANY)] * len(before),
            out_specs=[tile] * 8 + [gpar] + [rel] * 3),
        out_shape=[thin] * 8 + [jax.ShapeDtypeStruct((seqs * 8, width), f32)] + [thin] * 3,
        input_output_aliases={14 + i: i for i in range(len(before))},
        name="mixer_bwd",
        **MIXER,
    )(side, *args, par, *saved, gg, *before)


def ffn_kernel(xc, xct, gf, wk, wv, hid, gpre, gx, *grads):
    pre = jnp.maximum(mm(xc[...], wk[...]), 0.0)
    h = (pre * pre).astype(bf16)
    hid[...] = h
    g = (mmt(gf[...], wv[...]) * (2.0 * pre)).astype(bf16)
    gpre[...] = g
    if grads:
        d_val, d_key = grads
        d_val[...] = tmm(h, gf[...]).astype(bf16)
        d_key[...] = mm(xct[...], g).astype(bf16)
    g = mmt(g, wk[...])

    @pl.when(pl.program_id(0) == 0)
    def _():
        gx[...] = g

    @pl.when(pl.program_id(0) > 0)
    def _():
        gx[...] += g


FFN_BLOCK = 1024


def ffn_params(name, flops=5 * 10**9, moved=10**7):
    return dict(
        compiler_params=pltpu.CompilerParams(vmem_limit_bytes=32 * 1024 * 1024),
        cost_estimate=pl.CostEstimate(flops=flops, bytes_accessed=moved, transcendentals=0),
        name=name)


def ffn_half(xc, xct, gf, wk, wv, with_grads):
    rows, width = xc.shape
    units = wv.shape[0]
    tall = pl.BlockSpec((rows, width), lambda j: (0, 0))
    unit = pl.BlockSpec((rows, FFN_BLOCK), lambda j: (0, j))
    down = pl.BlockSpec((FFN_BLOCK, width), lambda j: (j, 0))
    across = pl.BlockSpec((width, FFN_BLOCK), lambda j: (0, j))
    hidden = jax.ShapeDtypeStruct((rows, units), bf16)
    more = with_grads * 1
    return pl.pallas_call(
        ffn_kernel,
        grid=(units // FFN_BLOCK,),
        in_specs=[tall, pl.BlockSpec((width, rows), lambda j: (0, 0)), tall, across, down],
        out_specs=[unit, unit, tall] + [down, across] * more,
        out_shape=[hidden, hidden, jax.ShapeDtypeStruct((rows, width), f32)]
        + [jax.ShapeDtypeStruct((units, width), bf16), jax.ShapeDtypeStruct((width, units), bf16)] * more,
        **ffn_params("ffn_half"),
    )(xc, xct, gf, wk, wv)


def grad_kernel(xct, gf, hid, gpre, val_got, key_got, d_val, d_key):
    d_val[...] = (tmm(hid[...], gf[...]) + val_got[...].astype(f32)).astype(bf16)
    d_key[...] = (mm(xct[...], gpre[...]) + key_got[...].astype(f32)).astype(bf16)


def ffn_grads(xct, gf, hid, gpre, val_got, key_got):
    width, rows = xct.shape
    units = hid.shape[1]
    unit = pl.BlockSpec((rows, FFN_BLOCK), lambda j: (0, j))
    down = pl.BlockSpec((FFN_BLOCK, width), lambda j: (j, 0))
    across = pl.BlockSpec((width, FFN_BLOCK), lambda j: (0, j))
    return pl.pallas_call(
        grad_kernel,
        grid=(units // FFN_BLOCK,),
        in_specs=[pl.BlockSpec((width, rows), lambda j: (0, 0)),
                  pl.BlockSpec((rows, width), lambda j: (0, 0)), unit, unit, down, across],
        out_specs=[down, across],
        out_shape=[jax.ShapeDtypeStruct((units, width), bf16),
                   jax.ShapeDtypeStruct((width, units + width // 2), bf16)],
        **ffn_params("ffn_grads"),
    )(xct, gf, hid, gpre, val_got, key_got)


def conc_kernel(att, gated, got, before, d_key):
    d_key[...] = (tmm(att[...], gated[...]) + got[...].astype(f32)).astype(bf16)


def conc_grad(att, gated, got, d_key):
    rows, width = att.shape
    cols = gated.shape[1]
    last = d_key.shape[1] // cols - 1
    return pl.pallas_call(
        conc_kernel,
        grid=(1,),
        in_specs=[pl.BlockSpec((rows, width), lambda j: (0, 0)),
                  pl.BlockSpec((rows, cols), lambda j: (0, 0)),
                  pl.BlockSpec((width, cols), lambda j: (0, 0)),
                  pl.BlockSpec(memory_space=pl.ANY)],
        out_specs=pl.BlockSpec((width, cols), lambda j: (0, last)),
        out_shape=jax.ShapeDtypeStruct(d_key.shape, bf16),
        input_output_aliases={3: 0},
        **ffn_params("conc_grad"),
    )(att, gated, got, d_key)


def proj_kernel(*refs, gots, split):
    cols = refs[0].shape[1]
    outs = refs[6 + gots:]
    for i in range(3):
        at = slice(i * cols, (i + 1) * cols)
        val = tmm(refs[i][...], refs[3 + i][...])
        for ref in refs[6:6 + gots]:
            val = val + ref[:, at].astype(f32)
        if not split:
            outs[0][:, at] = val.astype(bf16)
            continue
        for c in range(cols // 64):
            for h in range(2):
                outs[h][c * 32:(c + 1) * 32, at] = val[c * 64 + h * 32:c * 64 + h * 32 + 32].astype(bf16)


def proj_grad(gs, xs, keep, near, gots, split):
    rows, width = xs[0].shape
    half = width // 2
    full = pl.BlockSpec((half, 3 * half), lambda j: (0, 0))
    part = half // 2 if split else half
    n_out = 2 if split else 1
    res = pl.pallas_call(
        functools.partial(proj_kernel, gots=len(gots), split=split),
        grid=(1,),
        in_specs=[pl.BlockSpec((rows, half), lambda j: (0, keep))] * 3
        + [pl.BlockSpec((rows, half), lambda j: (0, 0 if near else 1))] * 3 + [full] * len(gots),
        out_specs=[pl.BlockSpec((part, 3 * half), lambda j: (0, 0))] * n_out,
        out_shape=[jax.ShapeDtypeStruct((part, 3 * half), bf16)] * n_out,
        **ffn_params("proj_grad", 3 * 10**8, 10**6),
    )(*gs, *xs, *gots)
    return res if split else res[0]


def small_kernel(core, gp, mix, gain, bias, early, out):
    half = out.shape[1] // 2
    out[:8, :] = gp[...]
    out[16:, :] = early[...]
    for ref, at in ((mix, 8), (gain, 14), (bias, 15)):
        n = ref.shape[0]
        a, b = ref[:, :half], ref[:, half:]
        turn = jnp.full((n, half), core[0], jnp.int32) == 1
        out[at:at + n, :half] = jnp.where(turn, b, a)
        out[at:at + n, half:] = jnp.where(turn, a, b)


def small_rows(core, gp, mix, gain, bias, early):
    vmem = pl.BlockSpec(memory_space=pltpu.VMEM)
    return pl.pallas_call(
        small_kernel,
        in_specs=[pl.BlockSpec(memory_space=pltpu.SMEM)] + [vmem] * 5,
        out_specs=vmem,
        out_shape=jax.ShapeDtypeStruct((24, gp.shape[1]), f32),
        name="small_rows",
    )(core.reshape(1), gp, mix, gain, bias, early)


def layer_norm(x, gain, bias):
    c = x - jnp.mean(x, -1, keepdims=True)
    return c * lax.rsqrt(jnp.mean(c * c, -1, keepdims=True) + 1e-5) * gain + bias


def prev(z):
    z = z.reshape(-1, T, z.shape[-1])
    z = jnp.concatenate([jnp.zeros_like(z[:, :1]), z[:, :-1]], 1)
    return z.reshape(-1, z.shape[-1])


def front(x, mix, gain, bias):
    h = layer_norm(x, gain, bias)
    d = prev(h) - h
    return tuple(h + d * mix[i] for i in range(mix.shape[0]))


def mm(a, b):
    return dn(a, b, 1, 0)


def mmt(a, b):
    return dn(a, b, 1, 1)


def tmm(a, b):
    return dn(a, b, 0, 0)


def lowrank_act(zw, za, zv, zg):
    return jnp.tanh(zw), za, zv, jax.nn.sigmoid(zg)


def swap(x, bit):
    n = lax.axis_size("dp")
    return lax.ppermute(x, "dp", [(i, i ^ bit) for i in range(n)])


def add(a, b):
    return (a.astype(f32) + b.astype(f32)).astype(bf16)


def pick(x, index, axis):
    return lax.dynamic_index_in_dim(x, index, axis, keepdims=False)


BOTH = (((2, 4), (3, 2)), ((2, 2), (2, 4)), ((1, 8), (1, 8)), ((0, 16), (0, 16)))
ONE = (((2, 4),), ((2, 2),), ((1, 8),), ((0, 16),))
TAIL = (((2, 2), (1, 8)), ((1, 8), (0, 16)), ((0, 16), (0, 2)))


def side_of(bit):
    return (lax.axis_index("dp") // bit) % 2


def sum_send(parts, step):
    return [swap(pick(part, 1 - side_of(bit), axis), bit) for part, (axis, bit) in zip(parts, step)]


def sum_take(parts, got, step):
    return [add(pick(part, side_of(bit), axis), g) for part, g, (axis, bit) in zip(parts, got, step)]


def two(g):
    g = g.reshape(2, 2, 2, 2, g.shape[0] // 16, g.shape[1])
    cut = g.shape[4] // 2
    return [g[..., :cut, :], g[..., cut:, :]]


def whole_sum(g):
    n = lax.axis_size("dp")
    groups = [list(range(c, n, 2)) for c in range(2)]
    g = g.reshape(n // 2, g.shape[0] // (n // 2), g.shape[1])
    return lax.psum_scatter(g, "dp", scatter_dimension=0, axis_index_groups=groups).astype(f32)


def join(a, b, axis, bit):
    mine = (lax.axis_index("dp") // bit) % 2
    return jnp.where(mine == 0, jnp.stack([a, b], axis), jnp.stack([b, a], axis))


def gather_send(parts, step):
    if lax.axis_size("dp") != 32:
        return parts
    return [swap(p, bit) for p, (axis, bit) in zip(parts, BOTH[3 - step])]


def gather_take(parts, got, step):
    if lax.axis_size("dp") != 32:
        return parts
    return [join(p, g, axis, bit) for p, g, (axis, bit) in zip(parts, got, BOTH[3 - step])]


def gather_step(parts, step):
    return gather_take(parts, gather_send(parts, step), step)


def chip_gather_end(parts):
    n = lax.axis_size("dp")
    if n != 32:
        groups = [list(range(c, n, 2)) for c in range(2)]
        return [lax.all_gather(p, "dp", axis=0, axis_index_groups=groups, tiled=True) for p in parts]
    return [p.reshape(-1, p.shape[-1]) for p in parts]


def tie(*values):
    return lax.optimization_barrier(values)


def on_core(keep, send):
    return (keep + swap(send, 1).astype(f32)).astype(bf16)


def trade_rows(h):
    core = lax.axis_index("dp") % 2
    h = h.reshape(2, h.shape[0] // 2, h.shape[1])
    own, got = pick(h, core, 0), swap(pick(h, 1 - core, 0).astype(bf16), 1).astype(f32)
    return jnp.where(core == 0, own, got), jnp.where(core == 0, got, own)


def on_device(x_in, first_in, spans, gout_in, mix, gains, biases, tying, extra, dwindle,
              squash, reducing, enlarging, ingoing, concluding, ffn_key, ffn_value):
    micro, seqs, length, width = x_in.shape
    rows = micro * seqs * length
    shard = mix.shape[1]
    core = lax.axis_index("dp") % 2
    chips = lax.axis_size("dp") // 2
    half = width // 2
    small = jnp.concatenate([mix, gains, biases, tying, extra[None], dwindle[None], squash], 0)
    n_small = small.shape[0]
    fill = jnp.zeros((80, shard), bf16)
    low_a = jnp.concatenate([reducing, jnp.concatenate([small[:16], fill], 0).T], 1)
    low_b = jnp.concatenate(
        [enlarging, small[16:], jnp.zeros((16 - n_small + 16, shard), bf16), fill], 0).T
    turned = jnp.swapaxes(ingoing, 1, 2)
    q_halves = jnp.stack([jnp.concatenate([turned[0][:, c * half:(c + 1) * half],
                                           turned[1][:, c * half:(c + 1) * half]], 1)
                          for c in range(2)])
    r_halves = jnp.stack([jnp.concatenate([turned[2][:, c * half:(c + 1) * half], low], 1)
                          for c, low in enumerate((low_a, low_b))])
    keys = ffn_key.reshape(shard, chips, 2, -1)
    k_halves = jnp.stack([jnp.concatenate([keys[:, :, c].reshape(shard, -1),
                                           concluding.T[:, c * half:(c + 1) * half]], 1)
                          for c in range(2)])

    def trade(halves):
        own, sent = pick(halves, core, 0), pick(halves, 1 - core, 0)
        return join(own, swap(sent, 1), 0, 1).reshape(2 * shard, -1)

    mixer = [trade(q_halves), trade(r_halves)]
    mixer = gather_step(gather_step(mixer, 0), 1)
    ffn = [trade(k_halves), ffn_value]
    mixer, ffn = tie(mixer, ffn)

    def one_send(p, step, which):
        axis, bit = BOTH[3 - step][which]
        return swap(p, bit) if lax.axis_size("dp") == 32 else p

    def one_take(p, got, step, which):
        axis, bit = BOTH[3 - step][which]
        return join(p, got, axis, bit) if lax.axis_size("dp") == 32 else p

    got, k_got = tie(gather_send(mixer, 2), one_send(ffn[0], 0, 0))
    mixer = gather_take(mixer, got, 2)
    f_key, f_val = one_take(ffn[0], k_got, 0, 0), ffn[1]
    got, k_got, v_got = tie(gather_send(mixer, 3), one_send(f_key, 1, 0), one_send(f_val, 0, 1))
    f_key, f_val = one_take(f_key, k_got, 1, 0), one_take(f_val, v_got, 0, 1)
    got, f_key, f_val = tie(got, f_key, f_val)
    v_got, k_got = one_send(f_val, 1, 1), one_send(f_key, 2, 0)
    mixer = chip_gather_end(gather_take(mixer, got, 3))
    far = [swap(p, 1) for p in mixer]

    def in_core_order(a, b, axis):
        return jnp.where(core == 0, jnp.concatenate([a, b], axis), jnp.concatenate([b, a], axis))

    wi = [(mixer[0][:, :half], far[0][:, :half]), (mixer[0][:, half:], far[0][:, half:]),
          (mixer[1][:, :half], far[1][:, :half])]
    low_a = jnp.where(core == 0, mixer[1][:, half:], far[1][:, half:])
    low_b = jnp.where(core == 0, far[1][:, half:], mixer[1][:, half:])
    w_in, w_out = low_a[:, :CUTS[4]], low_b[:, :CUTS[4]]
    small = jnp.concatenate([low_a[:, CUTS[4]:CUTS[4] + 16], low_b[:, CUTS[4]:CUTS[4] + 16]], 1)
    small = small.T.astype(f32)
    mix, gains, biases, tying = small[0:7], small[7:10], small[10:13], small[13:15]

    def by_core(a):
        return in_core_order(a[..., :half], a[..., half:], -1)

    par = jnp.concatenate([small[13:19], gains[1:2], biases[1:2]], 0)

    x = x_in.reshape(rows, width).astype(f32)
    first = first_in.reshape(rows, width)
    place = jnp.arange(length, dtype=jnp.int32)
    valid = (place[None, None, :] < spans[:, :, None]).astype(f32).reshape(rows, 1)
    g_out = valid * gout_in.reshape(rows, width).astype(f32)
    gf = g_out.astype(bf16)

    xs, pull_front = jax.vjp(front, by_core(x), by_core(mix[:6]), by_core(gains[0]), by_core(biases[0]))
    xs = [z.astype(bf16) for z in xs]
    xs, v_got, gf = tie(xs, v_got, gf)
    f_val = one_take(f_val, v_got, 1, 1)
    v_got = one_send(f_val, 2, 1)
    proj = [mmt(xs[j][:, :half], wi[i][0]) + mmt(xs[j][:, half:], wi[i][1])
            for i, j in enumerate((0, 2, 3))]
    w_in = in_core_order(w_in[:half], w_in[half:], 0)
    zs = [mm(xs[j], w_in[:, CUTS[i]:CUTS[i + 1]]) for i, j in enumerate(LOW_FROM)]
    ls, pull_low = jax.vjp(lowrank_act, *zs)
    ls = [z.astype(bf16) for z in ls]
    os_ = [mmt(ls[i], w_out[:, CUTS[i]:CUTS[i + 1]]) for i in range(4)]
    args = (*proj, *os_, first)
    done = mixer_fwd(args, par, 0, ())
    done, k_got, v_got = tie(done, k_got, v_got)
    ffn = [one_take(f_key, k_got, 2, 0), one_take(f_val, v_got, 2, 1)]
    ffn_got = gather_send(ffn, 3)
    for part in (1, 2, 3):
        done = mixer_fwd(args, par, part, done)
    done, ffn_got = tie(done, ffn_got)
    ffn = chip_gather_end(gather_take(ffn, ffn_got, 3))
    gated, *saved = done
    wk, wv = ffn
    wo = wk[:, -half:]
    wo_far, wk, wv = tie(swap(wo, 1), wk, wv)
    wk_far, wv_far = swap(wk, 1), swap(wv, 1)

    def side(a, c):
        return lax.dynamic_slice_in_dim(a, c * half, half, 1)

    gated_near, gated_far = side(gated, core), side(gated, 1 - core)
    mixed = x + mmt(gated_near, wo) + mmt(gated_far, wo_far)
    (xc,), pull_chan = jax.vjp(front, mixed, mix[6:7], gains[2], biases[2])
    xc = xc.astype(bf16)
    xct = xc.T
    hidden, g_pre, g_xc = ffn_half(xc, xct, gf, wk, wv, False)
    g_pre, wk_far, wv_far = tie(g_pre, wk_far, wv_far)
    hidden_far, _, g_xc_far, val_far, key_far = ffn_half(xc, xct, gf, wk_far, wv_far, True)

    scale = 1.0 / math.sqrt(rows * lax.axis_size("dp"))

    small_slice = lax.axis_size("dp") == 32
    side_y = lax.axis_index("dp") // 4 % 2 if small_slice else jnp.int32(0)
    side_y = side_y.reshape(1)
    steps = BOTH if small_slice else ((), (), (), ())

    def start(g):
        return two(g) if small_slice else whole_sum(g)

    def send(parts, step):
        return sum_send(parts, steps[step]) if small_slice else []

    def take(parts, got, step):
        return sum_take(parts, got, steps[step]) if small_slice else parts

    def finish(parts):
        return jnp.concatenate(parts, 0).astype(f32) if small_slice else parts

    val_got, key_got = swap(val_far, 1), swap(key_far, 1)
    g_mixed, g_mix_c, g_gain_c, g_bias_c = pull_chan((g_xc + g_xc_far,))
    g_mixed = g_out + g_mixed
    early = jnp.concatenate(
        [g_mix_c, g_gain_c[None], g_bias_c[None], jnp.zeros((5, width), f32)], 0)
    g_att = g_mixed.astype(bf16)
    conc_got = swap(tmm(g_att, gated_far).astype(bf16), 1)
    gg = in_core_order(mm(g_att, wo), mm(g_att, wo_far), 1)
    gg, val_got, key_got, conc_got = tie(gg, val_got, key_got, conc_got)
    d_value, d_key = ffn_grads(xct, gf, hidden, g_pre, val_got, key_got)
    d_key = conc_grad(g_att, gated_near, conc_got, d_key)
    d_value, d_key = start(d_value), start(d_key)
    v_got, k_got = send(d_value, 0), send(d_key, 0)
    gg, d_value, d_key = tie(gg, d_value, d_key)
    grads = mixer_bwd(args, par, saved, gg, side_y, 0, ())
    grads, v_got = tie(grads, v_got)
    d_value = take(d_value, v_got, 0)
    v_got = send(d_value, 1)
    grads = mixer_bwd(args, par, saved, gg, side_y, 1, grads)

    x_proj = [xs[0], xs[2], xs[3]]

    def proj_part(near):
        cols = slice(0, half) if near else slice(half, width)
        return jnp.concatenate([tmm(grads[9 + i][:, :half], x_proj[i][:, cols]) for i in range(3)], 1)

    away = on_core(proj_part(True), proj_part(False).astype(bf16))
    grads = mixer_bwd(args, par, saved, gg, side_y, 2, grads)
    grads, v_got, k_got, away = tie(grads, v_got, k_got, away)
    d_value, d_key = take(d_value, v_got, 1), take(d_key, k_got, 0)
    v_got, k_got = send(d_value, 2), send(d_key, 1)
    if small_slice:
        away = swap(away, 4)
    grads = mixer_bwd(args, par, saved, gg, side_y, 3, grads)
    grads, v_got, k_got = tie(grads, v_got, k_got)
    d_value, d_key = take(d_value, v_got, 2), take(d_key, k_got, 1)
    v_got, k_got = send(d_value, 3), send(d_key, 2)
    home = swap(proj_grad(grads[9:12], x_proj, 1, False, [], False), 1)
    gp = jnp.sum(grads[8].reshape(-1, 8, width), 0)
    g_proj, g_os, g_first = grads[:3], grads[3:7], grads[7]
    g_ls = tuple(mm(g_os[i], w_out[:, CUTS[i]:CUTS[i + 1]]) for i in range(4))
    g_zs = [z.astype(bf16) for z in pull_low(g_ls)]
    back = [mmt(g_zs[i], w_in[:, CUTS[i]:CUTS[i + 1]]) for i in range(4)]

    def down(i):
        return jnp.concatenate([mm(g_proj[i], wi[i][0]), mm(g_proj[i], wi[i][1])], 1)

    g_xs = (down(0), back[0], down(1), down(2) + back[2], back[1], back[3])
    low_a = jnp.concatenate([tmm(xs[j], g_zs[i]) for i, j in enumerate(LOW_FROM)], 1)
    low_a = in_core_order(low_a[:half], low_a[half:], 0)
    low_b = jnp.concatenate([tmm(g_os[i], ls[i]) for i in range(4)], 1)
    d_low = on_core(jnp.where(core == 0, low_a, low_b),
                    jnp.where(core == 0, low_b, low_a).astype(bf16))
    if small_slice:
        d_low = [d_low.reshape(2, 2, 2, 2, 64, -1)]
        l_got = sum_send(d_low, ONE[0])
    if small_slice:
        g_xs, away, home = tie(g_xs, away, home)
        d_proj = proj_grad(grads[9:12], x_proj, 1, True, [home, away], True)
        d_proj = [p.reshape(2, 2, 2, 32, -1) for p in d_proj]
        p_send = [pick(p, 1 - side_of(bit), axis) for p, (axis, bit) in zip(d_proj, TAIL[0])]
        p_send, v_got, k_got, l_got = tie(p_send, v_got, k_got, l_got)
        p_got = [swap(p, bit) for p, (axis, bit) in zip(p_send, TAIL[0])]
        d_key, d_low = take(d_key, k_got, 2), sum_take(d_low, l_got, ONE[0])
        l_got, k_got = sum_send(d_low, ONE[1]), send(d_key, 3)
    g_x, g_mix_t, g_gain_t, g_bias_t = pull_front(g_xs)
    g_x = g_mixed + by_core(g_x)
    d_small = small_rows(core, gp, g_mix_t, g_gain_t[None], g_bias_t[None], early)
    if small_slice:
        d_small, p_got, l_got, hidden, hidden_far = tie(d_small, p_got, l_got, hidden, hidden_far)
        d_proj, d_low = sum_take(d_proj, p_got, TAIL[0]), sum_take(d_low, l_got, ONE[1])
        p_got, l_got = sum_send(d_proj, TAIL[1]), sum_send(d_low, ONE[2])
        for bit in (1, 2, 4, 8, 16):
            d_small = d_small + swap(d_small, bit)
        out = mixed + mm(hidden, wv)
        out, p_got, l_got, k_got, v_got = tie(out, p_got, l_got, k_got, v_got)
        d_proj, d_low = sum_take(d_proj, p_got, TAIL[1]), sum_take(d_low, l_got, ONE[2])
        p_send = [pick(p, 1 - side_of(bit), axis) for p, (axis, bit) in zip(d_proj, TAIL[2])]
        p_send, v_got, k_got = tie(p_send, v_got, k_got)
        p_got = [swap(p, bit) for p, (axis, bit) in zip(p_send, TAIL[2])]
        l_got = sum_send(d_low, ONE[3])
        out = valid * (out + mm(hidden_far, wv_far))
        d_proj = finish(sum_take(d_proj, p_got, TAIL[2]))
        d_low = finish(sum_take(d_low, l_got, ONE[3]))
    else:
        home = proj_grad(grads[9:12], x_proj, 1, True, [home], False).reshape(width // 256, 1, 128, -1)
        d_proj = whole_sum(jnp.concatenate([home, away.reshape(home.shape)], 1).reshape(width, -1))
        d_low = whole_sum(d_low)
        d_small = lax.psum(d_small, "dp")
        out = valid * (mixed + mm(hidden, wv) + mm(hidden_far, wv_far))
    d_key = finish(take(d_key, k_got, 3))
    d_value = finish(take(d_value, v_got, 3))
    d_small = scale * lax.dynamic_slice_in_dim(d_small, lax.axis_index("dp") * shard, shard, 1)
    half_a, half_b = trade_rows(d_proj * scale)
    low_a, low_b = trade_rows(d_low * scale)
    key_a, key_b = trade_rows(d_key * scale)
    hw = half
    wide = [jnp.concatenate([half_a[:, i * hw:(i + 1) * hw], half_b[:, i * hw:(i + 1) * hw]], 1)
            for i in range(3)]
    d_in = jnp.stack([w.T for w in wide])
    d_conc = jnp.concatenate([key_a[:, -hw:], key_b[:, -hw:]], 1).T
    key_a, key_b = key_a[:, :-hw], key_b[:, :-hw]
    d_key = jnp.stack([key_a.reshape(shard, chips, -1), key_b.reshape(shard, chips, -1)], 2)
    d_key = d_key.reshape(shard, -1)
    return (
        out.astype(bf16).reshape(x_in.shape), g_x.astype(bf16).reshape(x_in.shape),
        g_first.reshape(x_in.shape),
        jnp.concatenate([d_small[8:14], d_small[16:17]], 0),
        jnp.concatenate([d_small[14:15], d_small[6:7], d_small[17:18]], 0),
        jnp.concatenate([d_small[15:16], d_small[7:8], d_small[18:19]], 0),
        d_small[0:2], d_small[2], d_small[3], d_small[4:6],
        low_a, low_b.T, d_in, d_conc, d_key, d_value * scale)


def solution(mesh):
    tok, row, col = P(None, "dp", None, None), P("dp", None), P(None, "dp")
    vec, cube = P("dp"), P(None, None, "dp")
    in_specs = (tok, tok, col, tok, col, col, col, col, vec, vec, col, row, col, cube, col, row, row)
    out_specs = (tok, tok, tok, col, col, col, col, vec, vec, col, row, col, cube, col, row, row)
    return jax.shard_map(
        on_device, mesh=mesh, in_specs=in_specs, out_specs=out_specs, check_vma=False)
```
